512 devices in a mesh: seq: 16 (over z, core), exp: 32 (over y, x).
Axes of the slice: x: 4, y: 8, z: 8, core: 2. Of those that a mesh axis runs over, the one named last changes fastest.
Arguments:
- tokens: bfloat16 [32, 4096, 768], P('exp', 'seq'), may hold values from -6 to 6
- w_in: bfloat16 [768, 3072], P('seq'), may hold values from -0.21875 to 0.21875
- w_small: bfloat16 [768, 56], replicated, may hold values from -0.21875 to 0.21875
- dt_bias: float32 [24], replicated, may hold values from -1 to 1
- decay_rate: float32 [24], replicated, may hold values from 4.8828125e-05 to 0.08, as said below
- conv_w: float32 [4, 1536], replicated, may hold values from -3 to 3
- conv_b: float32 [1536], replicated, may hold values from -3 to 3
- skip: float32 [24], replicated, may hold values from 0.5 to 1.5
- norm_gain: float32 [1536], replicated, may hold values from 0.1 to 1.9
- w_out: bfloat16 [1536, 768], P('seq'), may hold values from -0.15625 to 0.15625
- w_router: bfloat16 [768, 32], replicated, may hold values from -0.21875 to 0.21875
- expert_ids: int32 [32, 4096, 2], P('exp', 'seq'), may hold values from 0 to 31, all different within a row; in each aligned block of 256 rows (0 to 255, 256 to 511, ..., all dimensions but the last counted through in order) at most 48 rows name the same one
- w_gate: bfloat16 [32, 768, 768], P('exp'), may hold values from -0.21875 to 0.21875
- w_up: bfloat16 [32, 768, 768], P('exp'), may hold values from -0.21875 to 0.21875
- w_down: bfloat16 [32, 768, 768], P('exp'), may hold values from -0.21875 to 0.21875
Outputs:
- out: bfloat16 [32, 4096, 768], P('exp', 'seq')
The draws below stay inside these ranges and needn't reach their ends.
Inputs may be any that keep to these rules, and one draw needn't show every extreme that they name: `expert_ids`: in the rows of one device no expert is named by more than 48 tokens, a bound that some block reaches; the two experts of a token differ. `decay_rate`: positive rates, one per head.
All inputs are finite; a program needn't handle non-finite values.
Results may differ from the reference program's by a relative error of at most 0.015.
Values may be sent and summed in bfloat16 or wider, within the bound.
A program may use at most 64 MiB of HBM per device.

```python
import math
import jax
import jax.numpy as jnp
import numpy as np
from jax import lax

D = 768
H = 24
P_SIZE = 64
N = 16
K = 4
EH = 768
TOK_DEV = 256
SEQS = 32
LEN = 4096
EXPERTS = 32
CAP = 48
N_EXP = 32


def draw_decay_rate(key, part):
    key = jax.random.fold_in(key, 7)
    pick_key, fast_key, slow_key = jax.random.split(key, 3)
    fast = jax.random.randint(pick_key, (H,), 0, 2).astype(jnp.float32)
    slow = jnp.exp(jax.random.uniform(slow_key, (H,), jnp.float32, math.log(0.2), math.log(2.0))) / LEN
    quick = jnp.exp(jax.random.uniform(fast_key, (H,), jnp.float32, math.log(0.03), math.log(0.08)))
    return fast * quick + (1.0 - fast) * slow


def block_levels(stream_key, dims, shards, least, top_value):
    loudness = 1.0
    for dim, blocks in shards:
        heights = jax.random.uniform(jax.random.fold_in(jax.random.fold_in(stream_key, 6), dim), (blocks,), jnp.float32, least / len(shards), top_value / len(shards))
        loudness = loudness * jnp.repeat(jnp.exp(heights), dims[dim] // blocks).reshape((-1,) + (1,) * (len(dims) - 1 - dim))
    return loudness


def routed_block(own_key, own, number, rows, amount, top, most, slope):
    order = jax.random.permutation(own_key, amount)
    packed, common = load_shares(amount, rows * top, most, slope, True), load_shares(amount, rows * top, most, slope, False)
    places = jnp.arange(amount)

    def named(sizes, rotation):
        used = int((sizes > 0).sum())
        fixed = max(1, used // 4)
        shifted = fixed + (places - fixed + rotation * (used - fixed)) % max(1, amount - fixed)
        return jnp.zeros((amount,), jnp.int32).at[order[jnp.where(places < fixed, places, shifted)]].set(jnp.asarray(sizes, jnp.int32))

    sizes = jnp.where(number % 4 == 0, named(packed, number // 4), named(common, number - number // 4 - 1))
    mixed = jax.random.permutation(jax.random.fold_in(own, 3), amount)
    giver, taker = mixed[0:amount // 2 * 2:2], mixed[1:amount // 2 * 2:2]
    room = jnp.minimum(sizes[giver] - 1, most - sizes[taker]) // 2
    room = jnp.where((giver == order[0]) | (taker == order[0]) | (sizes[taker] == 0), 0, jnp.maximum(room, 0))
    shifted = jax.random.randint(jax.random.fold_in(own, 4), (amount // 2,), 0, 1 << 20) % (room + 1)
    sizes = sizes.at[giver].add(-shifted).at[taker].add(shifted)
    items = jnp.searchsorted(jnp.cumsum(sizes), jnp.arange(rows * top), side="right").astype(jnp.int32)
    grid = items.reshape(top, rows).T
    grid = grid[jax.random.permutation(jax.random.fold_in(own, 1), rows)]
    rotation = jax.random.randint(jax.random.fold_in(own, 2), (rows, 1), 0, top)
    return jnp.take_along_axis(grid, (jnp.arange(top)[None, :] + rotation) % top, axis=1)


def load_shares(count, total, most, skew, full):
    loads = [(1 << 20) // math.isqrt(standing ** skew) + 1 for standing in range(1, count + 1)]
    largest = most if full else min(most, max(-(-total // count), total * loads[0] // sum(loads)))
    least = 1 if total - largest >= count - 1 else 0
    holding, surplus = [largest] + [least] * (count - 1), total - largest - least * (count - 1)
    while surplus > 0:
        candidates = [i for i in range(1, count) if holding[i] < largest] or [i for i in range(1, count) if holding[i] < most]
        mass, remaining = sum([loads[i] for i in candidates]), surplus
        for i in candidates:
            extra = min(most - holding[i], max(1, remaining * loads[i] // mass), surplus)
            holding[i] = holding[i] + extra
            surplus = surplus - extra
    return np.array(holding)


def normal_values(stream_key, dims, spread, reach, pieces=(), held_as=jnp.bfloat16):
    array = spread * jax.random.normal(stream_key, dims, jnp.float32)
    if pieces:
        array = array * block_levels(stream_key, dims, pieces, -0.22, 0.18)
    return jnp.clip(array, -reach, reach).astype(held_as)


def setup_inputs(seed: int = 0) -> dict:
    key_list = jax.random.split(jax.random.key(seed), 16)
    tokens = normal_values(key_list[0], (SEQS, LEN, D), 1.0, 6.0, ((0, 32), (1, 16)))
    w_in = normal_values(key_list[1], (D, 2 * H * P_SIZE), D ** -0.5, 0.21875, ((0, 16),))
    w_small = normal_values(key_list[2], (D, 2 * N + H), D ** -0.5, 0.21875)
    dt_bias = jnp.clip(jax.random.uniform(key_list[3], (H,), jnp.float32, -1.0, 1.0), -1.0, 1.0)
    decay_rate = draw_decay_rate(jax.random.fold_in(key_list[15], 71), 0)
    conv_w = normal_values(key_list[5], (K, H * P_SIZE), 0.5, 3.0, (), jnp.float32)
    conv_b = normal_values(key_list[6], (H * P_SIZE,), 0.5, 3.0, (), jnp.float32)
    skip = jnp.clip(jax.random.uniform(key_list[7], (H,), jnp.float32, 0.5, 1.5), 0.5, 1.5)
    norm_gain = jnp.clip(1.0 + 0.18 * jax.random.normal(key_list[8], (H * P_SIZE,), jnp.float32), 0.1, 1.9)
    w_out = normal_values(key_list[9], (H * P_SIZE, D), (H * P_SIZE) ** -0.5, 0.15625, ((0, 16),))
    w_router = normal_values(key_list[10], (D, EXPERTS), D ** -0.5, 0.21875)
    expert_ids_keys = jax.random.split(jax.random.fold_in(key_list[11], 1), SEQS * LEN // TOK_DEV)
    expert_ids_turns = jax.random.permutation(jax.random.fold_in(key_list[11], 3), SEQS * LEN // TOK_DEV)
    expert_ids = jax.vmap(lambda own, number: routed_block(jax.random.fold_in(key_list[11], 2), own, number, TOK_DEV, EXPERTS, 2, CAP, 2))(expert_ids_keys, expert_ids_turns).reshape((SEQS, LEN, 2))
    w_gate = normal_values(key_list[12], (EXPERTS, D, EH), D ** -0.5, 0.21875, ((0, 32),))
    w_up = normal_values(key_list[13], (EXPERTS, D, EH), D ** -0.5, 0.21875, ((0, 32),))
    w_down = normal_values(key_list[14], (EXPERTS, EH, D), EH ** -0.5, 0.21875, ((0, 32),))
    return {"tokens": tokens, "w_in": w_in, "w_small": w_small, "dt_bias": dt_bias, "decay_rate": decay_rate, "conv_w": conv_w, "conv_b": conv_b, "skip": skip, "norm_gain": norm_gain, "w_out": w_out, "w_router": w_router, "expert_ids": expert_ids, "w_gate": w_gate, "w_up": w_up, "w_down": w_down}


EPSILON = 1e-05
ROW_BLOCK = 512

def rms_rows(values):
    return values * lax.rsqrt(lax.optimization_barrier(jnp.mean(values * values, axis=-1, keepdims=True)) + EPSILON)

def expert_block(rows_in, gate_mat, up_mat, down_mat):
    hidden = jax.nn.silu(jnp.dot(rows_in, gate_mat, preferred_element_type=jnp.float32)) * jnp.dot(rows_in, up_mat, preferred_element_type=jnp.float32)
    return jnp.dot(hidden.astype(jnp.bfloat16), down_mat, preferred_element_type=jnp.float32).astype(jnp.bfloat16)

def mixer_sequence(seq_tokens, w_in, w_small, dt_bias, decay_rate, conv_w, conv_b, skip, norm_gain, w_out):
    inner_w = w_out.shape[0]
    head_size = inner_w // H
    resid = seq_tokens.astype(jnp.float32)
    normed = rms_rows(resid).astype(jnp.bfloat16)
    projected = jnp.dot(normed, w_in, preferred_element_type=jnp.float32)
    gate_z = projected[:, :inner_w]
    inner = projected[:, inner_w:].astype(jnp.bfloat16)
    small = jnp.dot(normed, w_small, preferred_element_type=jnp.float32)
    b_in = small[:, :N]
    c_out = small[:, N:2 * N]
    step_size = jax.nn.softplus(small[:, 2 * N:] + dt_bias)
    padded = jnp.concatenate([jnp.zeros((K - 1, inner_w), jnp.bfloat16), inner], 0).astype(jnp.float32)
    conv = conv_b + conv_w[0] * padded[0:LEN]
    for k in range(1, K):
        conv = conv + conv_w[k] * padded[k:k + LEN]
    signal = jax.nn.silu(conv)
    log_decay = -step_size * decay_rate
    heads_in = signal.reshape(LEN, H, head_size)

    def advance(state, inputs):
        decay_now, step_now, signal_now, b_now, c_now = inputs
        state = jnp.exp(decay_now)[:, None, None] * state + (step_now[:, None] * signal_now)[:, :, None] * b_now[None, None, :]
        return (state, lax.optimization_barrier(jnp.sum(state * c_now[None, None, :], axis=-1)))
    start_state = jnp.zeros((H, head_size, N), jnp.float32)
    unused, scanned = lax.scan(advance, start_state, (log_decay, step_size, heads_in, b_in, c_out))
    scanned = scanned + skip[None, :, None] * heads_in
    gated = scanned.reshape(LEN, inner_w) * jax.nn.silu(gate_z)
    gated = (rms_rows(gated) * norm_gain).astype(jnp.bfloat16)
    mixed = resid + jnp.dot(gated, w_out, preferred_element_type=jnp.float32)
    return mixed.astype(jnp.bfloat16)

def reference(tokens, w_in, w_small, dt_bias, decay_rate, conv_w, conv_b, skip, norm_gain, w_out, w_router, expert_ids, w_gate, w_up, w_down):

    def per_volume(seq_tokens):
        return mixer_sequence(seq_tokens, w_in, w_small, dt_bias, decay_rate, conv_w, conv_b, skip, norm_gain, w_out)
    mixed = lax.map(per_volume, tokens)
    flat = mixed.reshape(SEQS * LEN, D)
    routed = rms_rows(flat.astype(jnp.float32)).astype(jnp.bfloat16)
    logits = jnp.dot(routed, w_router, preferred_element_type=jnp.float32)
    pair_ids = expert_ids.reshape(SEQS * LEN, 2).astype(jnp.int32)
    picked = jnp.take_along_axis(logits, pair_ids, axis=1)
    first = jax.nn.sigmoid(picked[:, 0] - picked[:, 1])
    pair_weight = jnp.stack([first, 1.0 - first], axis=1).reshape(-1)
    flat_ids = pair_ids.reshape(-1)
    pairs = flat_ids.shape[0]
    bound = SEQS * LEN
    order = jnp.arange(pairs, dtype=jnp.int32)
    spare = jnp.arange(ROW_BLOCK, dtype=jnp.int32)

    def one_expert(index, total):
        hit = (flat_ids == index).astype(jnp.int32)
        rank = (jnp.cumsum(hit) - 1).astype(jnp.int32)
        target = jnp.where(hit > 0, rank, bound + ROW_BLOCK).astype(jnp.int32)
        source = jnp.zeros((bound + ROW_BLOCK,), jnp.int32).at[target].set(order, mode='drop')
        count = jnp.sum(hit).astype(jnp.int32)

        def run_rows(block, acc):
            begin = (block * ROW_BLOCK).astype(jnp.int32)
            rows = lax.dynamic_slice_in_dim(source, begin, ROW_BLOCK, 0)
            valid = (begin + spare < count).astype(jnp.float32)
            answer = expert_block(routed[rows // 2], w_gate[index], w_up[index], w_down[index])
            term = answer.astype(jnp.float32) * (valid * pair_weight[rows])[:, None]
            return acc.at[rows // 2].add(term)
        blocks = ((count + ROW_BLOCK - 1) // ROW_BLOCK).astype(jnp.int32)
        return lax.fori_loop(jnp.int32(0), blocks, run_rows, total)
    total = lax.fori_loop(jnp.int32(0), jnp.int32(N_EXP), one_expert, flat.astype(jnp.float32))
    return total.astype(jnp.bfloat16).reshape(SEQS, LEN, D)
```

```python
import jax
import jax.numpy as jnp
from jax import lax
from jax.experimental import pallas as pl
from jax.experimental.pallas import tpu as pltpu
from jax.sharding import PartitionSpec as P

SCAN_BLOCK = 128


EPSILON = 1e-05
HIGHEST = lax.Precision.HIGHEST


def from_behind(block, axis, distance):
    devices = range(lax.axis_size(axis))
    route = [(i - distance, i) for i in devices if i - distance in devices]
    return lax.ppermute(block, axis, route)


def carried_in(part, axis, combine, identity):
    place = lax.axis_index(axis)
    gathered = jax.tree.map(lambda a: lax.all_gather(a, axis), part)
    state = jax.tree.map(lambda a, e: jnp.zeros_like(a) + jnp.asarray(e, a.dtype), part, identity)

    def one(lap, state):
        return combine(
            state, jax.tree.map(lambda a: lax.dynamic_index_in_dim(a, lap, 0, False), gathered)
        )

    return lax.fori_loop(0, place, one, state)


def rms_rows(values):
    return values * lax.rsqrt(jnp.mean(values * values, axis=-1, keepdims=True) + EPSILON)


def expert_block(rows_in, gate_mat, up_mat, down_mat):
    hidden = jax.nn.silu(jnp.dot(rows_in, gate_mat, preferred_element_type=jnp.float32)) * jnp.dot(
        rows_in, up_mat, preferred_element_type=jnp.float32
    )
    return jnp.dot(
        hidden.astype(jnp.bfloat16), down_mat, preferred_element_type=jnp.float32
    ).astype(jnp.bfloat16)


Y, X = 8, 4
CAP = 48
META = 16
MESH = pl.DeviceIdType.MESH


def exp_peers():
    e = lax.axis_index("exp")
    y, x = e // X, lax.rem(e, X)
    return y, x


def moe_kernel(
    blk_ref, mixed_ref, wg_ref, wu_ref, wd_ref, out_ref,
    gath, sbuf, arr, relay, ans, ret, back, part, rs_out, rs_in, hid,
    ysend, yrecv, xsend, xrecv, fsend, frecv, rsend, rrecv, bsend, brecv, psend, precv,
):
    rows = mixed_ref.shape[0]
    width = mixed_ref.shape[1]
    half = rows // 2
    slots = X * CAP
    y, x = exp_peers()

    def device(dy, dx):
        return {"exp": lax.rem(y + dy, Y) * X + lax.rem(x + dx, X)}

    up, down = device(1, 0), device(Y - 1, 0)

    def remote(src, dst, send, recv, to):
        return pltpu.make_async_remote_copy(
            src_ref=src, dst_ref=dst, send_sem=send, recv_sem=recv,
            device_id=to, device_id_type=MESH,
        )

    barrier = pltpu.get_barrier_semaphore()
    for to in (up, down, device(0, 1), device(0, X - 1)):
        pl.semaphore_signal(barrier, inc=1, device_id=to, device_id_type=MESH)
    pl.semaphore_wait(barrier, 4)

    spans = (pl.ds(0, META + half), pl.ds(META + half, half))

    def right(k, h):
        src = blk_ref if k == 1 else gath.at[k - 1]
        return remote(src.at[spans[h]], gath.at[k, spans[h]], ysend.at[0, k - 1, h], yrecv.at[k, h], up)

    def left(k, h):
        src = blk_ref if k == 1 else gath.at[Y - k + 1]
        return remote(src.at[spans[h]], gath.at[Y - k, spans[h]], ysend.at[1, k - 1, h], yrecv.at[Y - k, h], down)

    last = Y // 2

    def sent(k, h, side):
        return k < last or (k == last and h == side)

    def places(d):
        meta = gath[d, 0:META, 0:rows].astype(jnp.float32)
        at = []
        for c in range(2):
            off = meta[2 * c : 2 * c + 1, :] - (y * X).astype(jnp.float32)
            turn = off - x.astype(jnp.float32)
            turn = jnp.where(turn < 0.0, turn + X, turn)
            mine = (off >= 0.0) & (off < float(X))
            at.append(jnp.where(mine, turn * CAP + meta[2 * c + 1 : 2 * c + 2, :], -1.0))
        line = lax.broadcasted_iota(jnp.int32, (slots, 1), 0).astype(jnp.float32)
        return meta, line == at[0], line == at[1]

    def sideways(d):
        return 1 + (X - 2) * lax.rem(d, 2)

    def dispatch(d):
        meta, hit0, hit1 = places(d)
        pick = jnp.where(hit0 | hit1, 1.0, 0.0).astype(jnp.bfloat16)
        sbuf[d] = jnp.dot(pick, gath[d, META:, :], preferred_element_type=jnp.float32).astype(jnp.bfloat16)
        arr[d, 0:CAP] = sbuf[d, 0:CAP]
        for c in (1, 3):
            span = pl.ds(c * CAP, CAP)
            remote(sbuf.at[d, span], arr.at[d, span], xsend.at[d], xrecv.at[d], device(0, c)).start()
        remote(sbuf.at[d, pl.ds(2 * CAP, CAP)], relay.at[d], xsend.at[d], frecv.at[d], device(0, sideways(d))).start()

    def pass_on(d):
        copy = remote(relay.at[d], arr.at[d, pl.ds(2 * CAP, CAP)], fsend.at[d], xrecv.at[d], device(0, sideways(d)))
        remote(sbuf.at[d, pl.ds(2 * CAP, CAP)], relay.at[d], xsend.at[d], frecv.at[d], device(0, 1)).wait_recv()
        copy.start()

    others = pl.ds(CAP, slots - CAP)

    def expert(d):
        remote(sbuf.at[d, others], arr.at[d, others], xsend.at[d], xrecv.at[d], device(0, 1)).wait_recv()
        tile = 256

        def enter(i, carry):
            cols = pl.ds(pl.multiple_of(i * tile, tile), tile)
            gate = jnp.dot(arr[d], wg_ref[0, :, cols], preferred_element_type=jnp.float32)
            lift = jnp.dot(arr[d], wu_ref[0, :, cols], preferred_element_type=jnp.float32)
            hid[:, cols] = (gate * jax.nn.sigmoid(gate) * lift).astype(jnp.bfloat16)
            return carry

        def leave(i, carry):
            cols = pl.ds(pl.multiple_of(i * tile, tile), tile)
            ans[d, :, cols] = jnp.dot(hid[...], wd_ref[0, :, cols], preferred_element_type=jnp.float32).astype(jnp.bfloat16)
            return carry

        lax.fori_loop(0, wg_ref.shape[2] // tile, enter, 0)
        lax.fori_loop(0, width // tile, leave, 0)
        ret[d, 0:CAP] = ans[d, 0:CAP]
        for c in (1, 3):
            span = pl.ds(c * CAP, CAP)
            remote(ans.at[d, span], ret.at[d, span], rsend.at[d], rrecv.at[d], device(0, X - c)).start()
        remote(ans.at[d, pl.ds(2 * CAP, CAP)], back.at[d], rsend.at[d], brecv.at[d], device(0, sideways(d))).start()

    def pass_back(d):
        copy = remote(back.at[d], ret.at[d, pl.ds(2 * CAP, CAP)], bsend.at[d], rrecv.at[d], device(0, sideways(d)))
        remote(ans.at[d, pl.ds(2 * CAP, CAP)], back.at[d], rsend.at[d], brecv.at[d], device(0, 1)).wait_recv()
        copy.start()

    def combine(d):
        remote(ans.at[d, others], ret.at[d, others], rsend.at[d], rrecv.at[d], device(0, 1)).wait_recv()
        meta, hit0, hit1 = places(d)
        share = jnp.where(hit0, meta[4:5, :], 0.0) + jnp.where(hit1, meta[5:6, :], 0.0)
        part[d] = lax.dot_general(
            share.astype(jnp.bfloat16), ret[d], (((0,), (0,)), ((), ())), preferred_element_type=jnp.float32
        )

    for h in range(2):
        right(1, h).start()
        left(1, h).start()
    gath[0] = blk_ref[...]
    dispatch(0)

    def both(fn, k):
        def one(i, carry):
            fn(k + i * (Y - 2 * k))
            return carry

        if k == 0 or k == last:
            fn(jnp.int32(k))
        else:
            lax.fori_loop(0, 2, one, 0)

    for k in range(1, last):
        for h in range(2):
            right(k, h).wait_recv()
            if sent(k + 1, h, 0):
                right(k + 1, h).start()
            left(k, h).wait_recv()
            if sent(k + 1, h, 1):
                left(k + 1, h).start()
        both(dispatch, k)
        both(pass_on, k - 1)
        both(expert, k - 1)
        if k >= 2:
            both(pass_back, k - 2)
            both(combine, k - 2)
    right(last, 0).wait_recv()
    left(last, 1).wait_recv()
    both(dispatch, last)
    both(pass_on, last - 1)
    both(expert, last - 1)
    both(pass_on, last)
    both(pass_back, last - 2)
    both(expert, last)
    both(combine, last - 2)
    both(pass_back, last - 1)
    both(combine, last - 1)
    both(pass_back, last)
    both(combine, last)

    bands = (pl.ds(0, half), pl.ds(half, half))

    def go(d, h, side):
        to = down if side == 0 else up
        land = (d - 1 if side == 0 else d + 1) if d != last else (last - 1 if side == 0 else last + 1)
        slot = Y if land == Y else land
        return remote(
            rs_out.at[d, bands[h]], rs_in.at[slot, bands[h]], psend.at[d, h], precv.at[slot, h], to
        )

    rs_out[last] = part[last].astype(jnp.bfloat16)
    go(last, 0, 0).start()
    go(last, 1, 1).start()
    for k in range(last - 1, 0, -1):
        for h in range(2):
            for side in range(2):
                d = k if side == 0 else Y - k
                total = part[d, bands[h]]
                if k < last - 1 or h == side:
                    before = (d + 1 if side == 0 else d - 1) if k < last - 1 else last
                    go(before, h, side).wait_recv()
                    total = total + rs_in[d, bands[h]].astype(jnp.float32)
                rs_out[d, bands[h]] = total.astype(jnp.bfloat16)
                go(d, h, side).start()
    for h in range(2):
        go(1, h, 0).wait_recv()
        go(Y - 1, h, 1).wait_recv()
        total = (
            mixed_ref[bands[h]].astype(jnp.float32) + part[0, bands[h]]
            + rs_in[0, bands[h]].astype(jnp.float32) + rs_in[Y, bands[h]].astype(jnp.float32)
        )
        out_ref[bands[h]] = total.astype(jnp.bfloat16)

    for k in range(1, last + 1):
        for h in range(2):
            if sent(k, h, 0):
                right(k, h).wait_send()
            if sent(k, h, 1):
                left(k, h).wait_send()
    for d in range(Y):
        for h in range(2):
            if d != 0:
                go(d, h, 0).wait_send()

    def drain(d, carry):
        remote(sbuf.at[d, others], arr.at[d, others], xsend.at[d], xrecv.at[d], device(0, 1)).wait_send()
        remote(ans.at[d, others], ret.at[d, others], rsend.at[d], rrecv.at[d], device(0, 1)).wait_send()
        tail = pl.ds(2 * CAP, CAP)
        remote(relay.at[d], arr.at[d, tail], fsend.at[d], xrecv.at[d], device(0, 1)).wait_send()
        remote(back.at[d], ret.at[d, tail], bsend.at[d], rrecv.at[d], device(0, 1)).wait_send()
        return carry

    lax.fori_loop(0, Y, drain, 0)


def moe(blk, mixed, w_gate, w_up, w_down):
    rows, width = mixed.shape
    slots = X * CAP
    bf16 = jnp.bfloat16
    dma = pltpu.SemaphoreType.DMA
    vmem = pl.BlockSpec(memory_space=pltpu.VMEM)
    return pl.pallas_call(
        moe_kernel,
        out_shape=jax.ShapeDtypeStruct((rows, width), bf16),
        in_specs=[vmem] * 5,
        out_specs=vmem,
        scratch_shapes=[
            pltpu.VMEM((Y, META + rows, width), bf16),
            pltpu.VMEM((Y, slots, width), bf16),
            pltpu.VMEM((Y, slots, width), bf16),
            pltpu.VMEM((Y, CAP, width), bf16),
            pltpu.VMEM((Y, slots, width), bf16),
            pltpu.VMEM((Y, slots, width), bf16),
            pltpu.VMEM((Y, CAP, width), bf16),
            pltpu.VMEM((Y, rows, width), jnp.float32),
            pltpu.VMEM((Y, rows, width), bf16),
            pltpu.VMEM((Y + 1, rows, width), bf16),
            pltpu.VMEM((slots, w_gate.shape[2]), bf16),
            dma((2, Y // 2, 2)), dma((Y, 2)),
            dma((Y,)), dma((Y,)), dma((Y,)), dma((Y,)),
            dma((Y,)), dma((Y,)), dma((Y,)), dma((Y,)),
            dma((Y, 2)), dma((Y + 1, 2)),
        ],
        compiler_params=pltpu.CompilerParams(
            collective_id=1, has_side_effects=True, vmem_limit_bytes=48 * 1024 * 1024
        ),
        cost_estimate=pl.CostEstimate(flops=8 * 10**9, bytes_accessed=6 * 10**6, transcendentals=10**6),
        name="expert_exchange",
    )(blk, mixed, w_gate, w_up, w_down)


def local(
    tokens,
    w_in,
    w_small,
    dt_bias,
    decay_rate,
    conv_w,
    conv_b,
    skip,
    norm_gain,
    w_out,
    w_router,
    expert_ids,
    w_gate,
    w_up,
    w_down,
):
    tok_rows = tokens.shape[1]
    width = tokens.shape[2]
    heads = dt_bias.shape[0]
    inner_w = conv_w.shape[1]
    head_size = inner_w // heads
    state_size = (w_small.shape[1] - heads) // 2
    kernel = conv_w.shape[0]
    resid = tokens.reshape(tok_rows, width).astype(jnp.float32)
    normed = rms_rows(resid).astype(jnp.bfloat16)
    columns = normed
    projected = jnp.dot(
        columns, lax.all_gather(w_in, "seq", axis=0, tiled=True), preferred_element_type=jnp.float32
    )
    gate_z = projected[:, :inner_w]
    inner = projected[:, inner_w:].astype(jnp.bfloat16)
    small = jnp.dot(normed, w_small, preferred_element_type=jnp.float32)
    b_in = small[:, :state_size]
    c_out = small[:, state_size : 2 * state_size]
    step_size = jax.nn.softplus(small[:, 2 * state_size :] + dt_bias)
    rim = from_behind(inner[tok_rows - (kernel - 1) :], "seq", 1)
    padded = jnp.concatenate([rim, inner], 0).astype(jnp.float32)
    conv = conv_b + conv_w[0] * padded[0:tok_rows]
    for k in range(1, kernel):
        conv = conv + conv_w[k] * padded[k : k + tok_rows]
    signal = jax.nn.silu(conv)
    span = SCAN_BLOCK
    blocks = tok_rows // span
    log_decay = (-step_size * decay_rate).reshape(blocks, span, heads)
    step_blocks = step_size.reshape(blocks, span, heads)
    signal_blocks = signal.reshape(blocks, span, heads, head_size)
    b_blocks = b_in.reshape(blocks, span, state_size)
    c_blocks = c_out.reshape(blocks, span, state_size)
    running = jnp.cumsum(log_decay, axis=1)
    scores = jnp.einsum("zin,zjn->zij", c_blocks, b_blocks, precision=HIGHEST)
    lower = jnp.arange(span)[:, None] >= jnp.arange(span)[None, :]
    spread = running[:, :, None, :] - running[:, None, :, :]
    weight = (
        jnp.exp(jnp.where(lower[None, :, :, None], spread, -jnp.inf))
        * scores[:, :, :, None]
        * step_blocks[:, None, :, :]
    )
    within = jnp.einsum("zijh,zjhp->zihp", weight, signal_blocks, precision=HIGHEST)
    tail = jnp.exp(running[:, -1:, :] - running) * step_blocks
    block_state = jnp.einsum("zjh,zjhp,zjn->zhpn", tail, signal_blocks, b_blocks, precision=HIGHEST)
    block_decay = running[:, -1, :]
    carried = jnp.zeros((heads, head_size, state_size), jnp.float32)
    before = jnp.zeros((heads,), jnp.float32)
    starts = []
    befores = []
    for z in range(blocks):
        starts.append(carried)
        befores.append(before)
        carried = jnp.exp(block_decay[z])[:, None, None] * carried + block_state[z]
        before = before + block_decay[z]

    def link(earlier, later):
        return (earlier[0] + later[0], jnp.exp(later[0])[:, None, None] * earlier[1] + later[1])

    unused, incoming = carried_in(
        (before, carried), "seq", link, (jnp.zeros_like(before), jnp.zeros_like(carried))
    )
    entries = []
    for z in range(blocks):
        entries.append(starts[z] + jnp.exp(befores[z])[:, None, None] * incoming)
    entry = jnp.stack(entries, 0)
    across = jnp.exp(running)[..., None] * jnp.einsum(
        "zin,zhpn->zihp", c_blocks, entry, precision=HIGHEST
    )
    scanned = within + across + skip[None, None, :, None] * signal_blocks
    gated = scanned.reshape(tok_rows, inner_w) * jax.nn.silu(gate_z)
    gated = (rms_rows(gated) * norm_gain).astype(jnp.bfloat16)
    columns = gated
    mixer_sum = jnp.dot(
        columns,
        lax.all_gather(w_out, "seq", axis=0, tiled=True),
        preferred_element_type=jnp.float32,
    )
    mixed = (resid + mixer_sum).astype(jnp.bfloat16)
    routed = rms_rows(mixed.astype(jnp.float32)).astype(jnp.bfloat16)
    logits = jnp.dot(routed, w_router, preferred_element_type=jnp.float32)
    experts = w_router.shape[1]
    pair_ids = expert_ids.reshape(tok_rows * 2)
    choose = (pair_ids[:, None] == jnp.arange(experts, dtype=jnp.int32)[None, :]).astype(jnp.int32)
    picked = jnp.sum(
        choose.reshape(tok_rows, 2, experts).astype(jnp.float32) * logits[:, None, :], axis=-1
    )
    first = jax.nn.sigmoid(picked[:, 0] - picked[:, 1])
    pair_weight = jnp.stack([first, 1.0 - first], axis=1)
    earlier_hits = jnp.cumsum(choose, axis=0) - choose
    slot = jnp.sum(earlier_hits * choose, axis=1)
    slot_of = slot.reshape(tok_rows, 2)
    notes = jnp.stack(
        [
            expert_ids.reshape(tok_rows, 2)[:, 0].astype(jnp.float32),
            slot_of[:, 0].astype(jnp.float32),
            expert_ids.reshape(tok_rows, 2)[:, 1].astype(jnp.float32),
            slot_of[:, 1].astype(jnp.float32),
            first,
            1.0 - first,
        ],
        axis=0,
    )
    notes = jnp.pad(notes, ((0, META - 6), (0, width - tok_rows))).astype(jnp.bfloat16)
    block = jnp.concatenate([notes, routed], axis=0)
    total = moe(block, mixed, w_gate, w_up, w_down)
    return total.reshape(1, tok_rows, width)


def solution(mesh):
    in_specs = (
        P("exp", "seq", None),
        P("seq", None),
        P(),
        P(),
        P(),
        P(),
        P(),
        P(),
        P(),
        P("seq", None),
        P(),
        P("exp", "seq", None),
        P("exp", None, None),
        P("exp", None, None),
        P("exp", None, None),
    )
    out_specs = P("exp", "seq", None)
    return jax.shard_map(local, mesh=mesh, in_specs=in_specs, out_specs=out_specs, check_vma=False)
```

```python
import jax
import jax.numpy as jnp
from jax import lax
from jax.experimental import pallas as pl
from jax.experimental.pallas import tpu as pltpu
from jax.sharding import PartitionSpec as P

Y, X = 8, 4
CAP = 48
META = 16
MESH = pl.DeviceIdType.MESH


def exp_peers():
    e = lax.axis_index("exp")
    y, x = e // X, lax.rem(e, X)
    return y, x


def moe_kernel(
    blk_ref, mixed_ref, wg_ref, wu_ref, wd_ref, out_ref,
    gath, sbuf, arr, relay, ans, ret, back, part, rs_out, rs_in, hid,
    ysend, yrecv, xsend, xrecv, fsend, frecv, rsend, rrecv, bsend, brecv, psend, precv,
):
    rows = mixed_ref.shape[0]
    width = mixed_ref.shape[1]
    half = rows // 2
    slots = X * CAP
    y, x = exp_peers()

    def device(dy, dx):
        return {"exp": lax.rem(y + dy, Y) * X + lax.rem(x + dx, X)}

    up, down = device(1, 0), device(Y - 1, 0)

    def remote(src, dst, send, recv, to):
        return pltpu.make_async_remote_copy(
            src_ref=src, dst_ref=dst, send_sem=send, recv_sem=recv,
            device_id=to, device_id_type=MESH,
        )

    barrier = pltpu.get_barrier_semaphore()
    for to in (up, down, device(0, 1), device(0, X - 1)):
        pl.semaphore_signal(barrier, inc=1, device_id=to, device_id_type=MESH)
    pl.semaphore_wait(barrier, 4)

    spans = (pl.ds(0, META + half), pl.ds(META + half, half))

    def right(k, h):
        src = blk_ref if k == 1 else gath.at[k - 1]
        return remote(src.at[spans[h]], gath.at[k, spans[h]], ysend.at[0, k - 1, h], yrecv.at[k, h], up)

    def left(k, h):
        src = blk_ref if k == 1 else gath.at[Y - k + 1]
        return remote(src.at[spans[h]], gath.at[Y - k, spans[h]], ysend.at[1, k - 1, h], yrecv.at[Y - k, h], down)

    last = Y // 2

    def sent(k, h, side):
        return k < last or (k == last and h == side)

    def places(d):
        meta = gath[d, 0:META, 0:rows].astype(jnp.float32)
        at = []
        for c in range(2):
            off = meta[2 * c : 2 * c + 1, :] - (y * X).astype(jnp.float32)
            turn = off - x.astype(jnp.float32)
            turn = jnp.where(turn < 0.0, turn + X, turn)
            mine = (off >= 0.0) & (off < float(X))
            at.append(jnp.where(mine, turn * CAP + meta[2 * c + 1 : 2 * c + 2, :], -1.0))
        line = lax.broadcasted_iota(jnp.int32, (slots, 1), 0).astype(jnp.float32)
        return meta, line == at[0], line == at[1]

    def sideways(d):
        return 1 + (X - 2) * lax.rem(d, 2)

    def dispatch(d):
        meta, hit0, hit1 = places(d)
        pick = jnp.where(hit0 | hit1, 1.0, 0.0).astype(jnp.bfloat16)
        sbuf[d] = jnp.dot(pick, gath[d, META:, :], preferred_element_type=jnp.float32).astype(jnp.bfloat16)
        arr[d, 0:CAP] = sbuf[d, 0:CAP]
        for c in (1, 3):
            span = pl.ds(c * CAP, CAP)
            remote(sbuf.at[d, span], arr.at[d, span], xsend.at[d], xrecv.at[d], device(0, c)).start()
        remote(sbuf.at[d, pl.ds(2 * CAP, CAP)], relay.at[d], xsend.at[d], frecv.at[d], device(0, sideways(d))).start()

    def pass_on(d):
        copy = remote(relay.at[d], arr.at[d, pl.ds(2 * CAP, CAP)], fsend.at[d], xrecv.at[d], device(0, sideways(d)))
        remote(sbuf.at[d, pl.ds(2 * CAP, CAP)], relay.at[d], xsend.at[d], frecv.at[d], device(0, 1)).wait_recv()
        copy.start()

    others = pl.ds(CAP, slots - CAP)

    def expert(d):
        remote(sbuf.at[d, others], arr.at[d, others], xsend.at[d], xrecv.at[d], device(0, 1)).wait_recv()
        tile = 256

        def enter(i, carry):
            cols = pl.ds(pl.multiple_of(i * tile, tile), tile)
            gate = jnp.dot(arr[d], wg_ref[0, :, cols], preferred_element_type=jnp.float32)
            lift = jnp.dot(arr[d], wu_ref[0, :, cols], preferred_element_type=jnp.float32)
            hid[:, cols] = (gate * jax.nn.sigmoid(gate) * lift).astype(jnp.bfloat16)
            return carry

        def leave(i, carry):
            cols = pl.ds(pl.multiple_of(i * tile, tile), tile)
            ans[d, :, cols] = jnp.dot(hid[...], wd_ref[0, :, cols], preferred_element_type=jnp.float32).astype(jnp.bfloat16)
            return carry

        lax.fori_loop(0, wg_ref.shape[2] // tile, enter, 0)
        lax.fori_loop(0, width // tile, leave, 0)
        ret[d, 0:CAP] = ans[d, 0:CAP]
        for c in (1, 3):
            span = pl.ds(c * CAP, CAP)
            remote(ans.at[d, span], ret.at[d, span], rsend.at[d], rrecv.at[d], device(0, X - c)).start()
        remote(ans.at[d, pl.ds(2 * CAP, CAP)], back.at[d], rsend.at[d], brecv.at[d], device(0, sideways(d))).start()

    def pass_back(d):
        copy = remote(back.at[d], ret.at[d, pl.ds(2 * CAP, CAP)], bsend.at[d], rrecv.at[d], device(0, sideways(d)))
        remote(ans.at[d, pl.ds(2 * CAP, CAP)], back.at[d], rsend.at[d], brecv.at[d], device(0, 1)).wait_recv()
        copy.start()

    def combine(d):
        remote(ans.at[d, others], ret.at[d, others], rsend.at[d], rrecv.at[d], device(0, 1)).wait_recv()
        meta, hit0, hit1 = places(d)
        share = jnp.where(hit0, meta[4:5, :], 0.0) + jnp.where(hit1, meta[5:6, :], 0.0)
        part[d] = lax.dot_general(
            share.astype(jnp.bfloat16), ret[d], (((0,), (0,)), ((), ())), preferred_element_type=jnp.float32
        )

    for h in range(2):
        right(1, h).start()
        left(1, h).start()
    gath[0] = blk_ref[...]
    dispatch(0)

    def both(fn, k):
        def one(i, carry):
            fn(k + i * (Y - 2 * k))
            return carry

        if k == 0 or k == last:
            fn(jnp.int32(k))
        else:
            lax.fori_loop(0, 2, one, 0)

    for k in range(1, last):
        for h in range(2):
            right(k, h).wait_recv()
            if sent(k + 1, h, 0):
                right(k + 1, h).start()
            left(k, h).wait_recv()
            if sent(k + 1, h, 1):
                left(k + 1, h).start()
        both(dispatch, k)
        both(pass_on, k - 1)
        both(expert, k - 1)
        if k >= 2:
            both(pass_back, k - 2)
            both(combine, k - 2)
    right(last, 0).wait_recv()
    left(last, 1).wait_recv()
    both(dispatch, last)
    both(pass_on, last - 1)
    both(expert, last - 1)
    both(pass_on, last)
    both(pass_back, last - 2)
    both(expert, last)
    both(combine, last - 2)
    both(pass_back, last - 1)
    both(combine, last - 1)
    both(pass_back, last)
    both(combine, last)

    bands = (pl.ds(0, half), pl.ds(half, half))

    def go(d, h, side):
        to = down if side == 0 else up
        land = (d - 1 if side == 0 else d + 1) if d != last else (last - 1 if side == 0 else last + 1)
        slot = Y if land == Y else land
        return remote(
            rs_out.at[d, bands[h]], rs_in.at[slot, bands[h]], psend.at[d, h], precv.at[slot, h], to
        )

    rs_out[last] = part[last].astype(jnp.bfloat16)
    go(last, 0, 0).start()
    go(last, 1, 1).start()
    for k in range(last - 1, 0, -1):
        for h in range(2):
            for side in range(2):
                d = k if side == 0 else Y - k
                total = part[d, bands[h]]
                if k < last - 1 or h == side:
                    before = (d + 1 if side == 0 else d - 1) if k < last - 1 else last
                    go(before, h, side).wait_recv()
                    total = total + rs_in[d, bands[h]].astype(jnp.float32)
                rs_out[d, bands[h]] = total.astype(jnp.bfloat16)
                go(d, h, side).start()
    for h in range(2):
        go(1, h, 0).wait_recv()
        go(Y - 1, h, 1).wait_recv()
        total = (
            mixed_ref[bands[h]].astype(jnp.float32) + part[0, bands[h]]
            + rs_in[0, bands[h]].astype(jnp.float32) + rs_in[Y, bands[h]].astype(jnp.float32)
        )
        out_ref[bands[h]] = total.astype(jnp.bfloat16)

    for k in range(1, last + 1):
        for h in range(2):
            if sent(k, h, 0):
                right(k, h).wait_send()
            if sent(k, h, 1):
                left(k, h).wait_send()
    for d in range(Y):
        for h in range(2):
            if d != 0:
                go(d, h, 0).wait_send()

    def drain(d, carry):
        remote(sbuf.at[d, others], arr.at[d, others], xsend.at[d], xrecv.at[d], device(0, 1)).wait_send()
        remote(ans.at[d, others], ret.at[d, others], rsend.at[d], rrecv.at[d], device(0, 1)).wait_send()
        tail = pl.ds(2 * CAP, CAP)
        remote(relay.at[d], arr.at[d, tail], fsend.at[d], xrecv.at[d], device(0, 1)).wait_send()
        remote(back.at[d], ret.at[d, tail], bsend.at[d], rrecv.at[d], device(0, 1)).wait_send()
        return carry

    lax.fori_loop(0, Y, drain, 0)


def moe(blk, mixed, w_gate, w_up, w_down):
    rows, width = mixed.shape
    slots = X * CAP
    bf16 = jnp.bfloat16
    dma = pltpu.SemaphoreType.DMA
    vmem = pl.BlockSpec(memory_space=pltpu.VMEM)
    return pl.pallas_call(
        moe_kernel,
        out_shape=jax.ShapeDtypeStruct((rows, width), bf16),
        in_specs=[vmem] * 5,
        out_specs=vmem,
        scratch_shapes=[
            pltpu.VMEM((Y, META + rows, width), bf16),
            pltpu.VMEM((Y, slots, width), bf16),
            pltpu.VMEM((Y, slots, width), bf16),
            pltpu.VMEM((Y, CAP, width), bf16),
            pltpu.VMEM((Y, slots, width), bf16),
            pltpu.VMEM((Y, slots, width), bf16),
            pltpu.VMEM((Y, CAP, width), bf16),
            pltpu.VMEM((Y, rows, width), jnp.float32),
            pltpu.VMEM((Y, rows, width), bf16),
            pltpu.VMEM((Y + 1, rows, width), bf16),
            pltpu.VMEM((slots, w_gate.shape[2]), bf16),
            dma((2, Y // 2, 2)), dma((Y, 2)),
            dma((Y,)), dma((Y,)), dma((Y,)), dma((Y,)),
            dma((Y,)), dma((Y,)), dma((Y,)), dma((Y,)),
            dma((Y, 2)), dma((Y + 1, 2)),
        ],
        compiler_params=pltpu.CompilerParams(
            collective_id=1, has_side_effects=True, vmem_limit_bytes=48 * 1024 * 1024
        ),
        cost_estimate=pl.CostEstimate(flops=8 * 10**9, bytes_accessed=6 * 10**6, transcendentals=10**6),
        name="expert_exchange",
    )(blk, mixed, w_gate, w_up, w_down)


Z = 8
HALO = 16
EPSILON = 1e-05
HIGHEST = lax.Precision.HIGHEST
F32 = jnp.float32
BF16 = jnp.bfloat16


def mixer_kernel(
    tok_ref, win_ref, wsmall_ref, dtb_ref, rate_ref, cw_ref, cb_ref, skip_ref, gain_ref, wout_ref, wr_ref, ids_ref,
    mixed_ref, blk_ref,
    wi, wo, normed, ext, sig, gz, step_l, tail_l, run_l, wmat, bmat, cmat, yy, decs, dec_out, states, state_out,
    gg, half_out, half_in, notes,
    isend, irecv, nsend, nrecv, osend, orecv, mosend, morecv, dsend, drecv, ssend, srecv, misc_send, misc_recv,
):
    rows, width = tok_ref.shape
    both = 2 * rows
    inner_w = wi.shape[1] // 2
    heads = skip_ref.shape[1] // 2
    head_size = inner_w // heads
    n_state = (wsmall_ref.shape[1] - 2 * heads) // 2
    in_rows = win_ref.shape[0]
    out_rows = wout_ref.shape[0]
    part = inner_w // 2
    seat = lax.axis_index("seq")
    z, c = seat // 2, lax.rem(seat, 2)
    y, x = exp_peers()
    pair = lax.rem(y, 2), lax.rem(x, 2)

    def device(dz=0, core=None, dy=0, dx=0):
        return {
            "seq": lax.rem(z + dz, Z) * 2 + (c if core is None else core),
            "exp": lax.rem(y + dy, Y) * X + lax.rem(x + dx, X),
        }

    sibling = device(core=1 - c)

    def remote(src, dst, send, recv, to):
        return pltpu.make_async_remote_copy(
            src_ref=src, dst_ref=dst, send_sem=send, recv_sem=recv, device_id=to, device_id_type=MESH
        )

    barrier = pltpu.get_barrier_semaphore()
    peers = [sibling, device(dy=1), device(dy=Y - 1), device(dx=1), device(dx=X - 1)]
    peers += [device(dz=j) for j in range(1, Z)]
    for to in peers:
        pl.semaphore_signal(barrier, inc=1, device_id=to, device_id_type=MESH)
    pl.semaphore_wait(barrier, len(peers))

    def lanes(start, size):
        return pl.ds(pl.multiple_of(start, 128), size)

    def in_band(zs, h):
        return pl.ds(pl.multiple_of((2 * zs + h) * in_rows, 16), in_rows)

    def out_band(zs, h):
        return pl.ds(pl.multiple_of(lax.rem(2 * zs + h, Z) * out_rows, 16), out_rows)

    first_in = lanes(pair[0] * part, part)
    second_in = lanes(inner_w + pair[1] * part, part)
    first_out = lanes(pair[1] * part, part)

    def origin(k, side):
        return lax.rem(z + Z - k, Z) if side == 0 else lax.rem(z + k, Z)

    def landed(k, side):
        return k if side == 0 else Z - k

    def hop(k, h, side):
        band = in_band(origin(k - 1, side), h)
        to = device(dz=1 if side == 0 else Z - 1)
        return [
            remote(wi.at[band, cols], wi.at[band, cols], isend.at[side, k - 1, h], irecv.at[landed(k, side), h], to)
            for cols in (first_in, second_in)
        ]

    def in_whole(send, recv):
        return remote(wi.at[0:in_rows, 0:inner_w], wi.at[0:in_rows, 0:inner_w], send, recv, sibling)

    def hop_arrived(k, h, side):
        in_whole(isend.at[side, k - 1, h], irecv.at[landed(k, side), h]).wait_recv()

    def share(k, h, side):
        band = in_band(origin(k, side), h)
        off = landed(k, side)
        for cols, to in (
            (first_in, device(dy=1 if h == 0 else Y - 1)),
            (second_in, device(dx=1 if h == 0 else X - 1)),
        ):
            remote(wi.at[band, cols], wi.at[band, cols], nsend.at[off, h], nrecv.at[off, h], to).start()

    def out_hop(k, h, side):
        band = out_band(origin(k - 1, side), h)
        to = device(dz=1 if side == 0 else Z - 1)
        return remote(
            wo.at[band, first_out], wo.at[band, first_out], osend.at[side, k - 1, h], orecv.at[landed(k, side), h], to
        )

    def out_share(k, h, side):
        band = out_band(origin(k, side), h)
        off = landed(k, side)
        return remote(
            wo.at[band, first_out], wo.at[band, first_out], mosend.at[off, h], morecv.at[off, h],
            device(dx=1 if h == 0 else X - 1),
        )

    last = Z // 2

    def sent(k, h, side):
        return k < last or (k == last and h == side)

    def wanted(k, side):
        return origin(k, side) // last == c

    def units(k):
        return [(h, side) for h in range(2) for side in range(2) if sent(k, h, side)]

    wi[in_band(z, c), 0:inner_w] = win_ref[:, lanes(2 * inner_w + c * inner_w, inner_w)]
    wi[in_band(z, c), inner_w:] = win_ref[:, lanes(c * inner_w, inner_w)]

    def to_sibling():
        return [
            remote(
                win_ref.at[:, lanes(base + (1 - c) * inner_w, inner_w)],
                wi.at[in_band(z, c), pl.ds(at, inner_w)],
                misc_send.at[0], misc_recv.at[0], sibling,
            )
            for base, at in ((2 * inner_w, 0), (0, inner_w))
        ]

    for copy in to_sibling():
        copy.start()
    for side in range(2):
        for copy in hop(1, c, side):
            copy.start()

    def out_to_sibling():
        return remote(wout_ref, wo.at[out_band(z, c)], misc_send.at[4], misc_recv.at[4], sibling)

    home = z // last == c

    @pl.when(home)
    def _():
        wo[out_band(z, c), :] = wout_ref[...]

    @pl.when(jnp.logical_not(home))
    def _():
        out_to_sibling().start()

    resid = tok_ref[...].astype(F32)
    scale = lax.rsqrt(jnp.mean(resid * resid, axis=-1, keepdims=True) + EPSILON)
    mine = pl.ds(pl.multiple_of(HALO + c * rows, 16), rows)
    normed[mine, :] = (resid * scale).astype(BF16)

    def rows_across():
        return remote(normed.at[mine], normed.at[mine], misc_send.at[1], misc_recv.at[1], sibling)

    rows_across().start()
    other_in = remote(
        wi.at[0:in_rows], wi.at[0:in_rows], misc_send.at[0], misc_recv.at[0], sibling
    )
    other_in.wait_recv()
    for side in range(2):
        for copy in hop(1, 1 - c, side):
            copy.start()

    rows_across().wait_recv()

    def halo():
        return remote(
            normed.at[both : both + HALO], normed.at[0:HALO], misc_send.at[2], misc_recv.at[2], device(dz=1)
        )

    @pl.when(z < Z - 1)
    def _():
        halo().start()

    @pl.when(z == 0)
    def _():
        normed[0:HALO, :] = jnp.zeros((HALO, width), BF16)

    small = jnp.dot(normed[HALO:, :], wsmall_ref[...], preferred_element_type=F32)
    bmat[...] = small[:, 0:n_state]
    cmat[...] = small[:, n_state : 2 * n_state]
    raw = small[:, 2 * n_state :] + dtb_ref[...]
    step_all = jnp.maximum(raw, 0.0) + jnp.log1p(jnp.exp(-jnp.abs(raw)))
    decay_all = -step_all * rate_ref[...]

    def own_heads(v):
        return jnp.where(c == 0, v[:, 0:heads], v[:, heads : 2 * heads])

    step = own_heads(step_all)
    log_decay = own_heads(decay_all)
    head_of = lax.broadcasted_iota(jnp.int32, (heads, inner_w), 1) // head_size
    spread = (head_of == lax.broadcasted_iota(jnp.int32, (heads, inner_w), 0)).astype(BF16)
    spread_f = spread.astype(F32)

    def expand(v):
        high = v.astype(BF16)
        low = (v - high.astype(F32)).astype(BF16)
        return jnp.dot(high, spread, preferred_element_type=F32) + jnp.dot(low, spread, preferred_element_type=F32)

    row_id = lax.broadcasted_iota(jnp.int32, (rows, rows), 0)
    col_id = lax.broadcasted_iota(jnp.int32, (rows, rows), 1)
    lower = (row_id >= col_id).astype(F32)
    upper = (row_id <= col_id).astype(F32)
    running, running_t, ends, scores = [], [], [], []
    for q in range(2):
        piece = log_decay[q * rows : (q + 1) * rows]
        run = jnp.dot(lower, piece, precision=HIGHEST, preferred_element_type=F32)
        running.append(run)
        running_t.append(
            lax.dot_general(piece, upper, (((0,), (0,)), ((), ())), precision=HIGHEST, preferred_element_type=F32)
        )
        end = run[rows - 1 : rows]
        ends.append(end)
        span = pl.ds(q * rows, rows)
        here = step[q * rows : (q + 1) * rows]
        step_l[span, :] = expand(here)
        tail_l[span, :] = expand(here * jnp.exp(end - run))
        run_l[span, :] = expand(jnp.exp(run))
        grid = lax.dot_general(
            cmat[span, :], bmat[span, :], (((1,), (1,)), ((), ())), precision=HIGHEST, preferred_element_type=F32
        )
        scores.append(jnp.where(row_id >= col_id, grid, 0.0))
    ends_l = [
        jnp.dot(jnp.broadcast_to(end, (8, heads)), spread_f, precision=HIGHEST, preferred_element_type=F32)
        for end in ends
    ]
    dec_out[...] = ends_l[0] + ends_l[1]

    def decay_copy(j):
        return remote(dec_out, decs.at[j], dsend.at[j], drecv.at[j], device(dz=j))

    def state_copy(j):
        return remote(state_out, states.at[j], ssend.at[j], srecv.at[j], device(dz=j))

    for j in range(1, Z):

        @pl.when(z + j < Z)
        def _(j=j):
            decay_copy(j).start()

    def advance(k):
        for h, side in units(k):
            hop_arrived(k, h, side)
            if k < last and sent(k + 1, h, side):
                for copy in hop(k + 1, h, side):
                    copy.start()
            share(k, h, side)

    def weigh(q):
        for i in range(heads):
            gap = jnp.minimum(running[q][:, i : i + 1] - running_t[q][i : i + 1, :], 0.0)
            wmat[q * heads + i] = (jnp.exp(gap) * scores[q]).astype(BF16)

    advance(1)
    weigh(0)
    advance(2)
    weigh(1)
    advance(3)

    experts = wr_ref.shape[1]
    lane = lax.broadcasted_iota(jnp.int32, (rows, experts), 1)
    hits = [lane == ids_ref[:, k : k + 1] for k in range(2)]
    taken = (hits[0] | hits[1]).astype(F32).astype(BF16)
    before = jnp.dot((row_id > col_id).astype(F32).astype(BF16), taken, preferred_element_type=F32)
    place = [jnp.sum(jnp.where(hit, before, 0.0), axis=1, keepdims=True) for hit in hits]
    number = [jnp.sum(jnp.where(hit, lane.astype(F32), 0.0), axis=1, keepdims=True) for hit in hits]
    wide = lax.broadcasted_iota(jnp.int32, (rows, 128), 1)
    table = jnp.where(wide == 0, number[0], 0.0)
    table = jnp.where(wide == 1, place[0], table)
    table = jnp.where(wide == 2, number[1], table)
    notes[...] = jnp.where(wide == 3, place[1], table)

    advance(last)
    for k in range(1, last + 1):
        for h, side in units(k):
            off = landed(k, side)
            in_whole(nsend.at[off, h], nrecv.at[off, h]).wait_recv()

    @pl.when(home)
    def _():
        out_to_sibling().wait_recv()
        for h, side in units(1):
            out_hop(1, h, side).start()

    def out_advance(k):
        for h, side in units(k):

            @pl.when(wanted(k, side))
            def _(h=h, side=side):
                out_hop(k, h, side).wait_recv()
                if k < last and sent(k + 1, h, side):
                    out_hop(k + 1, h, side).start()
                out_share(k, h, side).start()

    @pl.when(z > 0)
    def _():
        halo().wait_recv()

    tile = 256

    def project(i, carry):
        cols = pl.ds(pl.multiple_of(i * tile, tile), tile)
        ext[:, cols] = jnp.dot(normed[...], wi[:, cols], preferred_element_type=F32).astype(BF16).astype(F32)
        return carry

    lax.fori_loop(0, inner_w // tile, project, 0)
    taps = cw_ref.shape[0]

    def convolve(i, carry):
        cols = pl.ds(pl.multiple_of(i * 128, 128), 128)
        params = lanes(c * inner_w + i * 128, 128)
        for q in range(2):
            acc = cb_ref[:, params] + jnp.zeros((rows, 128), F32)
            for k in range(taps):
                acc = acc + cw_ref[k : k + 1, params] * ext[pl.ds(HALO - taps + 1 + k + q * rows, rows), cols]
            sig[pl.ds(q * rows, rows), cols] = acc * jax.nn.sigmoid(acc)
        return carry

    lax.fori_loop(0, inner_w // 128, convolve, 0)
    own_state = []
    for q in range(2):
        span = pl.ds(q * rows, rows)
        own_state.append(
            lax.dot_general(
                bmat[span, :].astype(BF16), (sig[span, :] * tail_l[span, :]).astype(BF16), (((0,), (0,)), ((), ())),
                preferred_element_type=F32,
            )
        )
    state_out[...] = (jnp.exp(ends_l[1][0:1]) * own_state[0] + own_state[1]).astype(BF16)
    for j in range(1, Z):

        @pl.when(z + j < Z)
        def _(j=j):
            state_copy(j).start()

        @pl.when(z < j)
        def _(j=j):
            states[j] = jnp.zeros_like(state_out)
            decs[j] = jnp.zeros_like(dec_out)

    out_advance(1)

    def project_gate(i, carry):
        cols = pl.ds(pl.multiple_of(i * tile, tile), tile)
        weight = wi[:, pl.ds(pl.multiple_of(inner_w + i * tile, tile), tile)]
        gz[:, cols] = jnp.dot(normed[HALO:, :], weight, preferred_element_type=F32)
        return carry

    lax.fori_loop(0, inner_w // tile, project_gate, 0)
    out_advance(2)
    left_lane = lax.broadcasted_iota(jnp.int32, (rows, 128), 1) < head_size

    def within(p, carry):
        cols = pl.ds(pl.multiple_of(p * 128, 128), 128)
        skips = jnp.sum(
            jnp.where(
                lax.broadcasted_iota(jnp.int32, (heads * 2, 128), 0)
                == c * heads + 2 * p + lax.broadcasted_iota(jnp.int32, (heads * 2, 128), 1) // head_size,
                jnp.broadcast_to(skip_ref[...], (128, heads * 2)).T, 0.0,
            ),
            axis=0, keepdims=True,
        )
        for q in range(2):
            span = pl.ds(q * rows, rows)
            fresh = (sig[span, cols] * step_l[span, cols]).astype(BF16)
            a = jnp.dot(wmat[q * heads + 2 * p], fresh, preferred_element_type=F32)
            b = jnp.dot(wmat[q * heads + 2 * p + 1], fresh, preferred_element_type=F32)
            yy[span, cols] = jnp.where(left_lane, a, b) + skips * sig[span, cols]
        return carry

    lax.fori_loop(0, inner_w // 128, within, 0)
    out_advance(3)
    out_advance(last)

    entry = jnp.zeros((n_state, inner_w), F32)
    lead = jnp.zeros((1, inner_w), F32)
    for j in range(1, Z):

        @pl.when(z >= j)
        def _(j=j):
            decay_copy(j).wait_recv()
            state_copy(j).wait_recv()

        entry = entry + jnp.exp(lead) * states[j].astype(F32)
        lead = lead + decs[j, 0:1]
    gain = gain_ref[:, lanes(c * inner_w, inner_w)]
    squares = []
    for q in range(2):
        span = pl.ds(q * rows, rows)
        start = entry if q == 0 else jnp.exp(ends_l[0][0:1]) * entry + own_state[0]
        across = run_l[span, :] * jnp.dot(cmat[span, :].astype(BF16), start.astype(BF16), preferred_element_type=F32)
        gate = gz[span, :]
        gated = (yy[span, :] + across) * (gate * jax.nn.sigmoid(gate))
        squares.append(jnp.sum(gated * gated, axis=1, keepdims=True))
        gg[span, :] = (gated * gain).astype(BF16)

    @pl.when(home)
    def _():
        pass

    for k in range(1, last + 1):
        for h, side in units(k):

            @pl.when(wanted(k, side))
            def _(k=k, h=h, side=side):
                out_share(k, h, side).wait_recv()

    theirs = pl.ds(pl.multiple_of((1 - c) * rows, 16), rows)
    ours = pl.ds(pl.multiple_of(c * rows, 16), rows)

    def leave(i, carry):
        cols = pl.ds(pl.multiple_of(i * tile, tile), tile)
        half_out[:, cols] = jnp.dot(gg[theirs, :], wo[:, cols], preferred_element_type=F32).astype(BF16)
        return carry

    lax.fori_loop(0, width // tile, leave, 0)
    their_square = jnp.where(c == 0, squares[1], squares[0])
    our_square = jnp.where(c == 0, squares[0], squares[1])
    high = their_square.astype(BF16).astype(F32)
    half_out[:, width:] = jnp.where(wide < 64, high, their_square - high).astype(BF16)

    def halves():
        return remote(half_out, half_in, misc_send.at[3], misc_recv.at[3], sibling)

    halves().start()

    def stay(i, carry):
        cols = pl.ds(pl.multiple_of(i * tile, tile), tile)
        yy[0:rows, cols] = jnp.dot(gg[ours, :], wo[:, cols], preferred_element_type=F32)
        return carry

    lax.fori_loop(0, width // tile, stay, 0)
    halves().wait_recv()
    extra = half_in[:, width:].astype(F32)
    total = our_square + extra[:, 0:1] + extra[:, 64:65]
    norm = lax.rsqrt(total / (2 * inner_w) + EPSILON)
    mixed = (
        tok_ref[...].astype(F32) + norm * (yy[0:rows, 0:width] + half_in[:, 0:width].astype(F32))
    ).astype(BF16)
    mixed_ref[...] = mixed
    mixed_f = mixed.astype(F32)
    routed = (mixed_f * lax.rsqrt(jnp.mean(mixed_f * mixed_f, axis=-1, keepdims=True) + EPSILON)).astype(BF16)
    blk_ref[META:, :] = routed
    logits = jnp.dot(routed, wr_ref[...], preferred_element_type=F32)
    picked = [
        jnp.sum(jnp.where(lane == ids_ref[:, k : k + 1], logits, 0.0), axis=1, keepdims=True) for k in range(2)
    ]
    first = jax.nn.sigmoid(picked[0] - picked[1])
    table = jnp.where(wide == 4, first, notes[...])
    table = jnp.where(wide == 5, 1.0 - first, table)
    blk_ref[0:META, 0:rows] = table.T[0:META, :].astype(BF16)
    blk_ref[0:META, rows:] = jnp.zeros((META, width - rows), BF16)

    for copy in (other_in, rows_across(), halves()):
        copy.wait_send()

    @pl.when(z < Z - 1)
    def _():
        halo().wait_send()

    @pl.when(jnp.logical_not(home))
    def _():
        out_to_sibling().wait_send()

    for k in range(1, last + 1):
        for h, side in units(k):
            off = landed(k, side)
            in_whole(isend.at[side, k - 1, h], irecv.at[off, h]).wait_send()
            in_whole(nsend.at[off, h], nrecv.at[off, h]).wait_send()

            @pl.when(wanted(k - 1, side))
            def _(k=k, h=h, side=side):
                out_hop(k, h, side).wait_send()

            @pl.when(wanted(k, side))
            def _(k=k, h=h, side=side):
                out_share(k, h, side).wait_send()

    for j in range(1, Z):

        @pl.when(z + j < Z)
        def _(j=j):
            decay_copy(j).wait_send()
            state_copy(j).wait_send()


def mixer(tokens, w_in, w_small, dt_bias, decay_rate, conv_w, conv_b, skip, norm_gain, w_out, w_router, ids):
    rows, width = tokens.shape
    inner_w = conv_w.shape[1] // 2
    heads = dt_bias.shape[0] // 2
    n_state = (w_small.shape[1] - 2 * heads) // 2
    both = 2 * rows
    dma = pltpu.SemaphoreType.DMA
    vmem = pl.BlockSpec(memory_space=pltpu.VMEM)
    wide = pltpu.VMEM((both, inner_w), F32)
    line = lambda v: v.reshape(1, -1)
    return pl.pallas_call(
        mixer_kernel,
        out_shape=(
            jax.ShapeDtypeStruct((rows, width), BF16),
            jax.ShapeDtypeStruct((META + rows, width), BF16),
        ),
        in_specs=[vmem] * 12,
        out_specs=(vmem, vmem),
        scratch_shapes=[
            pltpu.VMEM((width, 2 * inner_w), BF16),
            pltpu.VMEM((inner_w, width), BF16),
            pltpu.VMEM((HALO + both, width), BF16),
            pltpu.VMEM((HALO + both, inner_w), F32),
            wide, wide, wide, wide, wide,
            pltpu.VMEM((2 * heads, rows, rows), BF16),
            pltpu.VMEM((both, n_state), F32),
            pltpu.VMEM((both, n_state), F32),
            wide,
            pltpu.VMEM((Z, 8, inner_w), F32),
            pltpu.VMEM((8, inner_w), F32),
            pltpu.VMEM((Z, n_state, inner_w), BF16),
            pltpu.VMEM((n_state, inner_w), BF16),
            pltpu.VMEM((both, inner_w), BF16),
            pltpu.VMEM((rows, width + 128), BF16),
            pltpu.VMEM((rows, width + 128), BF16),
            pltpu.VMEM((rows, 128), F32),
            dma((2, Z // 2, 2)), dma((Z, 2)), dma((Z, 2)), dma((Z, 2)),
            dma((2, Z // 2, 2)), dma((Z, 2)), dma((Z, 2)), dma((Z, 2)),
            dma((Z,)), dma((Z,)), dma((Z,)), dma((Z,)),
            dma((5,)), dma((5,)),
        ],
        compiler_params=pltpu.CompilerParams(
            collective_id=2, has_side_effects=True, vmem_limit_bytes=48 * 1024 * 1024
        ),
        name="state_space_mixer",
    )(
        tokens, w_in, w_small, line(dt_bias), line(decay_rate), conv_w, line(conv_b), line(skip), line(norm_gain),
        w_out, w_router, ids,
    )


def local(
    tokens,
    w_in,
    w_small,
    dt_bias,
    decay_rate,
    conv_w,
    conv_b,
    skip,
    norm_gain,
    w_out,
    w_router,
    expert_ids,
    w_gate,
    w_up,
    w_down,
):
    mixed, block = mixer(
        tokens[0], w_in, w_small, dt_bias, decay_rate, conv_w, conv_b, skip, norm_gain, w_out, w_router, expert_ids[0]
    )
    return moe(block, mixed, w_gate, w_up, w_down)[None]


def solution(mesh):
    in_specs = (
        P("exp", "seq", None),
        P("seq", None),
        P(),
        P(),
        P(),
        P(),
        P(),
        P(),
        P(),
        P("seq", None),
        P(),
        P("exp", "seq", None),
        P("exp", None, None),
        P("exp", None, None),
        P("exp", None, None),
    )
    out_specs = P("exp", "seq", None)
    return jax.shard_map(local, mesh=mesh, in_specs=in_specs, out_specs=out_specs, check_vma=False)
```

```python
import jax
import jax.numpy as jnp
from jax import lax
from jax.experimental import pallas as pl
from jax.experimental.pallas import tpu as pltpu
from jax.sharding import PartitionSpec as P

Y, X = 8, 4
CAP = 48
META = 16
MESH = pl.DeviceIdType.MESH


def exp_peers():
    e = lax.axis_index("exp")
    return e // X, lax.rem(e, X)


Z = 8
HALO = 16
EPSILON = 1e-05
HIGHEST = lax.Precision.HIGHEST
F32 = jnp.float32
BF16 = jnp.bfloat16


def layer_kernel(
    tok_hbm, win_hbm, wsmall_hbm, dtb_hbm, rate_hbm, cw_hbm, cb_hbm, skip_hbm, gain_hbm, wout_hbm, wr_hbm, ids_hbm,
    wg_hbm, wu_hbm, wd_hbm, out_ref,
    tok_ref, win_ref, wsmall_ref, dtb_ref, rate_ref, cw_ref, cb_ref, skip_ref, gain_ref, wout_ref, wr_ref, ids_ref,
    wg_ref, wu_ref, wd_ref, mixed_ref,
    wi, wo, normed, ext, sig, gz, step_l, tail_l, run_l, wmat, bmat, cmat, yy, skip_l, decs, dec_out, states, state_out,
    gg, half_out, half_in, notes,
    gath, sbuf, arr, ans, ret, part_of, rs_out, rs_in, hid,
    fetch_sem,
    isend, irecv, nsend, nrecv, osend, orecv, mosend, morecv, dsend, drecv, ssend, srecv, misc_send, misc_recv,
    ysend, yrecv, xsend, xrecv, rsend, rrecv, psend, precv,
):
    rows, width = tok_ref.shape
    both = 2 * rows
    inner_w = wi.shape[1] // 2
    heads = skip_ref.shape[0] // 2
    head_size = inner_w // heads
    n_state = (wsmall_ref.shape[0] - 2 * heads) // 2
    in_rows = win_ref.shape[0]
    out_rows = wout_ref.shape[0]
    part = inner_w // 2
    seat = lax.axis_index("seq")
    z, c = seat // 2, lax.rem(seat, 2)
    y, x = exp_peers()
    pair = lax.rem(y, 2), lax.rem(x, 2)

    def device(dz=0, core=None, dy=0, dx=0):
        return {
            "seq": lax.rem(z + dz, Z) * 2 + (c if core is None else core),
            "exp": lax.rem(y + dy, Y) * X + lax.rem(x + dx, X),
        }

    sibling = device(core=1 - c)

    def remote(src, dst, send, recv, to):
        return pltpu.make_async_remote_copy(
            src_ref=src, dst_ref=dst, send_sem=send, recv_sem=recv, device_id=to, device_id_type=MESH
        )

    pairs = (
        (win_hbm, win_ref), (tok_hbm, tok_ref), (wout_hbm, wout_ref), (wsmall_hbm, wsmall_ref), (dtb_hbm, dtb_ref),
        (rate_hbm, rate_ref), (skip_hbm, skip_ref), (ids_hbm, ids_ref), (cw_hbm, cw_ref), (cb_hbm, cb_ref),
        (gain_hbm, gain_ref), (wr_hbm, wr_ref), (wg_hbm, wg_ref), (wu_hbm, wu_ref), (wd_hbm, wd_ref),
    )
    fetches = [pltpu.make_async_copy(src, dst, fetch_sem.at[n]) for n, (src, dst) in enumerate(pairs)]
    for copy in fetches:
        copy.start()

    barrier = pltpu.get_barrier_semaphore()
    peers = [sibling, device(dy=1), device(dy=Y - 1), device(dx=1), device(dx=X - 1)]
    peers += [device(dx=2)] + [device(dz=j) for j in range(1, Z)]
    for to in peers:
        pl.semaphore_signal(barrier, inc=1, device_id=to, device_id_type=MESH)
    pl.semaphore_wait(barrier, len(peers))

    def lanes(start, size):
        return pl.ds(pl.multiple_of(start, 128), size)

    def in_band(zs, h):
        return pl.ds(pl.multiple_of((2 * zs + h) * in_rows, 16), in_rows)

    def out_band(zs, h):
        return pl.ds(pl.multiple_of(lax.rem(2 * zs + h, Z) * out_rows, 16), out_rows)

    first_in = lanes(pair[0] * part, part)
    second_in = lanes(inner_w + pair[1] * part, part)
    first_out = lanes(pair[1] * part, part)

    def origin(k, side):
        return lax.rem(z + Z - k, Z) if side == 0 else lax.rem(z + k, Z)

    def landed(k, side):
        return k if side == 0 else Z - k

    def hop(k, h, side):
        band = in_band(origin(k - 1, side), h)
        to = device(dz=1 if side == 0 else Z - 1)
        return [
            remote(wi.at[band, cols], wi.at[band, cols], isend.at[side, k - 1, h], irecv.at[landed(k, side), h], to)
            for cols in (first_in, second_in)
        ]

    def in_whole(send, recv):
        return remote(wi.at[0:in_rows, 0:inner_w], wi.at[0:in_rows, 0:inner_w], send, recv, sibling)

    def hop_arrived(k, h, side):
        in_whole(isend.at[side, k - 1, h], irecv.at[landed(k, side), h]).wait_recv()

    def share(k, h, side):
        band = in_band(origin(k, side), h)
        off = landed(k, side)
        for cols, to in (
            (first_in, device(dy=1 if h == 0 else Y - 1)),
            (second_in, device(dx=1 if h == 0 else X - 1)),
        ):
            remote(wi.at[band, cols], wi.at[band, cols], nsend.at[off, h], nrecv.at[off, h], to).start()

    def out_hop(k, h, side):
        band = out_band(origin(k - 1, side), h)
        to = device(dz=1 if side == 0 else Z - 1)
        return remote(
            wo.at[band, first_out], wo.at[band, first_out], osend.at[side, k - 1, h], orecv.at[landed(k, side), h], to
        )

    def out_share(k, h, side):
        band = out_band(origin(k, side), h)
        off = landed(k, side)
        return remote(
            wo.at[band, first_out], wo.at[band, first_out], mosend.at[off, h], morecv.at[off, h],
            device(dx=1 if h == 0 else X - 1),
        )

    last = Z // 2

    def sent(k, h, side):
        return k < last or (k == last and h == side)

    def wanted(k, side):
        return origin(k, side) // last == c

    def units(k):
        return [(h, side) for h in range(2) for side in range(2) if sent(k, h, side)]

    fetches[0].wait()
    wi[in_band(z, c), 0:inner_w] = win_ref[:, lanes(2 * inner_w + c * inner_w, inner_w)]
    wi[in_band(z, c), inner_w:] = win_ref[:, lanes(c * inner_w, inner_w)]

    def to_sibling():
        return [
            remote(
                win_ref.at[:, lanes(base + (1 - c) * inner_w, inner_w)],
                wi.at[in_band(z, c), pl.ds(at, inner_w)],
                misc_send.at[0], misc_recv.at[0], sibling,
            )
            for base, at in ((2 * inner_w, 0), (0, inner_w))
        ]

    for copy in to_sibling():
        copy.start()
    for side in range(2):
        for copy in hop(1, c, side):
            copy.start()

    def out_to_sibling():
        return remote(wout_ref, wo.at[out_band(z, c)], misc_send.at[4], misc_recv.at[4], sibling)

    fetches[1].wait()
    fetches[2].wait()
    home = z // last == c

    @pl.when(home)
    def _():
        wo[out_band(z, c), :] = wout_ref[...]

    @pl.when(jnp.logical_not(home))
    def _():
        out_to_sibling().start()

    resid = tok_ref[...].astype(F32)
    scale = lax.rsqrt(jnp.mean(resid * resid, axis=-1, keepdims=True) + EPSILON)
    mine = pl.ds(pl.multiple_of(HALO + c * rows, 16), rows)
    normed[mine, :] = (resid * scale).astype(BF16)

    def rows_across():
        return remote(normed.at[mine], normed.at[mine], misc_send.at[1], misc_recv.at[1], sibling)

    rows_across().start()
    other_in = remote(
        wi.at[0:in_rows], wi.at[0:in_rows], misc_send.at[0], misc_recv.at[0], sibling
    )
    other_in.wait_recv()
    for side in range(2):
        for copy in hop(1, 1 - c, side):
            copy.start()

    rows_across().wait_recv()

    def halo():
        return remote(
            normed.at[both : both + HALO], normed.at[0:HALO], misc_send.at[2], misc_recv.at[2], device(dz=1)
        )

    @pl.when(z < Z - 1)
    def _():
        halo().start()

    @pl.when(z == 0)
    def _():
        normed[0:HALO, :] = jnp.zeros((HALO, width), BF16)

    for copy in fetches[3:8]:
        copy.wait()
    small = lax.dot_general(
        normed[HALO:, :], wsmall_ref[...], (((1,), (1,)), ((), ())), preferred_element_type=F32
    )
    bmat[...] = small[:, 0:n_state]
    cmat[...] = small[:, n_state : 2 * n_state]
    raw = small[:, 2 * n_state :] + dtb_ref[...].reshape(1, 2 * heads)
    step_all = jnp.maximum(raw, 0.0) + jnp.log1p(jnp.exp(-jnp.abs(raw)))
    decay_all = -step_all * rate_ref[...].reshape(1, 2 * heads)

    def own_heads(v):
        return jnp.where(c == 0, v[:, 0:heads], v[:, heads : 2 * heads])

    step = own_heads(step_all)
    log_decay = own_heads(decay_all)
    head_of = lax.broadcasted_iota(jnp.int32, (heads, inner_w), 1) // head_size
    spread = (head_of == lax.broadcasted_iota(jnp.int32, (heads, inner_w), 0)).astype(BF16)
    spread_f = spread.astype(F32)

    def expand(v):
        high = v.astype(BF16)
        low = (v - high.astype(F32)).astype(BF16)
        return jnp.dot(high, spread, preferred_element_type=F32) + jnp.dot(low, spread, preferred_element_type=F32)

    row_id = lax.broadcasted_iota(jnp.int32, (rows, rows), 0)
    col_id = lax.broadcasted_iota(jnp.int32, (rows, rows), 1)
    lower = (row_id >= col_id).astype(F32)
    upper = (row_id <= col_id).astype(F32)
    running, running_t, ends, scores = [], [], [], []
    for q in range(2):
        piece = log_decay[q * rows : (q + 1) * rows]
        run = jnp.dot(lower, piece, precision=HIGHEST, preferred_element_type=F32)
        running.append(run)
        running_t.append(
            lax.dot_general(piece, upper, (((0,), (0,)), ((), ())), precision=HIGHEST, preferred_element_type=F32)
        )
        end = run[rows - 1 : rows]
        ends.append(end)
        span = pl.ds(q * rows, rows)
        here = step[q * rows : (q + 1) * rows]
        step_l[span, :] = expand(here)
        tail_l[span, :] = expand(here * jnp.exp(end - run))
        run_l[span, :] = expand(jnp.exp(run))
        grid = lax.dot_general(
            cmat[span, :], bmat[span, :], (((1,), (1,)), ((), ())), precision=HIGHEST, preferred_element_type=F32
        )
        scores.append(jnp.where(row_id >= col_id, grid, 0.0))
    ends_l = [
        jnp.dot(jnp.broadcast_to(end, (8, heads)), spread_f, precision=HIGHEST, preferred_element_type=F32)
        for end in ends
    ]
    dec_out[...] = ends_l[0] + ends_l[1]
    skip_l[...] = jnp.dot(
        jnp.broadcast_to(own_heads(skip_ref[...].reshape(1, 2 * heads)), (8, heads)), spread_f,
        precision=HIGHEST, preferred_element_type=F32,
    )

    def decay_copy(j):
        return remote(dec_out, decs.at[j], dsend.at[j], drecv.at[j], device(dz=j))

    def state_copy(j):
        return remote(state_out, states.at[j], ssend.at[j], srecv.at[j], device(dz=j))

    for j in range(1, Z):

        @pl.when(z + j < Z)
        def _(j=j):
            decay_copy(j).start()

    def advance(k):
        for h, side in units(k):
            hop_arrived(k, h, side)
            if k < last and sent(k + 1, h, side):
                for copy in hop(k + 1, h, side):
                    copy.start()
            share(k, h, side)

    def weigh(q):
        for i in range(heads):
            gap = jnp.minimum(running[q][:, i : i + 1] - running_t[q][i : i + 1, :], 0.0)
            wmat[q * heads + i] = (jnp.exp(gap) * scores[q]).astype(BF16)

    @pl.when(home)
    def _():
        out_to_sibling().wait_recv()
        for h, side in units(1):
            out_hop(1, h, side).start()

    def out_advance(k):
        for h, side in units(k):

            @pl.when(wanted(k, side))
            def _(h=h, side=side):
                out_hop(k, h, side).wait_recv()
                if k < last and sent(k + 1, h, side):
                    out_hop(k + 1, h, side).start()
                out_share(k, h, side).start()

    advance(1)
    weigh(0)
    advance(2)
    out_advance(1)
    weigh(1)
    advance(3)
    out_advance(2)

    experts = wr_ref.shape[0]
    line = lax.broadcasted_iota(jnp.int32, (experts, rows), 0)
    hits = [line == ids_ref[k : k + 1, :] for k in range(2)]
    taken = (hits[0] | hits[1]).astype(F32).astype(BF16)
    before = jnp.dot(taken, (row_id < col_id).astype(F32).astype(BF16), preferred_element_type=F32)
    for k in range(2):
        notes[2 * k : 2 * k + 1, :] = jnp.sum(jnp.where(hits[k], line.astype(F32), 0.0), axis=0, keepdims=True)
        notes[2 * k + 1 : 2 * k + 2, :] = jnp.sum(jnp.where(hits[k], before, 0.0), axis=0, keepdims=True)
    notes[6:, :] = jnp.zeros((META - 6, rows), F32)

    advance(last)
    for k in range(1, last + 1):
        for h, side in units(k):
            off = landed(k, side)
            in_whole(nsend.at[off, h], nrecv.at[off, h]).wait_recv()

    out_advance(3)

    @pl.when(z > 0)
    def _():
        halo().wait_recv()

    tile = 256

    def project(i, carry):
        cols = pl.ds(pl.multiple_of(i * tile, tile), tile)
        ext[:, cols] = jnp.dot(normed[...], wi[:, cols], preferred_element_type=F32).astype(BF16).astype(F32)
        return carry

    lax.fori_loop(0, inner_w // tile, project, 0)
    for copy in fetches[8:12]:
        copy.wait()
    taps = cw_ref.shape[0]

    def convolve(i, carry):
        cols = pl.ds(pl.multiple_of(i * 128, 128), 128)
        params = lanes(c * inner_w + i * 128, 128)
        for q in range(2):
            acc = cb_ref[params].reshape(1, 128) + jnp.zeros((rows, 128), F32)
            for k in range(taps):
                acc = acc + cw_ref[k : k + 1, params] * ext[pl.ds(HALO - taps + 1 + k + q * rows, rows), cols]
            sig[pl.ds(q * rows, rows), cols] = acc * jax.nn.sigmoid(acc)
        return carry

    lax.fori_loop(0, inner_w // 128, convolve, 0)
    own_state = []
    for q in range(2):
        span = pl.ds(q * rows, rows)
        own_state.append(
            lax.dot_general(
                bmat[span, :].astype(BF16), (sig[span, :] * tail_l[span, :]).astype(BF16), (((0,), (0,)), ((), ())),
                preferred_element_type=F32,
            )
        )
    state_out[...] = (jnp.exp(ends_l[1][0:1]) * own_state[0] + own_state[1]).astype(BF16)
    for j in range(1, Z):

        @pl.when(z + j < Z)
        def _(j=j):
            state_copy(j).start()

        @pl.when(z < j)
        def _(j=j):
            states[j] = jnp.zeros_like(state_out)
            decs[j] = jnp.zeros_like(dec_out)

    out_advance(last)

    def project_gate(i, carry):
        cols = pl.ds(pl.multiple_of(i * tile, tile), tile)
        weight = wi[:, pl.ds(pl.multiple_of(inner_w + i * tile, tile), tile)]
        gz[:, cols] = jnp.dot(normed[HALO:, :], weight, preferred_element_type=F32)
        return carry

    lax.fori_loop(0, inner_w // tile, project_gate, 0)
    left_lane = lax.broadcasted_iota(jnp.int32, (rows, 128), 1) < head_size

    def within(p, carry):
        cols = pl.ds(pl.multiple_of(p * 128, 128), 128)
        skips = skip_l[0:1, cols]
        for q in range(2):
            span = pl.ds(q * rows, rows)
            fresh = (sig[span, cols] * step_l[span, cols]).astype(BF16)
            a = jnp.dot(wmat[q * heads + 2 * p], fresh, preferred_element_type=F32)
            b = jnp.dot(wmat[q * heads + 2 * p + 1], fresh, preferred_element_type=F32)
            yy[span, cols] = jnp.where(left_lane, a, b) + skips * sig[span, cols]
        return carry

    lax.fori_loop(0, inner_w // 128, within, 0)

    entry = jnp.zeros((n_state, inner_w), F32)
    lead = jnp.zeros((1, inner_w), F32)
    for j in range(1, Z):

        @pl.when(z >= j)
        def _(j=j):
            decay_copy(j).wait_recv()
            state_copy(j).wait_recv()

        entry = entry + jnp.exp(lead) * states[j].astype(F32)
        lead = lead + decs[j, 0:1]
    gain = gain_ref[lanes(c * inner_w, inner_w)].reshape(1, inner_w)
    squares = []
    for q in range(2):
        span = pl.ds(q * rows, rows)
        start = entry if q == 0 else jnp.exp(ends_l[0][0:1]) * entry + own_state[0]
        across = run_l[span, :] * jnp.dot(cmat[span, :].astype(BF16), start.astype(BF16), preferred_element_type=F32)
        gate = gz[span, :]
        gated = (yy[span, :] + across) * (gate * jax.nn.sigmoid(gate))
        squares.append(jnp.sum(gated * gated, axis=1, keepdims=True))
        gg[span, :] = (gated * gain).astype(BF16)

    for k in range(1, last + 1):
        for h, side in units(k):

            @pl.when(wanted(k, side))
            def _(k=k, h=h, side=side):
                out_share(k, h, side).wait_recv()

    theirs = pl.ds(pl.multiple_of((1 - c) * rows, 16), rows)
    ours = pl.ds(pl.multiple_of(c * rows, 16), rows)

    def leave(i, carry):
        cols = pl.ds(pl.multiple_of(i * tile, tile), tile)
        half_out[:, cols] = jnp.dot(gg[theirs, :], wo[:, cols], preferred_element_type=F32).astype(BF16)
        return carry

    lax.fori_loop(0, width // tile, leave, 0)
    wide = lax.broadcasted_iota(jnp.int32, (rows, 128), 1)
    their_square = jnp.where(c == 0, squares[1], squares[0])
    our_square = jnp.where(c == 0, squares[0], squares[1])
    high = their_square.astype(BF16).astype(F32)
    half_out[:, width:] = jnp.where(wide < 64, high, their_square - high).astype(BF16)

    def halves():
        return remote(half_out, half_in, misc_send.at[3], misc_recv.at[3], sibling)

    halves().start()

    def stay(i, carry):
        cols = pl.ds(pl.multiple_of(i * tile, tile), tile)
        yy[0:rows, cols] = jnp.dot(gg[ours, :], wo[:, cols], preferred_element_type=F32)
        return carry

    lax.fori_loop(0, width // tile, stay, 0)
    halves().wait_recv()
    extra = half_in[:, width:].astype(F32)
    total = our_square + extra[:, 0:1] + extra[:, 64:65]
    norm = lax.rsqrt(total / (2 * inner_w) + EPSILON)
    mixed = (
        tok_ref[...].astype(F32) + norm * (yy[0:rows, 0:width] + half_in[:, 0:width].astype(F32))
    ).astype(BF16)
    mixed_ref[...] = mixed
    mixed_f = mixed.astype(F32)
    routed = (mixed_f * lax.rsqrt(jnp.mean(mixed_f * mixed_f, axis=-1, keepdims=True) + EPSILON)).astype(BF16)
    gath[0, META:, :] = routed
    logits = lax.dot_general(wr_ref[...], routed, (((1,), (1,)), ((), ())), preferred_element_type=F32)
    picked = [jnp.sum(jnp.where(hit, logits, 0.0), axis=0, keepdims=True) for hit in hits]
    first = jax.nn.sigmoid(picked[0] - picked[1])
    notes[4:5, :] = first
    notes[5:6, :] = 1.0 - first
    gath[0, 0:META, 0:rows] = notes[...].astype(BF16)
    gath[0, 0:META, rows:] = jnp.zeros((META, width - rows), BF16)

    for copy in fetches[12:]:
        copy.wait()
    half = rows // 2
    slots = X * CAP
    up, down = device(dy=1), device(dy=Y - 1)
    spans = (pl.ds(0, META + half), pl.ds(META + half, half))
    bands = (pl.ds(0, half), pl.ds(half, half))

    def right(k, h):
        return remote(
            gath.at[k - 1, spans[h]], gath.at[k, spans[h]], ysend.at[0, k - 1, h], yrecv.at[k, h], up
        )

    def left(k, h):
        return remote(
            gath.at[(Y - k + 1) % Y, spans[h]], gath.at[Y - k, spans[h]], ysend.at[1, k - 1, h], yrecv.at[Y - k, h], down
        )

    def seat_of(d):
        return 0 if d == 0 else 1 if d == last else 2 * d if d < last else 2 * (Y - d) + 1

    def places(d):
        meta = gath[d, 0:META, 0:rows].astype(F32)
        at = []
        for k in range(2):
            off = meta[2 * k : 2 * k + 1, :] - (y * X).astype(F32)
            turn = off - x.astype(F32)
            turn = jnp.where(turn < 0.0, turn + X, turn)
            inside = (off >= 0.0) & (off < float(X))
            at.append(jnp.where(inside, turn * CAP + meta[2 * k + 1 : 2 * k + 2, :], -1.0))
        order = lax.broadcasted_iota(jnp.int32, (slots, 1), 0).astype(F32)
        return meta, order == at[0], order == at[1]

    def slab(n, k=0, size=slots):
        return pl.ds(n * slots + k * CAP, size)

    def sideways(n, k):
        return remote(sbuf.at[slab(n, k, CAP)], arr.at[slab(n, k, CAP)], xsend.at[n], xrecv.at[n], device(dx=k))

    def homeward(n, k):
        return remote(ans.at[slab(n, k, CAP)], ret.at[slab(n, k, CAP)], rsend.at[n], rrecv.at[n], device(dx=X - k))

    def all_sideways(n):
        span = slab(n, 1, slots - CAP)
        return remote(sbuf.at[span], arr.at[span], xsend.at[n], xrecv.at[n], up)

    def all_homeward(n):
        span = slab(n, 1, slots - CAP)
        return remote(ans.at[span], ret.at[span], rsend.at[n], rrecv.at[n], up)

    def dispatch(d):
        n = seat_of(d)
        meta, hit0, hit1 = places(d)
        pick = jnp.where(hit0 | hit1, 1.0, 0.0).astype(BF16)
        sbuf[slab(n), :] = jnp.dot(pick, gath[d, META:, :], preferred_element_type=F32).astype(BF16)
        for k in (2, 1, 3):
            sideways(n, k).start()
        arr[slab(n, 0, CAP), :] = sbuf[slab(n, 0, CAP), :]

    def expert(first_seat, count):
        for n in range(first_seat, first_seat + count):
            all_sideways(n).wait_recv()
        span = pl.ds(first_seat * slots, count * slots)
        inside = pl.ds(0, count * slots)

        def enter(i, carry):
            cols = pl.ds(pl.multiple_of(i * tile, tile), tile)
            gate = jnp.dot(arr[span, :], wg_ref[0, :, cols], preferred_element_type=F32)
            lift = jnp.dot(arr[span, :], wu_ref[0, :, cols], preferred_element_type=F32)
            hid[inside, cols] = (gate * jax.nn.sigmoid(gate) * lift).astype(BF16)
            return carry

        def close(i, carry):
            cols = pl.ds(pl.multiple_of(i * tile, tile), tile)
            ans[span, cols] = jnp.dot(hid[inside, :], wd_ref[0, :, cols], preferred_element_type=F32).astype(BF16)
            return carry

        lax.fori_loop(0, wg_ref.shape[2] // tile, enter, 0)
        lax.fori_loop(0, width // tile, close, 0)
        for n in range(first_seat, first_seat + count):
            for k in (2, 1, 3):
                homeward(n, k).start()
            ret[slab(n, 0, CAP), :] = ans[slab(n, 0, CAP), :]

    def combine(d):
        n = seat_of(d)
        all_homeward(n).wait_recv()
        meta, hit0, hit1 = places(d)
        share_of = jnp.where(hit0, meta[4:5, :], 0.0) + jnp.where(hit1, meta[5:6, :], 0.0)
        part_of[d] = lax.dot_general(
            share_of.astype(BF16), ret[slab(n), :], (((0,), (0,)), ((), ())), preferred_element_type=F32
        )

    def ring(k):
        for h in range(2):
            if sent(k, h, 0):
                right(k, h).wait_recv()
                if k < last and sent(k + 1, h, 0):
                    right(k + 1, h).start()
            if sent(k, h, 1):
                left(k, h).wait_recv()
                if k < last and sent(k + 1, h, 1):
                    left(k + 1, h).start()

    for h in range(2):
        right(1, h).start()
        left(1, h).start()
    dispatch(0)
    ring(1)
    dispatch(1)
    dispatch(Y - 1)
    ring(2)
    dispatch(2)
    dispatch(Y - 2)
    expert(seat_of(0), 1)
    ring(3)
    dispatch(3)
    dispatch(Y - 3)
    expert(seat_of(1), 2)
    combine(0)
    ring(last)
    dispatch(last)
    expert(seat_of(3), 2)
    expert(seat_of(last), 1)
    expert(seat_of(2), 2)

    def target(d, side):
        return d - 1 if side == 0 else d + 1

    def go(d, h, side):
        land = target(d, side)
        return remote(
            rs_out.at[d, bands[h]], rs_in.at[land, bands[h]], psend.at[d, h], precv.at[land, h],
            down if side == 0 else up,
        )

    def push(k, h, side):
        d = k if side == 0 else Y - k
        total = part_of[d, bands[h]]
        if k < last - 1 or (k == last - 1 and h == side):
            before_d = d + 1 if side == 0 else d - 1
            go(before_d, h, side).wait_recv()
            total = total + rs_in[d, bands[h]].astype(F32)
        rs_out[d, bands[h]] = total.astype(BF16)
        go(d, h, side).start()

    combine(3)
    push(3, 1, 0)
    combine(Y - 3)
    push(3, 0, 1)
    combine(last)
    push(last, 0, 0)
    push(last, 1, 1)
    combine(2)
    combine(Y - 2)
    push(2, 1, 0)
    push(2, 0, 1)
    combine(1)
    combine(Y - 1)
    push(3, 0, 0)
    push(3, 1, 1)
    push(1, 1, 0)
    push(1, 0, 1)
    push(2, 0, 0)
    push(2, 1, 1)
    push(1, 0, 0)
    push(1, 1, 1)
    for h in range(2):
        go(1, h, 0).wait_recv()
        go(Y - 1, h, 1).wait_recv()
        total = (
            mixed_ref[bands[h]].astype(F32) + part_of[0, bands[h]]
            + rs_in[0, bands[h]].astype(F32) + rs_in[Y, bands[h]].astype(F32)
        )
        out_ref[bands[h]] = total.astype(BF16)

    for copy in (other_in, rows_across(), halves()):
        copy.wait_send()

    @pl.when(z < Z - 1)
    def _():
        halo().wait_send()

    @pl.when(jnp.logical_not(home))
    def _():
        out_to_sibling().wait_send()

    for k in range(1, last + 1):
        for h, side in units(k):
            off = landed(k, side)
            in_whole(isend.at[side, k - 1, h], irecv.at[off, h]).wait_send()
            in_whole(nsend.at[off, h], nrecv.at[off, h]).wait_send()

            @pl.when(wanted(k - 1, side))
            def _(k=k, h=h, side=side):
                out_hop(k, h, side).wait_send()

            @pl.when(wanted(k, side))
            def _(k=k, h=h, side=side):
                out_share(k, h, side).wait_send()

    for j in range(1, Z):

        @pl.when(z + j < Z)
        def _(j=j):
            decay_copy(j).wait_send()
            state_copy(j).wait_send()
    for k in range(1, last + 1):
        for h in range(2):
            if sent(k, h, 0):
                right(k, h).wait_send()
            if sent(k, h, 1):
                left(k, h).wait_send()
    for d in range(Y):
        for h in range(2):
            if d != 0:
                go(d, h, 0).wait_send()
        all_sideways(d).wait_send()
        all_homeward(d).wait_send()


def layer(tokens, w_in, w_small, dt_bias, decay_rate, conv_w, conv_b, skip, norm_gain, w_out, w_router, ids, *experts):
    rows, width = tokens.shape
    inner_w = conv_w.shape[1] // 2
    heads = dt_bias.shape[0] // 2
    n_state = (w_small.shape[0] - 2 * heads) // 2
    both = 2 * rows
    slots = X * CAP
    hidden = experts[0].shape[2]
    dma = pltpu.SemaphoreType.DMA
    wide = pltpu.VMEM((both, inner_w), F32)
    operands = (
        tokens, w_in, w_small, dt_bias, decay_rate, conv_w, conv_b, skip, norm_gain, w_out, w_router, ids, *experts
    )
    return pl.pallas_call(
        layer_kernel,
        out_shape=jax.ShapeDtypeStruct((rows, width), BF16),
        in_specs=[pl.BlockSpec(memory_space=pltpu.HBM)] * len(operands),
        out_specs=pl.BlockSpec(memory_space=pltpu.VMEM),
        scratch_shapes=[pltpu.VMEM(v.shape, v.dtype) for v in operands] + [
            pltpu.VMEM((rows, width), BF16),
            pltpu.VMEM((width, 2 * inner_w), BF16),
            pltpu.VMEM((inner_w, width), BF16),
            pltpu.VMEM((HALO + both, width), BF16),
            pltpu.VMEM((HALO + both, inner_w), F32),
            wide, wide, wide, wide, wide,
            pltpu.VMEM((2 * heads, rows, rows), BF16),
            pltpu.VMEM((both, n_state), F32),
            pltpu.VMEM((both, n_state), F32),
            wide,
            pltpu.VMEM((8, inner_w), F32),
            pltpu.VMEM((Z, 8, inner_w), F32),
            pltpu.VMEM((8, inner_w), F32),
            pltpu.VMEM((Z, n_state, inner_w), BF16),
            pltpu.VMEM((n_state, inner_w), BF16),
            pltpu.VMEM((both, inner_w), BF16),
            pltpu.VMEM((rows, width + 128), BF16),
            pltpu.VMEM((rows, width + 128), BF16),
            pltpu.VMEM((META, rows), F32),
            pltpu.VMEM((Y, META + rows, width), BF16),
            pltpu.VMEM((Y * slots, width), BF16),
            pltpu.VMEM((Y * slots, width), BF16),
            pltpu.VMEM((Y * slots, width), BF16),
            pltpu.VMEM((Y * slots, width), BF16),
            pltpu.VMEM((Y, rows, width), F32),
            pltpu.VMEM((Y, rows, width), BF16),
            pltpu.VMEM((Y + 1, rows, width), BF16),
            pltpu.VMEM((2 * slots, hidden), BF16),
            dma((len(operands),)),
            dma((2, Z // 2, 2)), dma((Z, 2)), dma((Z, 2)), dma((Z, 2)),
            dma((2, Z // 2, 2)), dma((Z, 2)), dma((Z, 2)), dma((Z, 2)),
            dma((Z,)), dma((Z,)), dma((Z,)), dma((Z,)),
            dma((5,)), dma((5,)),
            dma((2, Y // 2, 2)), dma((Y, 2)), dma((Y,)), dma((Y,)), dma((Y,)), dma((Y,)),
            dma((Y, 2)), dma((Y + 1, 2)),
        ],
        compiler_params=pltpu.CompilerParams(
            collective_id=1, has_side_effects=True, vmem_limit_bytes=60 * 1024 * 1024
        ),
        name="mixer_and_experts",
    )(*operands)


def local(
    tokens,
    w_in,
    w_small,
    dt_bias,
    decay_rate,
    conv_w,
    conv_b,
    skip,
    norm_gain,
    w_out,
    w_router,
    expert_ids,
    w_gate,
    w_up,
    w_down,
):
    return layer(
        tokens[0], w_in, w_small.T, dt_bias, decay_rate, conv_w, conv_b, skip, norm_gain, w_out, w_router.T,
        expert_ids[0].T, w_gate, w_up, w_down,
    )[None]


def solution(mesh):
    in_specs = (
        P("exp", "seq", None),
        P("seq", None),
        P(),
        P(),
        P(),
        P(),
        P(),
        P(),
        P(),
        P("seq", None),
        P(),
        P("exp", "seq", None),
        P("exp", None, None),
        P("exp", None, None),
        P("exp", None, None),
    )
    out_specs = P("exp", "seq", None)
    return jax.shard_map(local, mesh=mesh, in_specs=in_specs, out_specs=out_specs, check_vma=False)
```

```python
import jax
import jax.numpy as jnp
from jax import lax
from jax.experimental import pallas as pl
from jax.experimental.pallas import tpu as pltpu
from jax.sharding import PartitionSpec as P

Y, X = 8, 4
CAP = 48
META = 16
MESH = pl.DeviceIdType.MESH


def exp_peers():
    e = lax.axis_index("exp")
    return e // X, lax.rem(e, X)


Z = 8
HALO = 16
EPSILON = 1e-05
HIGHEST = lax.Precision.HIGHEST
F32 = jnp.float32
BF16 = jnp.bfloat16


def layer_kernel(
    tok_hbm, win_hbm, wsmall_hbm, dtb_hbm, rate_hbm, cw_hbm, cb_hbm, skip_hbm, gain_hbm, wout_hbm, wr_hbm, ids_hbm,
    wg_hbm, wu_hbm, wd_hbm, out_ref,
    tok_ref, win_ref, wsmall_ref, dtb_ref, rate_ref, cw_ref, cb_ref, skip_ref, gain_ref, wout_ref, wr_ref, ids_ref,
    wg_ref, wu_ref, wd_ref, mixed_ref,
    wi, wo, normed, ext, sig, gz, step_l, tail_l, run_l, wmat, bmat, cmat, yy, skip_l, decs, dec_out, states, state_out,
    gg, half_out, half_in, notes,
    gath, memo, sbuf, arr, ans, ret, part_of, rs_out, rs_in, hid,
    fetch_sem,
    isend, irecv, nsend, nrecv, osend, orecv, mosend, morecv, dsend, drecv, ssend, srecv, misc_send, misc_recv,
    ysend, yrecv, asend, arecv, xsend, xrecv, rsend, rrecv, psend, precv,
):
    rows, width = tok_ref.shape
    both = 2 * rows
    inner_w = wi.shape[1] // 2
    heads = skip_ref.shape[0] // 2
    head_size = inner_w // heads
    n_state = (wsmall_ref.shape[0] - 2 * heads) // 2
    in_rows = win_ref.shape[0]
    out_rows = wout_ref.shape[0]
    part = inner_w // 2
    seat = lax.axis_index("seq")
    z, c = seat // 2, lax.rem(seat, 2)
    y, x = exp_peers()
    pair = lax.rem(y, 2), lax.rem(x, 2)

    def device(dz=0, core=None, dy=0, dx=0):
        return {
            "seq": lax.rem(z + dz, Z) * 2 + (c if core is None else core),
            "exp": lax.rem(y + dy, Y) * X + lax.rem(x + dx, X),
        }

    sibling = device(core=1 - c)

    def remote(src, dst, send, recv, to):
        return pltpu.make_async_remote_copy(
            src_ref=src, dst_ref=dst, send_sem=send, recv_sem=recv, device_id=to, device_id_type=MESH
        )

    pairs = (
        (win_hbm, win_ref), (tok_hbm, tok_ref), (wout_hbm, wout_ref), (wsmall_hbm, wsmall_ref), (dtb_hbm, dtb_ref),
        (rate_hbm, rate_ref), (skip_hbm, skip_ref), (ids_hbm, ids_ref), (cw_hbm, cw_ref), (cb_hbm, cb_ref),
        (gain_hbm, gain_ref), (wr_hbm, wr_ref), (wg_hbm, wg_ref), (wu_hbm, wu_ref), (wd_hbm, wd_ref),
    )
    fetches = [pltpu.make_async_copy(src, dst, fetch_sem.at[n]) for n, (src, dst) in enumerate(pairs)]
    for copy in fetches:
        copy.start()

    barrier = pltpu.get_barrier_semaphore()
    peers = [sibling, device(dy=1), device(dy=Y - 1), device(dx=1), device(dx=X - 1)]
    peers += [device(dx=2)] + [device(dz=j) for j in range(1, Z)]
    for to in peers:
        pl.semaphore_signal(barrier, inc=1, device_id=to, device_id_type=MESH)
    pl.semaphore_wait(barrier, len(peers))

    def lanes(start, size):
        return pl.ds(pl.multiple_of(start, 128), size)

    def in_band(zs, h):
        return pl.ds(pl.multiple_of((2 * zs + h) * in_rows, 16), in_rows)

    def out_band(zs, h):
        return pl.ds(pl.multiple_of(lax.rem(2 * zs + h, Z) * out_rows, 16), out_rows)

    first_in = lanes(pair[0] * part, part)
    second_in = lanes(inner_w + pair[1] * part, part)
    first_out = lanes(pair[1] * part, part)

    def origin(k, side):
        return lax.rem(z + Z - k, Z) if side == 0 else lax.rem(z + k, Z)

    def landed(k, side):
        return k if side == 0 else Z - k

    def hop(k, h, side):
        band = in_band(origin(k - 1, side), h)
        to = device(dz=1 if side == 0 else Z - 1)
        return [
            remote(wi.at[band, cols], wi.at[band, cols], isend.at[side, k - 1, h], irecv.at[landed(k, side), h], to)
            for cols in (first_in, second_in)
        ]

    def in_whole(send, recv):
        return remote(wi.at[0:in_rows, 0:inner_w], wi.at[0:in_rows, 0:inner_w], send, recv, sibling)

    def hop_arrived(k, h, side):
        in_whole(isend.at[side, k - 1, h], irecv.at[landed(k, side), h]).wait_recv()

    def share(k, h, side):
        band = in_band(origin(k, side), h)
        off = landed(k, side)
        for cols, to in (
            (first_in, device(dy=1 if h == 0 else Y - 1)),
            (second_in, device(dx=1 if h == 0 else X - 1)),
        ):
            remote(wi.at[band, cols], wi.at[band, cols], nsend.at[off, h], nrecv.at[off, h], to).start()

    def out_hop(k, h, side):
        band = out_band(origin(k - 1, side), h)
        to = device(dz=1 if side == 0 else Z - 1)
        return remote(
            wo.at[band, first_out], wo.at[band, first_out], osend.at[side, k - 1, h], orecv.at[landed(k, side), h], to
        )

    def out_share(k, h, side):
        band = out_band(origin(k, side), h)
        off = landed(k, side)
        return remote(
            wo.at[band, first_out], wo.at[band, first_out], mosend.at[off, h], morecv.at[off, h],
            device(dx=1 if h == 0 else X - 1),
        )

    last = Z // 2

    def sent(k, h, side):
        return k < last or (k == last and h == side)

    def wanted(k, side):
        return origin(k, side) // last == c

    def units(k):
        return [(h, side) for h in range(2) for side in range(2) if sent(k, h, side)]

    fetches[0].wait()
    wi[in_band(z, c), 0:inner_w] = win_ref[:, lanes(2 * inner_w + c * inner_w, inner_w)]
    wi[in_band(z, c), inner_w:] = win_ref[:, lanes(c * inner_w, inner_w)]

    def to_sibling():
        return [
            remote(
                win_ref.at[:, lanes(base + (1 - c) * inner_w, inner_w)],
                wi.at[in_band(z, c), pl.ds(at, inner_w)],
                misc_send.at[0], misc_recv.at[0], sibling,
            )
            for base, at in ((2 * inner_w, 0), (0, inner_w))
        ]

    for copy in to_sibling():
        copy.start()
    for side in range(2):
        for copy in hop(1, c, side):
            copy.start()

    def out_to_sibling():
        return remote(wout_ref, wo.at[out_band(z, c)], misc_send.at[4], misc_recv.at[4], sibling)

    fetches[1].wait()
    fetches[2].wait()
    home = z // last == c

    @pl.when(home)
    def _():
        wo[out_band(z, c), :] = wout_ref[...]

    @pl.when(jnp.logical_not(home))
    def _():
        out_to_sibling().start()

    resid = tok_ref[...].astype(F32)
    scale = lax.rsqrt(jnp.mean(resid * resid, axis=-1, keepdims=True) + EPSILON)
    mine = pl.ds(pl.multiple_of(HALO + c * rows, 16), rows)
    normed[mine, :] = (resid * scale).astype(BF16)

    def rows_across():
        return remote(normed.at[mine], normed.at[mine], misc_send.at[1], misc_recv.at[1], sibling)

    rows_across().start()
    other_in = remote(
        wi.at[0:in_rows], wi.at[0:in_rows], misc_send.at[0], misc_recv.at[0], sibling
    )
    other_in.wait_recv()
    for side in range(2):
        for copy in hop(1, 1 - c, side):
            copy.start()

    rows_across().wait_recv()

    def halo():
        return remote(
            normed.at[both : both + HALO], normed.at[0:HALO], misc_send.at[2], misc_recv.at[2], device(dz=1)
        )

    @pl.when(z < Z - 1)
    def _():
        halo().start()

    @pl.when(z == 0)
    def _():
        normed[0:HALO, :] = jnp.zeros((HALO, width), BF16)

    for copy in fetches[3:8]:
        copy.wait()
    small = lax.dot_general(
        normed[HALO:, :], wsmall_ref[...], (((1,), (1,)), ((), ())), preferred_element_type=F32
    )
    bmat[...] = small[:, 0:n_state]
    cmat[...] = small[:, n_state : 2 * n_state]
    raw = small[:, 2 * n_state :] + dtb_ref[...].reshape(1, 2 * heads)
    step_all = jnp.maximum(raw, 0.0) + jnp.log1p(jnp.exp(-jnp.abs(raw)))
    decay_all = -step_all * rate_ref[...].reshape(1, 2 * heads)

    def own_heads(v):
        return jnp.where(c == 0, v[:, 0:heads], v[:, heads : 2 * heads])

    step = own_heads(step_all)
    log_decay = own_heads(decay_all)
    head_of = lax.broadcasted_iota(jnp.int32, (heads, inner_w), 1) // head_size
    spread = (head_of == lax.broadcasted_iota(jnp.int32, (heads, inner_w), 0)).astype(BF16)
    spread_f = spread.astype(F32)

    def expand(v):
        high = v.astype(BF16)
        low = (v - high.astype(F32)).astype(BF16)
        return jnp.dot(high, spread, preferred_element_type=F32) + jnp.dot(low, spread, preferred_element_type=F32)

    row_id = lax.broadcasted_iota(jnp.int32, (rows, rows), 0)
    col_id = lax.broadcasted_iota(jnp.int32, (rows, rows), 1)
    lower = (row_id >= col_id).astype(F32)
    upper = (row_id <= col_id).astype(F32)
    running, running_t, ends, scores = [], [], [], []
    for q in range(2):
        piece = log_decay[q * rows : (q + 1) * rows]
        run = jnp.dot(lower, piece, precision=HIGHEST, preferred_element_type=F32)
        running.append(run)
        running_t.append(
            lax.dot_general(piece, upper, (((0,), (0,)), ((), ())), precision=HIGHEST, preferred_element_type=F32)
        )
        end = run[rows - 1 : rows]
        ends.append(end)
        span = pl.ds(q * rows, rows)
        here = step[q * rows : (q + 1) * rows]
        step_l[span, :] = expand(here)
        tail_l[span, :] = expand(here * jnp.exp(end - run))
        run_l[span, :] = expand(jnp.exp(run))
        grid = lax.dot_general(
            cmat[span, :], bmat[span, :], (((1,), (1,)), ((), ())), precision=HIGHEST, preferred_element_type=F32
        )
        scores.append(jnp.where(row_id >= col_id, grid, 0.0))
    ends_l = [
        jnp.dot(jnp.broadcast_to(end, (8, heads)), spread_f, precision=HIGHEST, preferred_element_type=F32)
        for end in ends
    ]
    dec_out[...] = ends_l[0] + ends_l[1]
    skip_l[...] = jnp.dot(
        jnp.broadcast_to(own_heads(skip_ref[...].reshape(1, 2 * heads)), (8, heads)), spread_f,
        precision=HIGHEST, preferred_element_type=F32,
    )

    def decay_copy(j):
        return remote(dec_out, decs.at[j], dsend.at[j], drecv.at[j], device(dz=j))

    def state_copy(j):
        return remote(state_out, states.at[j], ssend.at[j], srecv.at[j], device(dz=j))

    for j in range(1, Z):

        @pl.when(z + j < Z)
        def _(j=j):
            decay_copy(j).start()

    def advance(k):
        for h, side in units(k):
            hop_arrived(k, h, side)
            if k < last and sent(k + 1, h, side):
                for copy in hop(k + 1, h, side):
                    copy.start()
            share(k, h, side)

    def weigh(q):
        for i in range(heads):
            gap = jnp.minimum(running[q][:, i : i + 1] - running_t[q][i : i + 1, :], 0.0)
            wmat[q * heads + i] = (jnp.exp(gap) * scores[q]).astype(BF16)

    @pl.when(home)
    def _():
        out_to_sibling().wait_recv()
        for h, side in units(1):
            out_hop(1, h, side).start()

    def out_advance(k):
        for h, side in units(k):

            @pl.when(wanted(k, side))
            def _(h=h, side=side):
                out_hop(k, h, side).wait_recv()
                if k < last and sent(k + 1, h, side):
                    out_hop(k + 1, h, side).start()
                out_share(k, h, side).start()

    advance(1)
    weigh(0)
    advance(2)
    out_advance(1)
    weigh(1)
    advance(3)
    out_advance(2)

    experts = wr_ref.shape[0]
    line = lax.broadcasted_iota(jnp.int32, (experts, rows), 0)
    hits = [line == ids_ref[k : k + 1, :] for k in range(2)]
    taken = (hits[0] | hits[1]).astype(F32).astype(BF16)
    before = jnp.dot(taken, (row_id < col_id).astype(F32).astype(BF16), preferred_element_type=F32)
    for k in range(2):
        notes[2 * k : 2 * k + 1, :] = jnp.sum(jnp.where(hits[k], line.astype(F32), 0.0), axis=0, keepdims=True)
        notes[2 * k + 1 : 2 * k + 2, :] = jnp.sum(jnp.where(hits[k], before, 0.0), axis=0, keepdims=True)
    notes[6:, :] = jnp.zeros((META - 6, rows), F32)

    advance(last)
    for k in range(1, last + 1):
        for h, side in units(k):
            off = landed(k, side)
            in_whole(nsend.at[off, h], nrecv.at[off, h]).wait_recv()

    out_advance(3)

    @pl.when(z > 0)
    def _():
        halo().wait_recv()

    tile = 256

    def project(i, carry):
        cols = pl.ds(pl.multiple_of(i * tile, tile), tile)
        ext[:, cols] = jnp.dot(normed[...], wi[:, cols], preferred_element_type=F32).astype(BF16).astype(F32)
        return carry

    lax.fori_loop(0, inner_w // tile, project, 0)
    for copy in fetches[8:12]:
        copy.wait()
    taps = cw_ref.shape[0]

    def convolve(i, carry):
        cols = pl.ds(pl.multiple_of(i * 128, 128), 128)
        params = lanes(c * inner_w + i * 128, 128)
        for q in range(2):
            acc = cb_ref[params].reshape(1, 128) + jnp.zeros((rows, 128), F32)
            for k in range(taps):
                acc = acc + cw_ref[k : k + 1, params] * ext[pl.ds(HALO - taps + 1 + k + q * rows, rows), cols]
            sig[pl.ds(q * rows, rows), cols] = acc * jax.nn.sigmoid(acc)
        return carry

    lax.fori_loop(0, inner_w // 128, convolve, 0)
    own_state = []
    for q in range(2):
        span = pl.ds(q * rows, rows)
        own_state.append(
            lax.dot_general(
                bmat[span, :].astype(BF16), (sig[span, :] * tail_l[span, :]).astype(BF16), (((0,), (0,)), ((), ())),
                preferred_element_type=F32,
            )
        )
    state_out[...] = (jnp.exp(ends_l[1][0:1]) * own_state[0] + own_state[1]).astype(BF16)
    for j in range(1, Z):

        @pl.when(z + j < Z)
        def _(j=j):
            state_copy(j).start()

        @pl.when(z < j)
        def _(j=j):
            states[j] = jnp.zeros_like(state_out)
            decs[j] = jnp.zeros_like(dec_out)

    out_advance(last)

    def project_gate(i, carry):
        cols = pl.ds(pl.multiple_of(i * tile, tile), tile)
        weight = wi[:, pl.ds(pl.multiple_of(inner_w + i * tile, tile), tile)]
        gz[:, cols] = jnp.dot(normed[HALO:, :], weight, preferred_element_type=F32)
        return carry

    lax.fori_loop(0, inner_w // tile, project_gate, 0)
    left_lane = lax.broadcasted_iota(jnp.int32, (rows, 128), 1) < head_size

    def within(p, carry):
        cols = pl.ds(pl.multiple_of(p * 128, 128), 128)
        skips = skip_l[0:1, cols]
        for q in range(2):
            span = pl.ds(q * rows, rows)
            fresh = (sig[span, cols] * step_l[span, cols]).astype(BF16)
            a = jnp.dot(wmat[q * heads + 2 * p], fresh, preferred_element_type=F32)
            b = jnp.dot(wmat[q * heads + 2 * p + 1], fresh, preferred_element_type=F32)
            yy[span, cols] = jnp.where(left_lane, a, b) + skips * sig[span, cols]
        return carry

    lax.fori_loop(0, inner_w // 128, within, 0)

    entry = jnp.zeros((n_state, inner_w), F32)
    lead = jnp.zeros((1, inner_w), F32)
    for j in range(1, Z):

        @pl.when(z >= j)
        def _(j=j):
            decay_copy(j).wait_recv()
            state_copy(j).wait_recv()

        entry = entry + jnp.exp(lead) * states[j].astype(F32)
        lead = lead + decs[j, 0:1]
    gain = gain_ref[lanes(c * inner_w, inner_w)].reshape(1, inner_w)
    squares = []
    for q in range(2):
        span = pl.ds(q * rows, rows)
        start = entry if q == 0 else jnp.exp(ends_l[0][0:1]) * entry + own_state[0]
        across = run_l[span, :] * jnp.dot(cmat[span, :].astype(BF16), start.astype(BF16), preferred_element_type=F32)
        gate = gz[span, :]
        gated = (yy[span, :] + across) * (gate * jax.nn.sigmoid(gate))
        squares.append(jnp.sum(gated * gated, axis=1, keepdims=True))
        gg[span, :] = (gated * gain).astype(BF16)

    for k in range(1, last + 1):
        for h, side in units(k):

            @pl.when(wanted(k, side))
            def _(k=k, h=h, side=side):
                out_share(k, h, side).wait_recv()

    theirs = pl.ds(pl.multiple_of((1 - c) * rows, 16), rows)
    ours = pl.ds(pl.multiple_of(c * rows, 16), rows)

    def leave(i, carry):
        cols = pl.ds(pl.multiple_of(i * tile, tile), tile)
        half_out[:, cols] = jnp.dot(gg[theirs, :], wo[:, cols], preferred_element_type=F32).astype(BF16)
        return carry

    lax.fori_loop(0, width // tile, leave, 0)
    wide = lax.broadcasted_iota(jnp.int32, (rows, 128), 1)
    their_square = jnp.where(c == 0, squares[1], squares[0])
    our_square = jnp.where(c == 0, squares[0], squares[1])
    high = their_square.astype(BF16).astype(F32)
    half_out[:, width:] = jnp.where(wide < 64, high, their_square - high).astype(BF16)

    def halves():
        return remote(half_out, half_in, misc_send.at[3], misc_recv.at[3], sibling)

    halves().start()

    def stay(i, carry):
        cols = pl.ds(pl.multiple_of(i * tile, tile), tile)
        yy[0:rows, cols] = jnp.dot(gg[ours, :], wo[:, cols], preferred_element_type=F32)
        return carry

    lax.fori_loop(0, width // tile, stay, 0)
    halves().wait_recv()
    extra = half_in[:, width:].astype(F32)
    total = our_square + extra[:, 0:1] + extra[:, 64:65]
    norm = lax.rsqrt(total / (2 * inner_w) + EPSILON)
    mixed = (
        tok_ref[...].astype(F32) + norm * (yy[0:rows, 0:width] + half_in[:, 0:width].astype(F32))
    ).astype(BF16)
    mixed_ref[...] = mixed
    mixed_f = mixed.astype(F32)
    routed = (mixed_f * lax.rsqrt(jnp.mean(mixed_f * mixed_f, axis=-1, keepdims=True) + EPSILON)).astype(BF16)
    gath[0] = routed
    logits = lax.dot_general(wr_ref[...], routed, (((1,), (1,)), ((), ())), preferred_element_type=F32)
    picked = [jnp.sum(jnp.where(hit, logits, 0.0), axis=0, keepdims=True) for hit in hits]
    first = jax.nn.sigmoid(picked[0] - picked[1])
    notes[4:5, :] = first
    notes[5:6, :] = 1.0 - first
    memo[0] = notes[...].astype(BF16)

    for copy in fetches[12:]:
        copy.wait()
    half = rows // 2
    slots = X * CAP
    up, down = device(dy=1), device(dy=Y - 1)
    bands = (pl.ds(0, half), pl.ds(half, half))

    def right(k, h):
        return remote(
            gath.at[k - 1, bands[h]], gath.at[k, bands[h]], ysend.at[0, k - 1, h], yrecv.at[k, h], up
        )

    def left(k, h):
        return remote(
            gath.at[(Y - k + 1) % Y, bands[h]], gath.at[Y - k, bands[h]], ysend.at[1, k - 1, h], yrecv.at[Y - k, h], down
        )

    def notes_right(k):
        return remote(memo.at[k - 1], memo.at[k], asend.at[0, k - 1], arecv.at[k], up)

    def notes_left(k):
        return remote(memo.at[(Y - k + 1) % Y], memo.at[Y - k], asend.at[1, k - 1], arecv.at[Y - k], down)

    def seat_of(d):
        return 0 if d == 0 else 1 if d == last else 2 * d if d < last else 2 * (Y - d) + 1

    def places(d):
        meta = memo[d].astype(F32)
        at = []
        for k in range(2):
            off = meta[2 * k : 2 * k + 1, :] - (y * X).astype(F32)
            turn = off - x.astype(F32)
            turn = jnp.where(turn < 0.0, turn + X, turn)
            inside = (off >= 0.0) & (off < float(X))
            at.append(jnp.where(inside, turn * CAP + meta[2 * k + 1 : 2 * k + 2, :], -1.0))
        order = lax.broadcasted_iota(jnp.int32, (slots, 1), 0).astype(F32)
        return meta, order == at[0], order == at[1]

    def slab(n, k=0, size=slots):
        return pl.ds(n * slots + k * CAP, size)

    def sideways(n, k):
        return remote(sbuf.at[slab(n, k, CAP)], arr.at[slab(n, k, CAP)], xsend.at[n], xrecv.at[n], device(dx=k))

    def homeward(n, k):
        return remote(ans.at[slab(n, k, CAP)], ret.at[slab(n, k, CAP)], rsend.at[n], rrecv.at[n], device(dx=X - k))

    def all_sideways(n):
        span = slab(n, 1, slots - CAP)
        return remote(sbuf.at[span], arr.at[span], xsend.at[n], xrecv.at[n], up)

    def all_homeward(n):
        span = slab(n, 1, slots - CAP)
        return remote(ans.at[span], ret.at[span], rsend.at[n], rrecv.at[n], up)

    def dispatch(d):
        n = seat_of(d)
        meta, hit0, hit1 = places(d)
        pick = jnp.where(hit0 | hit1, 1.0, 0.0).astype(BF16)
        sbuf[slab(n), :] = jnp.dot(pick, gath[d], preferred_element_type=F32).astype(BF16)
        for k in (2, 1, 3):
            sideways(n, k).start()
        arr[slab(n, 0, CAP), :] = sbuf[slab(n, 0, CAP), :]

    def expert(first_seat, count):
        for n in range(first_seat, first_seat + count):
            all_sideways(n).wait_recv()
        span = pl.ds(first_seat * slots, count * slots)
        inside = pl.ds(0, count * slots)

        def enter(i, carry):
            cols = pl.ds(pl.multiple_of(i * tile, tile), tile)
            gate = jnp.dot(arr[span, :], wg_ref[0, :, cols], preferred_element_type=F32)
            lift = jnp.dot(arr[span, :], wu_ref[0, :, cols], preferred_element_type=F32)
            hid[inside, cols] = (gate * jax.nn.sigmoid(gate) * lift).astype(BF16)
            return carry

        def close(i, carry):
            cols = pl.ds(pl.multiple_of(i * tile, tile), tile)
            ans[span, cols] = jnp.dot(hid[inside, :], wd_ref[0, :, cols], preferred_element_type=F32).astype(BF16)
            return carry

        lax.fori_loop(0, wg_ref.shape[2] // tile, enter, 0)
        lax.fori_loop(0, width // tile, close, 0)
        for n in range(first_seat, first_seat + count):
            for k in (2, 1, 3):
                homeward(n, k).start()
            ret[slab(n, 0, CAP), :] = ans[slab(n, 0, CAP), :]

    def combine(d):
        n = seat_of(d)
        all_homeward(n).wait_recv()
        meta, hit0, hit1 = places(d)
        share_of = jnp.where(hit0, meta[4:5, :], 0.0) + jnp.where(hit1, meta[5:6, :], 0.0)
        part_of[d] = lax.dot_general(
            share_of.astype(BF16), ret[slab(n), :], (((0,), (0,)), ((), ())), preferred_element_type=F32
        )

    def ring(k, h):
        if sent(k, h, 0):
            right(k, h).wait_recv()
            if k < last and sent(k + 1, h, 0):
                right(k + 1, h).start()
        if sent(k, h, 1):
            left(k, h).wait_recv()
            if k < last and sent(k + 1, h, 1):
                left(k + 1, h).start()
        if h == 0:
            notes_right(k).wait_recv()
            if k < last:
                notes_left(k).wait_recv()
                notes_right(k + 1).start()
            if k < last - 1:
                notes_left(k + 1).start()

    for h in range(2):
        right(1, h).start()
        left(1, h).start()
        if h == 0:
            notes_right(1).start()
            notes_left(1).start()
    dispatch(0)
    ring(1, 0)
    ring(1, 1)
    dispatch(1)
    dispatch(Y - 1)
    expert(seat_of(0), 1)
    ring(2, 0)
    expert(seat_of(1), 2)
    ring(2, 1)
    dispatch(2)
    dispatch(Y - 2)
    combine(0)
    ring(3, 0)
    expert(seat_of(2), 2)
    ring(3, 1)
    dispatch(3)
    dispatch(Y - 3)
    combine(1)
    combine(Y - 1)
    ring(last, 0)
    ring(last, 1)
    dispatch(last)
    expert(seat_of(3), 2)
    expert(seat_of(last), 1)

    def target(d, side):
        return d - 1 if side == 0 else d + 1

    def go(d, h, side):
        land = target(d, side)
        return remote(
            rs_out.at[d, bands[h]], rs_in.at[land, bands[h]], psend.at[d, h], precv.at[land, h],
            down if side == 0 else up,
        )

    def push(k, h, side):
        d = k if side == 0 else Y - k
        total = part_of[d, bands[h]]
        if k < last - 1 or (k == last - 1 and h == side):
            before_d = d + 1 if side == 0 else d - 1
            go(before_d, h, side).wait_recv()
            total = total + rs_in[d, bands[h]].astype(F32)
        rs_out[d, bands[h]] = total.astype(BF16)
        go(d, h, side).start()

    combine(2)
    combine(Y - 2)
    combine(3)
    push(3, 1, 0)
    combine(Y - 3)
    push(3, 0, 1)
    combine(last)
    push(last, 0, 0)
    push(last, 1, 1)
    push(2, 1, 0)
    push(2, 0, 1)
    push(3, 0, 0)
    push(3, 1, 1)
    push(1, 1, 0)
    push(1, 0, 1)
    push(2, 0, 0)
    push(2, 1, 1)
    push(1, 0, 0)
    push(1, 1, 1)
    for h in range(2):
        go(1, h, 0).wait_recv()
        go(Y - 1, h, 1).wait_recv()
        total = (
            mixed_ref[bands[h]].astype(F32) + part_of[0, bands[h]]
            + rs_in[0, bands[h]].astype(F32) + rs_in[Y, bands[h]].astype(F32)
        )
        out_ref[bands[h]] = total.astype(BF16)

    for copy in (other_in, rows_across(), halves()):
        copy.wait_send()

    @pl.when(z < Z - 1)
    def _():
        halo().wait_send()

    @pl.when(jnp.logical_not(home))
    def _():
        out_to_sibling().wait_send()

    for k in range(1, last + 1):
        for h, side in units(k):
            off = landed(k, side)
            in_whole(isend.at[side, k - 1, h], irecv.at[off, h]).wait_send()
            in_whole(nsend.at[off, h], nrecv.at[off, h]).wait_send()

            @pl.when(wanted(k - 1, side))
            def _(k=k, h=h, side=side):
                out_hop(k, h, side).wait_send()

            @pl.when(wanted(k, side))
            def _(k=k, h=h, side=side):
                out_share(k, h, side).wait_send()

    for j in range(1, Z):

        @pl.when(z + j < Z)
        def _(j=j):
            decay_copy(j).wait_send()
            state_copy(j).wait_send()
    for k in range(1, last + 1):
        notes_right(k).wait_send()
        if k < last:
            notes_left(k).wait_send()
        for h in range(2):
            if sent(k, h, 0):
                right(k, h).wait_send()
            if sent(k, h, 1):
                left(k, h).wait_send()
    for d in range(Y):
        for h in range(2):
            if d != 0:
                go(d, h, 0).wait_send()
        all_sideways(d).wait_send()
        all_homeward(d).wait_send()


def layer(tokens, w_in, w_small, dt_bias, decay_rate, conv_w, conv_b, skip, norm_gain, w_out, w_router, ids, *experts):
    rows, width = tokens.shape
    inner_w = conv_w.shape[1] // 2
    heads = dt_bias.shape[0] // 2
    n_state = (w_small.shape[0] - 2 * heads) // 2
    both = 2 * rows
    slots = X * CAP
    hidden = experts[0].shape[2]
    dma = pltpu.SemaphoreType.DMA
    wide = pltpu.VMEM((both, inner_w), F32)
    operands = (
        tokens, w_in, w_small, dt_bias, decay_rate, conv_w, conv_b, skip, norm_gain, w_out, w_router, ids, *experts
    )
    return pl.pallas_call(
        layer_kernel,
        out_shape=jax.ShapeDtypeStruct((rows, width), BF16),
        in_specs=[pl.BlockSpec(memory_space=pltpu.HBM)] * len(operands),
        out_specs=pl.BlockSpec(memory_space=pltpu.VMEM),
        scratch_shapes=[pltpu.VMEM(v.shape, v.dtype) for v in operands] + [
            pltpu.VMEM((rows, width), BF16),
            pltpu.VMEM((width, 2 * inner_w), BF16),
            pltpu.VMEM((inner_w, width), BF16),
            pltpu.VMEM((HALO + both, width), BF16),
            pltpu.VMEM((HALO + both, inner_w), F32),
            wide, wide, wide, wide, wide,
            pltpu.VMEM((2 * heads, rows, rows), BF16),
            pltpu.VMEM((both, n_state), F32),
            pltpu.VMEM((both, n_state), F32),
            wide,
            pltpu.VMEM((8, inner_w), F32),
            pltpu.VMEM((Z, 8, inner_w), F32),
            pltpu.VMEM((8, inner_w), F32),
            pltpu.VMEM((Z, n_state, inner_w), BF16),
            pltpu.VMEM((n_state, inner_w), BF16),
            pltpu.VMEM((both, inner_w), BF16),
            pltpu.VMEM((rows, width + 128), BF16),
            pltpu.VMEM((rows, width + 128), BF16),
            pltpu.VMEM((META, rows), F32),
            pltpu.VMEM((Y, rows, width), BF16),
            pltpu.VMEM((Y, META, rows), BF16),
            pltpu.VMEM((Y * slots, width), BF16),
            pltpu.VMEM((Y * slots, width), BF16),
            pltpu.VMEM((Y * slots, width), BF16),
            pltpu.VMEM((Y * slots, width), BF16),
            pltpu.VMEM((Y, rows, width), F32),
            pltpu.VMEM((Y, rows, width), BF16),
            pltpu.VMEM((Y + 1, rows, width), BF16),
            pltpu.VMEM((2 * slots, hidden), BF16),
            dma((len(operands),)),
            dma((2, Z // 2, 2)), dma((Z, 2)), dma((Z, 2)), dma((Z, 2)),
            dma((2, Z // 2, 2)), dma((Z, 2)), dma((Z, 2)), dma((Z, 2)),
            dma((Z,)), dma((Z,)), dma((Z,)), dma((Z,)),
            dma((5,)), dma((5,)),
            dma((2, Y // 2, 2)), dma((Y, 2)), dma((2, Y // 2)), dma((Y,)), dma((Y,)), dma((Y,)), dma((Y,)), dma((Y,)),
            dma((Y, 2)), dma((Y + 1, 2)),
        ],
        compiler_params=pltpu.CompilerParams(
            collective_id=1, has_side_effects=True, vmem_limit_bytes=60 * 1024 * 1024
        ),
        name="mixer_and_experts",
    )(*operands)


def local(
    tokens,
    w_in,
    w_small,
    dt_bias,
    decay_rate,
    conv_w,
    conv_b,
    skip,
    norm_gain,
    w_out,
    w_router,
    expert_ids,
    w_gate,
    w_up,
    w_down,
):
    return layer(
        tokens[0], w_in, w_small.T, dt_bias, decay_rate, conv_w, conv_b, skip, norm_gain, w_out, w_router.T,
        expert_ids[0].T, w_gate, w_up, w_down,
    )[None]


def solution(mesh):
    in_specs = (
        P("exp", "seq", None),
        P("seq", None),
        P(),
        P(),
        P(),
        P(),
        P(),
        P(),
        P(),
        P("seq", None),
        P(),
        P("exp", "seq", None),
        P("exp", None, None),
        P("exp", None, None),
        P("exp", None, None),
    )
    out_specs = P("exp", "seq", None)
    return jax.shard_map(local, mesh=mesh, in_specs=in_specs, out_specs=out_specs, check_vma=False)
```

```python
import jax
import jax.numpy as jnp
from jax import lax
from jax.experimental import pallas as pl
from jax.experimental.pallas import tpu as pltpu
from jax.sharding import PartitionSpec as P

Y, X = 8, 4
CAP = 48
META = 16
MESH = pl.DeviceIdType.MESH


def exp_peers():
    e = lax.axis_index("exp")
    return e // X, lax.rem(e, X)


Z = 8
HALO = 16
EPSILON = 1e-05
HIGHEST = lax.Precision.HIGHEST
F32 = jnp.float32
BF16 = jnp.bfloat16


def layer_kernel(
    tok_hbm, win_hbm, wsmall_hbm, dtb_hbm, rate_hbm, cw_hbm, cb_hbm, skip_hbm, gain_hbm, wout_hbm, wr_hbm, ids_hbm,
    wg_hbm, wu_hbm, wd_hbm, out_ref,
    tok_ref, win_ref, wsmall_ref, dtb_ref, rate_ref, cw_ref, cb_ref, skip_ref, gain_ref, wout_ref, wr_ref, ids_ref,
    wg_ref, wu_ref, wd_ref, mixed_ref,
    wi, wo, normed, ext, sig, gz, step_l, tail_l, run_l, wmat, bmat, cmat, yy, skip_l, decs, dec_out, states, state_out,
    gg, half_out, half_in, notes,
    gath, memo, sbuf, arr, ans, ret, part_of, rs_out, rs_in, hid,
    fetch_sem,
    isend, irecv, nsend, nrecv, osend, orecv, mosend, morecv, dsend, drecv, ssend, srecv, misc_send, misc_recv,
    ysend, yrecv, asend, arecv, xsend, xrecv, rsend, rrecv, psend, precv,
):
    rows, width = tok_ref.shape
    both = 2 * rows
    inner_w = wi.shape[1] // 2
    heads = skip_ref.shape[0] // 2
    head_size = inner_w // heads
    n_state = (wsmall_ref.shape[0] - 2 * heads) // 2
    in_rows = win_ref.shape[0]
    out_rows = wout_ref.shape[0]
    part = inner_w // 2
    seat = lax.axis_index("seq")
    z, c = seat // 2, lax.rem(seat, 2)
    y, x = exp_peers()
    pair = lax.rem(y, 2), lax.rem(x, 2)

    def device(dz=0, core=None, dy=0, dx=0):
        return {
            "seq": lax.rem(z + dz, Z) * 2 + (c if core is None else core),
            "exp": lax.rem(y + dy, Y) * X + lax.rem(x + dx, X),
        }

    sibling = device(core=1 - c)

    def remote(src, dst, send, recv, to):
        return pltpu.make_async_remote_copy(
            src_ref=src, dst_ref=dst, send_sem=send, recv_sem=recv, device_id=to, device_id_type=MESH
        )

    pairs = (
        (win_hbm, win_ref), (tok_hbm, tok_ref), (wout_hbm, wout_ref), (wsmall_hbm, wsmall_ref), (dtb_hbm, dtb_ref),
        (rate_hbm, rate_ref), (skip_hbm, skip_ref), (ids_hbm, ids_ref), (cw_hbm, cw_ref), (cb_hbm, cb_ref),
        (gain_hbm, gain_ref), (wr_hbm, wr_ref), (wg_hbm, wg_ref), (wu_hbm, wu_ref), (wd_hbm, wd_ref),
    )
    fetches = [pltpu.make_async_copy(src, dst, fetch_sem.at[n]) for n, (src, dst) in enumerate(pairs)]
    for copy in fetches:
        copy.start()

    barrier = pltpu.get_barrier_semaphore()
    peers = [sibling, device(dy=1), device(dy=Y - 1), device(dx=1), device(dx=X - 1)]
    peers += [device(dx=2)] + [device(dz=j) for j in range(1, Z)]
    for to in peers:
        pl.semaphore_signal(barrier, inc=1, device_id=to, device_id_type=MESH)
    pl.semaphore_wait(barrier, len(peers))

    def lanes(start, size):
        return pl.ds(pl.multiple_of(start, 128), size)

    def in_band(zs, h):
        return pl.ds(pl.multiple_of((2 * zs + h) * in_rows, 16), in_rows)

    def out_band(zs, h):
        return pl.ds(pl.multiple_of(lax.rem(2 * zs + h, Z) * out_rows, 16), out_rows)

    first_in = lanes(pair[0] * part, part)
    second_in = lanes(inner_w + pair[1] * part, part)
    first_out = lanes(pair[1] * part, part)

    def origin(k, side):
        return lax.rem(z + Z - k, Z) if side == 0 else lax.rem(z + k, Z)

    def landed(k, side):
        return k if side == 0 else Z - k

    def hop(k, h, side):
        band = in_band(origin(k - 1, side), h)
        to = device(dz=1 if side == 0 else Z - 1)
        return [
            remote(wi.at[band, cols], wi.at[band, cols], isend.at[side, k - 1, h], irecv.at[landed(k, side), h], to)
            for cols in (first_in, second_in)
        ]

    def in_whole(send, recv):
        return remote(wi.at[0:in_rows, 0:inner_w], wi.at[0:in_rows, 0:inner_w], send, recv, sibling)

    def hop_arrived(k, h, side):
        in_whole(isend.at[side, k - 1, h], irecv.at[landed(k, side), h]).wait_recv()

    def share(k, h, side):
        band = in_band(origin(k, side), h)
        off = landed(k, side)
        for cols, to in (
            (first_in, device(dy=1 if h == 0 else Y - 1)),
            (second_in, device(dx=1 if h == 0 else X - 1)),
        ):
            remote(wi.at[band, cols], wi.at[band, cols], nsend.at[off, h], nrecv.at[off, h], to).start()

    def out_hop(k, h, side):
        band = out_band(origin(k - 1, side), h)
        to = device(dz=1 if side == 0 else Z - 1)
        return remote(
            wo.at[band, first_out], wo.at[band, first_out], osend.at[side, k - 1, h], orecv.at[landed(k, side), h], to
        )

    def out_share(k, h, side):
        band = out_band(origin(k, side), h)
        off = landed(k, side)
        return remote(
            wo.at[band, first_out], wo.at[band, first_out], mosend.at[off, h], morecv.at[off, h],
            device(dx=1 if h == 0 else X - 1),
        )

    last = Z // 2

    def sent(k, h, side):
        return k < last or (k == last and h == side)

    def wanted(k, side):
        return origin(k, side) // last == c

    def units(k):
        return [(h, side) for h in range(2) for side in range(2) if sent(k, h, side)]

    fetches[0].wait()
    wi[in_band(z, c), 0:inner_w] = win_ref[:, lanes(2 * inner_w + c * inner_w, inner_w)]
    wi[in_band(z, c), inner_w:] = win_ref[:, lanes(c * inner_w, inner_w)]

    def to_sibling():
        return [
            remote(
                win_ref.at[:, lanes(base + (1 - c) * inner_w, inner_w)],
                wi.at[in_band(z, c), pl.ds(at, inner_w)],
                misc_send.at[0], misc_recv.at[0], sibling,
            )
            for base, at in ((2 * inner_w, 0), (0, inner_w))
        ]

    for copy in to_sibling():
        copy.start()
    for side in range(2):
        for copy in hop(1, c, side):
            copy.start()

    def out_to_sibling():
        return remote(wout_ref, wo.at[out_band(z, c)], misc_send.at[4], misc_recv.at[4], sibling)

    fetches[1].wait()
    fetches[2].wait()
    home = z // last == c

    @pl.when(home)
    def _():
        wo[out_band(z, c), :] = wout_ref[...]

    @pl.when(jnp.logical_not(home))
    def _():
        out_to_sibling().start()

    resid = tok_ref[...].astype(F32)
    scale = lax.rsqrt(jnp.mean(resid * resid, axis=-1, keepdims=True) + EPSILON)
    mine = pl.ds(pl.multiple_of(HALO + c * rows, 16), rows)
    normed[mine, :] = (resid * scale).astype(BF16)

    def rows_across():
        return remote(normed.at[mine], normed.at[mine], misc_send.at[1], misc_recv.at[1], sibling)

    rows_across().start()
    other_in = remote(
        wi.at[0:in_rows], wi.at[0:in_rows], misc_send.at[0], misc_recv.at[0], sibling
    )
    other_in.wait_recv()
    for side in range(2):
        for copy in hop(1, 1 - c, side):
            copy.start()

    rows_across().wait_recv()

    def halo():
        return remote(
            normed.at[both : both + HALO], normed.at[0:HALO], misc_send.at[2], misc_recv.at[2], device(dz=1)
        )

    @pl.when(z < Z - 1)
    def _():
        halo().start()

    @pl.when(z == 0)
    def _():
        normed[0:HALO, :] = jnp.zeros((HALO, width), BF16)

    for copy in fetches[3:8]:
        copy.wait()
    small = lax.dot_general(
        normed[HALO:, :], wsmall_ref[...], (((1,), (1,)), ((), ())), preferred_element_type=F32
    )
    bmat[...] = small[:, 0:n_state]
    cmat[...] = small[:, n_state : 2 * n_state]
    raw = small[:, 2 * n_state :] + dtb_ref[...].reshape(1, 2 * heads)
    step_all = jnp.maximum(raw, 0.0) + jnp.log1p(jnp.exp(-jnp.abs(raw)))
    decay_all = -step_all * rate_ref[...].reshape(1, 2 * heads)

    def own_heads(v):
        return jnp.where(c == 0, v[:, 0:heads], v[:, heads : 2 * heads])

    step = own_heads(step_all)
    log_decay = own_heads(decay_all)
    def advance(k):
        for h, side in units(k):
            hop_arrived(k, h, side)
            if k < last and sent(k + 1, h, side):
                for copy in hop(k + 1, h, side):
                    copy.start()
            share(k, h, side)

    @pl.when(home)
    def _():
        out_to_sibling().wait_recv()
        for h, side in units(1):
            out_hop(1, h, side).start()

    def out_advance(k):
        for h, side in units(k):

            @pl.when(wanted(k, side))
            def _(h=h, side=side):
                out_hop(k, h, side).wait_recv()
                if k < last and sent(k + 1, h, side):
                    out_hop(k + 1, h, side).start()
                out_share(k, h, side).start()

    advance(1)
    head_of = lax.broadcasted_iota(jnp.int32, (heads, inner_w), 1) // head_size
    spread = (head_of == lax.broadcasted_iota(jnp.int32, (heads, inner_w), 0)).astype(BF16)
    spread_f = spread.astype(F32)

    def expand(v):
        high = v.astype(BF16)
        low = (v - high.astype(F32)).astype(BF16)
        return jnp.dot(high, spread, preferred_element_type=F32) + jnp.dot(low, spread, preferred_element_type=F32)

    row_id = lax.broadcasted_iota(jnp.int32, (rows, rows), 0)
    col_id = lax.broadcasted_iota(jnp.int32, (rows, rows), 1)
    lower = (row_id >= col_id).astype(F32)
    upper = (row_id <= col_id).astype(F32)
    running, running_t, ends, scores = [], [], [], []
    for q in range(2):
        piece = log_decay[q * rows : (q + 1) * rows]
        run = jnp.dot(lower, piece, precision=HIGHEST, preferred_element_type=F32)
        running.append(run)
        running_t.append(
            lax.dot_general(piece, upper, (((0,), (0,)), ((), ())), precision=HIGHEST, preferred_element_type=F32)
        )
        end = run[rows - 1 : rows]
        ends.append(end)
        span = pl.ds(q * rows, rows)
        here = step[q * rows : (q + 1) * rows]
        step_l[span, :] = expand(here)
        tail_l[span, :] = expand(here * jnp.exp(end - run))
        run_l[span, :] = expand(jnp.exp(run))
        grid = lax.dot_general(
            cmat[span, :], bmat[span, :], (((1,), (1,)), ((), ())), precision=HIGHEST, preferred_element_type=F32
        )
        scores.append(jnp.where(row_id >= col_id, grid, 0.0))
    ends_l = [
        jnp.dot(jnp.broadcast_to(end, (8, heads)), spread_f, precision=HIGHEST, preferred_element_type=F32)
        for end in ends
    ]
    dec_out[...] = ends_l[0] + ends_l[1]
    skip_l[...] = jnp.dot(
        jnp.broadcast_to(own_heads(skip_ref[...].reshape(1, 2 * heads)), (8, heads)), spread_f,
        precision=HIGHEST, preferred_element_type=F32,
    )

    def decay_copy(j):
        return remote(dec_out, decs.at[j], dsend.at[j], drecv.at[j], device(dz=j))

    def state_copy(j):
        return remote(state_out, states.at[j], ssend.at[j], srecv.at[j], device(dz=j))

    for j in range(1, Z):

        @pl.when(z + j < Z)
        def _(j=j):
            decay_copy(j).start()

    def weigh(q):
        for i in range(heads):
            gap = jnp.minimum(running[q][:, i : i + 1] - running_t[q][i : i + 1, :], 0.0)
            wmat[q * heads + i] = (jnp.exp(gap) * scores[q]).astype(BF16)

    advance(2)
    out_advance(1)
    weigh(0)
    advance(3)
    out_advance(2)
    weigh(1)

    experts = wr_ref.shape[0]
    line = lax.broadcasted_iota(jnp.int32, (experts, rows), 0)
    hits = [line == ids_ref[k : k + 1, :] for k in range(2)]
    taken = (hits[0] | hits[1]).astype(F32).astype(BF16)
    before = jnp.dot(taken, (row_id < col_id).astype(F32).astype(BF16), preferred_element_type=F32)
    for k in range(2):
        notes[2 * k : 2 * k + 1, :] = jnp.sum(jnp.where(hits[k], line.astype(F32), 0.0), axis=0, keepdims=True)
        notes[2 * k + 1 : 2 * k + 2, :] = jnp.sum(jnp.where(hits[k], before, 0.0), axis=0, keepdims=True)
    notes[6:, :] = jnp.zeros((META - 6, rows), F32)

    advance(last)
    for k in range(1, last + 1):
        for h, side in units(k):
            off = landed(k, side)
            in_whole(nsend.at[off, h], nrecv.at[off, h]).wait_recv()

    out_advance(3)

    @pl.when(z > 0)
    def _():
        halo().wait_recv()

    tile = 256

    def project(i, carry):
        cols = pl.ds(pl.multiple_of(i * tile, tile), tile)
        ext[:, cols] = jnp.dot(normed[...], wi[:, cols], preferred_element_type=F32).astype(BF16).astype(F32)
        return carry

    lax.fori_loop(0, inner_w // tile, project, 0)
    for copy in fetches[8:12]:
        copy.wait()
    taps = cw_ref.shape[0]

    def convolve(i, carry):
        cols = pl.ds(pl.multiple_of(i * 128, 128), 128)
        params = lanes(c * inner_w + i * 128, 128)
        for q in range(2):
            acc = cb_ref[params].reshape(1, 128) + jnp.zeros((rows, 128), F32)
            for k in range(taps):
                acc = acc + cw_ref[k : k + 1, params] * ext[pl.ds(HALO - taps + 1 + k + q * rows, rows), cols]
            sig[pl.ds(q * rows, rows), cols] = acc * jax.nn.sigmoid(acc)
        return carry

    lax.fori_loop(0, inner_w // 128, convolve, 0)
    own_state = []
    for q in range(2):
        span = pl.ds(q * rows, rows)
        own_state.append(
            lax.dot_general(
                bmat[span, :].astype(BF16), (sig[span, :] * tail_l[span, :]).astype(BF16), (((0,), (0,)), ((), ())),
                preferred_element_type=F32,
            )
        )
    state_out[...] = (jnp.exp(ends_l[1][0:1]) * own_state[0] + own_state[1]).astype(BF16)
    for j in range(1, Z):

        @pl.when(z + j < Z)
        def _(j=j):
            state_copy(j).start()

        @pl.when(z < j)
        def _(j=j):
            states[j] = jnp.zeros_like(state_out)
            decs[j] = jnp.zeros_like(dec_out)

    out_advance(last)

    def project_gate(i, carry):
        cols = pl.ds(pl.multiple_of(i * tile, tile), tile)
        weight = wi[:, pl.ds(pl.multiple_of(inner_w + i * tile, tile), tile)]
        gz[:, cols] = jnp.dot(normed[HALO:, :], weight, preferred_element_type=F32)
        return carry

    lax.fori_loop(0, inner_w // tile, project_gate, 0)
    left_lane = lax.broadcasted_iota(jnp.int32, (rows, 128), 1) < head_size

    def within(p, carry):
        cols = pl.ds(pl.multiple_of(p * 128, 128), 128)
        skips = skip_l[0:1, cols]
        for q in range(2):
            span = pl.ds(q * rows, rows)
            fresh = (sig[span, cols] * step_l[span, cols]).astype(BF16)
            a = jnp.dot(wmat[q * heads + 2 * p], fresh, preferred_element_type=F32)
            b = jnp.dot(wmat[q * heads + 2 * p + 1], fresh, preferred_element_type=F32)
            yy[span, cols] = jnp.where(left_lane, a, b) + skips * sig[span, cols]
        return carry

    lax.fori_loop(0, inner_w // 128, within, 0)

    entry = jnp.zeros((n_state, inner_w), F32)
    lead = jnp.zeros((1, inner_w), F32)
    for j in range(1, Z):

        @pl.when(z >= j)
        def _(j=j):
            decay_copy(j).wait_recv()
            state_copy(j).wait_recv()

        entry = entry + jnp.exp(lead) * states[j].astype(F32)
        lead = lead + decs[j, 0:1]
    gain = gain_ref[lanes(c * inner_w, inner_w)].reshape(1, inner_w)
    squares = []
    for q in range(2):
        span = pl.ds(q * rows, rows)
        start = entry if q == 0 else jnp.exp(ends_l[0][0:1]) * entry + own_state[0]
        across = run_l[span, :] * jnp.dot(cmat[span, :].astype(BF16), start.astype(BF16), preferred_element_type=F32)
        gate = gz[span, :]
        gated = (yy[span, :] + across) * (gate * jax.nn.sigmoid(gate))
        squares.append(jnp.sum(gated * gated, axis=1, keepdims=True))
        gg[span, :] = (gated * gain).astype(BF16)

    for k in range(1, last + 1):
        for h, side in units(k):

            @pl.when(wanted(k, side))
            def _(k=k, h=h, side=side):
                out_share(k, h, side).wait_recv()

    theirs = pl.ds(pl.multiple_of((1 - c) * rows, 16), rows)
    ours = pl.ds(pl.multiple_of(c * rows, 16), rows)

    def leave(i, carry):
        cols = pl.ds(pl.multiple_of(i * tile, tile), tile)
        half_out[:, cols] = jnp.dot(gg[theirs, :], wo[:, cols], preferred_element_type=F32).astype(BF16)
        return carry

    lax.fori_loop(0, width // tile, leave, 0)
    wide = lax.broadcasted_iota(jnp.int32, (rows, 128), 1)
    their_square = jnp.where(c == 0, squares[1], squares[0])
    our_square = jnp.where(c == 0, squares[0], squares[1])
    high = their_square.astype(BF16).astype(F32)
    half_out[:, width:] = jnp.where(wide < 64, high, their_square - high).astype(BF16)

    def halves():
        return remote(half_out, half_in, misc_send.at[3], misc_recv.at[3], sibling)

    halves().start()

    def stay(i, carry):
        cols = pl.ds(pl.multiple_of(i * tile, tile), tile)
        yy[0:rows, cols] = jnp.dot(gg[ours, :], wo[:, cols], preferred_element_type=F32)
        return carry

    lax.fori_loop(0, width // tile, stay, 0)
    halves().wait_recv()
    extra = half_in[:, width:].astype(F32)
    total = our_square + extra[:, 0:1] + extra[:, 64:65]
    norm = lax.rsqrt(total / (2 * inner_w) + EPSILON)
    mixed = (
        tok_ref[...].astype(F32) + norm * (yy[0:rows, 0:width] + half_in[:, 0:width].astype(F32))
    ).astype(BF16)
    mixed_ref[...] = mixed
    mixed_f = mixed.astype(F32)
    routed = (mixed_f * lax.rsqrt(jnp.mean(mixed_f * mixed_f, axis=-1, keepdims=True) + EPSILON)).astype(BF16)
    gath[0] = routed
    logits = lax.dot_general(wr_ref[...], routed, (((1,), (1,)), ((), ())), preferred_element_type=F32)
    picked = [jnp.sum(jnp.where(hit, logits, 0.0), axis=0, keepdims=True) for hit in hits]
    first = jax.nn.sigmoid(picked[0] - picked[1])
    notes[4:5, :] = first
    notes[5:6, :] = 1.0 - first
    memo[0] = notes[...].astype(BF16)

    for copy in fetches[12:]:
        copy.wait()
    half = rows // 2
    slots = X * CAP
    up, down = device(dy=1), device(dy=Y - 1)
    bands = (pl.ds(0, half), pl.ds(half, half))

    def right(k, h):
        return remote(
            gath.at[k - 1, bands[h]], gath.at[k, bands[h]], ysend.at[0, k - 1, h], yrecv.at[k, h], up
        )

    def left(k, h):
        return remote(
            gath.at[(Y - k + 1) % Y, bands[h]], gath.at[Y - k, bands[h]], ysend.at[1, k - 1, h], yrecv.at[Y - k, h], down
        )

    def notes_right(k):
        return remote(memo.at[k - 1], memo.at[k], asend.at[0, k - 1], arecv.at[k], up)

    def notes_left(k):
        return remote(memo.at[(Y - k + 1) % Y], memo.at[Y - k], asend.at[1, k - 1], arecv.at[Y - k], down)

    def seat_of(d):
        return 0 if d == 0 else 1 if d == last else 2 * d if d < last else 2 * (Y - d) + 1

    def places(d):
        meta = memo[d].astype(F32)
        at = []
        for k in range(2):
            off = meta[2 * k : 2 * k + 1, :] - (y * X).astype(F32)
            turn = off - x.astype(F32)
            turn = jnp.where(turn < 0.0, turn + X, turn)
            inside = (off >= 0.0) & (off < float(X))
            at.append(jnp.where(inside, turn * CAP + meta[2 * k + 1 : 2 * k + 2, :], -1.0))
        order = lax.broadcasted_iota(jnp.int32, (slots, 1), 0).astype(F32)
        return meta, order == at[0], order == at[1]

    def slab(n, k=0, size=slots):
        return pl.ds(n * slots + k * CAP, size)

    def sideways(n, k):
        return remote(sbuf.at[slab(n, k, CAP)], arr.at[slab(n, k, CAP)], xsend.at[n], xrecv.at[n], device(dx=k))

    def homeward(n, k):
        return remote(ans.at[slab(n, k, CAP)], ret.at[slab(n, k, CAP)], rsend.at[n], rrecv.at[n], device(dx=X - k))

    def all_sideways(n):
        span = slab(n, 1, slots - CAP)
        return remote(sbuf.at[span], arr.at[span], xsend.at[n], xrecv.at[n], up)

    def all_homeward(n):
        span = slab(n, 1, slots - CAP)
        return remote(ans.at[span], ret.at[span], rsend.at[n], rrecv.at[n], up)

    def dispatch(d):
        n = seat_of(d)
        meta, hit0, hit1 = places(d)
        pick = jnp.where(hit0 | hit1, 1.0, 0.0).astype(BF16)
        sbuf[slab(n), :] = jnp.dot(pick, gath[d], preferred_element_type=F32).astype(BF16)
        for k in (2, 1, 3):
            sideways(n, k).start()
        arr[slab(n, 0, CAP), :] = sbuf[slab(n, 0, CAP), :]

    def expert(first_seat, count, answer=True):
        for n in range(first_seat, first_seat + count):
            all_sideways(n).wait_recv()
        span = pl.ds(first_seat * slots, count * slots)
        inside = pl.ds(0, count * slots)

        def enter(i, carry):
            cols = pl.ds(pl.multiple_of(i * tile, tile), tile)
            gate = jnp.dot(arr[span, :], wg_ref[0, :, cols], preferred_element_type=F32)
            lift = jnp.dot(arr[span, :], wu_ref[0, :, cols], preferred_element_type=F32)
            hid[inside, cols] = (gate * jax.nn.sigmoid(gate) * lift).astype(BF16)
            return carry

        def close(i, carry):
            cols = pl.ds(pl.multiple_of(i * tile, tile), tile)
            ans[span, cols] = jnp.dot(hid[inside, :], wd_ref[0, :, cols], preferred_element_type=F32).astype(BF16)
            return carry

        lax.fori_loop(0, wg_ref.shape[2] // tile, enter, 0)
        lax.fori_loop(0, width // tile, close, 0)
        if answer:
            reply(first_seat, count)

    def reply(first_seat, count):
        for n in range(first_seat, first_seat + count):
            for k in (2, 1, 3):
                homeward(n, k).start()
            ret[slab(n, 0, CAP), :] = ans[slab(n, 0, CAP), :]

    def combine(d):
        n = seat_of(d)
        all_homeward(n).wait_recv()
        meta, hit0, hit1 = places(d)
        share_of = jnp.where(hit0, meta[4:5, :], 0.0) + jnp.where(hit1, meta[5:6, :], 0.0)
        part_of[d] = lax.dot_general(
            share_of.astype(BF16), ret[slab(n), :], (((0,), (0,)), ((), ())), preferred_element_type=F32
        )

    def ring(k, h):
        if sent(k, h, 0):
            right(k, h).wait_recv()
            if k < last and sent(k + 1, h, 0):
                right(k + 1, h).start()
        if sent(k, h, 1):
            left(k, h).wait_recv()
            if k < last and sent(k + 1, h, 1):
                left(k + 1, h).start()
        if h == 0:
            notes_right(k).wait_recv()
            if k < last:
                notes_left(k).wait_recv()
                notes_right(k + 1).start()
            if k < last - 1:
                notes_left(k + 1).start()

    for h in range(2):
        right(1, h).start()
        left(1, h).start()
        if h == 0:
            notes_right(1).start()
            notes_left(1).start()
    dispatch(0)
    ring(1, 0)
    ring(1, 1)
    dispatch(1)
    dispatch(Y - 1)
    ring(2, 0)
    ring(2, 1)
    dispatch(2)
    dispatch(Y - 2)
    expert(seat_of(0), 1)
    ring(3, 0)
    ring(3, 1)
    dispatch(3)
    dispatch(Y - 3)
    expert(seat_of(1), 2, False)
    ring(last, 0)
    ring(last, 1)
    dispatch(last)
    expert(seat_of(2), 2, False)
    expert(seat_of(3), 2)
    expert(seat_of(last), 1)

    def target(d, side):
        return d - 1 if side == 0 else d + 1

    def go(d, h, side):
        land = target(d, side)
        return remote(
            rs_out.at[d, bands[h]], rs_in.at[land, bands[h]], psend.at[d, h], precv.at[land, h],
            down if side == 0 else up,
        )

    def push(k, h, side):
        d = k if side == 0 else Y - k
        total = part_of[d, bands[h]]
        if k < last - 1 or (k == last - 1 and h == side):
            before_d = d + 1 if side == 0 else d - 1
            go(before_d, h, side).wait_recv()
            total = total + rs_in[d, bands[h]].astype(F32)
        rs_out[d, bands[h]] = total.astype(BF16)
        go(d, h, side).start()

    combine(0)
    combine(3)
    push(3, 1, 0)
    combine(Y - 3)
    push(3, 0, 1)
    combine(last)
    push(last, 0, 0)
    push(last, 1, 1)
    reply(seat_of(2), 2)
    reply(seat_of(1), 2)
    push(3, 0, 0)
    push(3, 1, 1)
    combine(2)
    push(2, 1, 0)
    combine(Y - 2)
    push(2, 0, 1)
    combine(1)
    combine(Y - 1)
    push(2, 0, 0)
    push(2, 1, 1)
    push(1, 1, 0)
    push(1, 0, 1)
    push(1, 0, 0)
    push(1, 1, 1)
    for h in range(2):
        go(1, h, 0).wait_recv()
        go(Y - 1, h, 1).wait_recv()
        total = (
            mixed_ref[bands[h]].astype(F32) + part_of[0, bands[h]]
            + rs_in[0, bands[h]].astype(F32) + rs_in[Y, bands[h]].astype(F32)
        )
        out_ref[bands[h]] = total.astype(BF16)

    for copy in (other_in, rows_across(), halves()):
        copy.wait_send()

    @pl.when(z < Z - 1)
    def _():
        halo().wait_send()

    @pl.when(jnp.logical_not(home))
    def _():
        out_to_sibling().wait_send()

    for k in range(1, last + 1):
        for h, side in units(k):
            off = landed(k, side)
            in_whole(isend.at[side, k - 1, h], irecv.at[off, h]).wait_send()
            in_whole(nsend.at[off, h], nrecv.at[off, h]).wait_send()

            @pl.when(wanted(k - 1, side))
            def _(k=k, h=h, side=side):
                out_hop(k, h, side).wait_send()

            @pl.when(wanted(k, side))
            def _(k=k, h=h, side=side):
                out_share(k, h, side).wait_send()

    for j in range(1, Z):

        @pl.when(z + j < Z)
        def _(j=j):
            decay_copy(j).wait_send()
            state_copy(j).wait_send()
    for k in range(1, last + 1):
        notes_right(k).wait_send()
        if k < last:
            notes_left(k).wait_send()
        for h in range(2):
            if sent(k, h, 0):
                right(k, h).wait_send()
            if sent(k, h, 1):
                left(k, h).wait_send()
    for d in range(Y):
        for h in range(2):
            if d != 0:
                go(d, h, 0).wait_send()
        all_sideways(d).wait_send()
        all_homeward(d).wait_send()


def layer(tokens, w_in, w_small, dt_bias, decay_rate, conv_w, conv_b, skip, norm_gain, w_out, w_router, ids, *experts):
    rows, width = tokens.shape
    inner_w = conv_w.shape[1] // 2
    heads = dt_bias.shape[0] // 2
    n_state = (w_small.shape[0] - 2 * heads) // 2
    both = 2 * rows
    slots = X * CAP
    hidden = experts[0].shape[2]
    dma = pltpu.SemaphoreType.DMA
    wide = pltpu.VMEM((both, inner_w), F32)
    operands = (
        tokens, w_in, w_small, dt_bias, decay_rate, conv_w, conv_b, skip, norm_gain, w_out, w_router, ids, *experts
    )
    return pl.pallas_call(
        layer_kernel,
        out_shape=jax.ShapeDtypeStruct((rows, width), BF16),
        in_specs=[pl.BlockSpec(memory_space=pltpu.HBM)] * len(operands),
        out_specs=pl.BlockSpec(memory_space=pltpu.VMEM),
        scratch_shapes=[pltpu.VMEM(v.shape, v.dtype) for v in operands] + [
            pltpu.VMEM((rows, width), BF16),
            pltpu.VMEM((width, 2 * inner_w), BF16),
            pltpu.VMEM((inner_w, width), BF16),
            pltpu.VMEM((HALO + both, width), BF16),
            pltpu.VMEM((HALO + both, inner_w), F32),
            wide, wide, wide, wide, wide,
            pltpu.VMEM((2 * heads, rows, rows), BF16),
            pltpu.VMEM((both, n_state), F32),
            pltpu.VMEM((both, n_state), F32),
            wide,
            pltpu.VMEM((8, inner_w), F32),
            pltpu.VMEM((Z, 8, inner_w), F32),
            pltpu.VMEM((8, inner_w), F32),
            pltpu.VMEM((Z, n_state, inner_w), BF16),
            pltpu.VMEM((n_state, inner_w), BF16),
            pltpu.VMEM((both, inner_w), BF16),
            pltpu.VMEM((rows, width + 128), BF16),
            pltpu.VMEM((rows, width + 128), BF16),
            pltpu.VMEM((META, rows), F32),
            pltpu.VMEM((Y, rows, width), BF16),
            pltpu.VMEM((Y, META, rows), BF16),
            pltpu.VMEM((Y * slots, width), BF16),
            pltpu.VMEM((Y * slots, width), BF16),
            pltpu.VMEM((Y * slots, width), BF16),
            pltpu.VMEM((Y * slots, width), BF16),
            pltpu.VMEM((Y, rows, width), F32),
            pltpu.VMEM((Y, rows, width), BF16),
            pltpu.VMEM((Y + 1, rows, width), BF16),
            pltpu.VMEM((2 * slots, hidden), BF16),
            dma((len(operands),)),
            dma((2, Z // 2, 2)), dma((Z, 2)), dma((Z, 2)), dma((Z, 2)),
            dma((2, Z // 2, 2)), dma((Z, 2)), dma((Z, 2)), dma((Z, 2)),
            dma((Z,)), dma((Z,)), dma((Z,)), dma((Z,)),
            dma((5,)), dma((5,)),
            dma((2, Y // 2, 2)), dma((Y, 2)), dma((2, Y // 2)), dma((Y,)), dma((Y,)), dma((Y,)), dma((Y,)), dma((Y,)),
            dma((Y, 2)), dma((Y + 1, 2)),
        ],
        compiler_params=pltpu.CompilerParams(
            collective_id=1, has_side_effects=True, vmem_limit_bytes=60 * 1024 * 1024
        ),
        name="mixer_and_experts",
    )(*operands)


def local(
    tokens,
    w_in,
    w_small,
    dt_bias,
    decay_rate,
    conv_w,
    conv_b,
    skip,
    norm_gain,
    w_out,
    w_router,
    expert_ids,
    w_gate,
    w_up,
    w_down,
):
    return layer(
        tokens[0], w_in, w_small.T, dt_bias, decay_rate, conv_w, conv_b, skip, norm_gain, w_out, w_router.T,
        expert_ids[0].T, w_gate, w_up, w_down,
    )[None]


def solution(mesh):
    in_specs = (
        P("exp", "seq", None),
        P("seq", None),
        P(),
        P(),
        P(),
        P(),
        P(),
        P(),
        P(),
        P("seq", None),
        P(),
        P("exp", "seq", None),
        P("exp", None, None),
        P("exp", None, None),
        P("exp", None, None),
    )
    out_specs = P("exp", "seq", None)
    return jax.shard_map(local, mesh=mesh, in_specs=in_specs, out_specs=out_specs, check_vma=False)
```

```python
import jax
import jax.numpy as jnp
from jax import lax
from jax.experimental import pallas as pl
from jax.experimental.pallas import tpu as pltpu
from jax.sharding import PartitionSpec as P

Y, X = 8, 4
CAP = 48
META = 16
MESH = pl.DeviceIdType.MESH


def exp_peers():
    e = lax.axis_index("exp")
    return e // X, lax.rem(e, X)


Z = 8
HALO = 16
EPSILON = 1e-05
HIGHEST = lax.Precision.HIGHEST
F32 = jnp.float32
BF16 = jnp.bfloat16


def layer_kernel(
    tok_hbm, win_hbm, wsmall_hbm, dtb_hbm, rate_hbm, cw_hbm, cb_hbm, skip_hbm, gain_hbm, wout_hbm, wr_hbm, ids_hbm,
    wg_hbm, wu_hbm, wd_hbm, out_ref,
    tok_ref, win_ref, wsmall_ref, dtb_ref, rate_ref, cw_ref, cb_ref, skip_ref, gain_ref, wout_ref, wr_ref, ids_ref,
    wg_ref, wu_ref, wd_ref, mixed_ref,
    wi, wo, normed, ext, sig, gz, step_l, tail_l, run_l, wmat, bmat, cmat, yy, skip_l, decs, dec_out, states, state_out,
    gg, half_out, half_in, notes,
    gath, memo, sbuf, arr, ans, ret, part_of, rs_out, rs_in, hid,
    fetch_sem,
    isend, irecv, nsend, nrecv, osend, orecv, mosend, morecv, dsend, drecv, ssend, srecv, misc_send, misc_recv,
    ysend, yrecv, asend, arecv, xsend, xrecv, rsend, rrecv, psend, precv,
):
    rows, width = tok_ref.shape
    both = 2 * rows
    inner_w = wi.shape[1] // 2
    heads = skip_ref.shape[0] // 2
    head_size = inner_w // heads
    n_state = (wsmall_ref.shape[0] - 2 * heads) // 2
    in_rows = win_ref.shape[0]
    out_rows = wout_ref.shape[0]
    part = inner_w // 2
    seat = lax.axis_index("seq")
    z, c = seat // 2, lax.rem(seat, 2)
    y, x = exp_peers()
    pair = lax.rem(y, 2), lax.rem(x, 2)

    def device(dz=0, core=None, dy=0, dx=0):
        return {
            "seq": lax.rem(z + dz, Z) * 2 + (c if core is None else core),
            "exp": lax.rem(y + dy, Y) * X + lax.rem(x + dx, X),
        }

    sibling = device(core=1 - c)

    def remote(src, dst, send, recv, to):
        return pltpu.make_async_remote_copy(
            src_ref=src, dst_ref=dst, send_sem=send, recv_sem=recv, device_id=to, device_id_type=MESH
        )

    pairs = (
        (win_hbm, win_ref), (tok_hbm, tok_ref), (wout_hbm, wout_ref), (wsmall_hbm, wsmall_ref), (dtb_hbm, dtb_ref),
        (rate_hbm, rate_ref), (skip_hbm, skip_ref), (ids_hbm, ids_ref), (cw_hbm, cw_ref), (cb_hbm, cb_ref),
        (gain_hbm, gain_ref), (wr_hbm, wr_ref), (wg_hbm, wg_ref), (wu_hbm, wu_ref), (wd_hbm, wd_ref),
    )
    fetches = [pltpu.make_async_copy(src, dst, fetch_sem.at[n]) for n, (src, dst) in enumerate(pairs)]
    for copy in fetches:
        copy.start()

    barrier = pltpu.get_barrier_semaphore()
    peers = [sibling, device(dy=1), device(dy=Y - 1), device(dx=1), device(dx=X - 1)]
    peers += [device(dx=2)] + [device(dz=j) for j in range(1, Z)]
    for to in peers:
        pl.semaphore_signal(barrier, inc=1, device_id=to, device_id_type=MESH)

    def lanes(start, size):
        return pl.ds(pl.multiple_of(start, 128), size)

    def in_band(zs, h):
        return pl.ds(pl.multiple_of((2 * zs + h) * in_rows, 16), in_rows)

    def out_band(zs, h):
        return pl.ds(pl.multiple_of(lax.rem(2 * zs + h, Z) * out_rows, 16), out_rows)

    first_in = lanes(pair[0] * part, part)
    second_in = lanes(inner_w + pair[1] * part, part)
    first_out = lanes(pair[1] * part, part)

    def origin(k, side):
        return lax.rem(z + Z - k, Z) if side == 0 else lax.rem(z + k, Z)

    def landed(k, side):
        return k if side == 0 else Z - k

    def hop(k, h, side):
        band = in_band(origin(k - 1, side), h)
        to = device(dz=1 if side == 0 else Z - 1)
        return [
            remote(wi.at[band, cols], wi.at[band, cols], isend.at[side, k - 1, h], irecv.at[landed(k, side), h], to)
            for cols in (first_in, second_in)
        ]

    def in_whole(send, recv):
        return remote(wi.at[0:in_rows, 0:inner_w], wi.at[0:in_rows, 0:inner_w], send, recv, sibling)

    def hop_arrived(k, h, side):
        in_whole(isend.at[side, k - 1, h], irecv.at[landed(k, side), h]).wait_recv()

    def share(k, h, side):
        band = in_band(origin(k, side), h)
        off = landed(k, side)
        for cols, to in (
            (first_in, device(dy=1 if h == 0 else Y - 1)),
            (second_in, device(dx=1 if h == 0 else X - 1)),
        ):
            remote(wi.at[band, cols], wi.at[band, cols], nsend.at[off, h], nrecv.at[off, h], to).start()

    def out_hop(k, h, side):
        band = out_band(origin(k - 1, side), h)
        to = device(dz=1 if side == 0 else Z - 1)
        return remote(
            wo.at[band, first_out], wo.at[band, first_out], osend.at[side, k - 1, h], orecv.at[landed(k, side), h], to
        )

    def out_share(k, h, side):
        band = out_band(origin(k, side), h)
        off = landed(k, side)
        return remote(
            wo.at[band, first_out], wo.at[band, first_out], mosend.at[off, h], morecv.at[off, h],
            device(dx=1 if h == 0 else X - 1),
        )

    last = Z // 2

    def sent(k, h, side):
        return k < last or (k == last and h == side)

    def wanted(k, side):
        return origin(k, side) // last == c

    def units(k):
        return [(h, side) for h in range(2) for side in range(2) if sent(k, h, side)]

    fetches[0].wait()
    wi[in_band(z, c), 0:inner_w] = win_ref[:, lanes(2 * inner_w + c * inner_w, inner_w)]
    wi[in_band(z, c), inner_w:] = win_ref[:, lanes(c * inner_w, inner_w)]

    def to_sibling():
        return [
            remote(
                win_ref.at[:, lanes(base + (1 - c) * inner_w, inner_w)],
                wi.at[in_band(z, c), pl.ds(at, inner_w)],
                misc_send.at[0], misc_recv.at[0], sibling,
            )
            for base, at in ((2 * inner_w, 0), (0, inner_w))
        ]

    def out_to_sibling():
        return remote(wout_ref, wo.at[out_band(z, c)], misc_send.at[4], misc_recv.at[4], sibling)

    fetches[1].wait()
    fetches[2].wait()
    home = z // last == c

    resid = tok_ref[...].astype(F32)
    scale = lax.rsqrt(jnp.mean(resid * resid, axis=-1, keepdims=True) + EPSILON)
    mine = pl.ds(pl.multiple_of(HALO + c * rows, 16), rows)
    normed[mine, :] = (resid * scale).astype(BF16)

    pl.semaphore_wait(barrier, len(peers))
    for copy in to_sibling():
        copy.start()
    for side in range(2):
        for copy in hop(1, c, side):
            copy.start()

    def rows_across():
        return remote(normed.at[mine], normed.at[mine], misc_send.at[1], misc_recv.at[1], sibling)

    rows_across().start()

    @pl.when(home)
    def _():
        wo[out_band(z, c), :] = wout_ref[...]

    @pl.when(jnp.logical_not(home))
    def _():
        out_to_sibling().start()

    other_in = remote(
        wi.at[0:in_rows], wi.at[0:in_rows], misc_send.at[0], misc_recv.at[0], sibling
    )
    other_in.wait_recv()
    for side in range(2):
        for copy in hop(1, 1 - c, side):
            copy.start()

    rows_across().wait_recv()

    def halo():
        return remote(
            normed.at[both : both + HALO], normed.at[0:HALO], misc_send.at[2], misc_recv.at[2], device(dz=1)
        )

    @pl.when(z < Z - 1)
    def _():
        halo().start()

    @pl.when(z == 0)
    def _():
        normed[0:HALO, :] = jnp.zeros((HALO, width), BF16)

    for copy in fetches[3:8]:
        copy.wait()
    small = lax.dot_general(
        normed[HALO:, :], wsmall_ref[...], (((1,), (1,)), ((), ())), preferred_element_type=F32
    )
    bmat[...] = small[:, 0:n_state]
    cmat[...] = small[:, n_state : 2 * n_state]
    raw = small[:, 2 * n_state :] + dtb_ref[...].reshape(1, 2 * heads)
    step_all = jnp.maximum(raw, 0.0) + jnp.log1p(jnp.exp(-jnp.abs(raw)))
    decay_all = -step_all * rate_ref[...].reshape(1, 2 * heads)

    def own_heads(v):
        return jnp.where(c == 0, v[:, 0:heads], v[:, heads : 2 * heads])

    step = own_heads(step_all)
    log_decay = own_heads(decay_all)
    def advance(k):
        for h, side in units(k):
            hop_arrived(k, h, side)
            if k < last and sent(k + 1, h, side):
                for copy in hop(k + 1, h, side):
                    copy.start()
        for h, side in units(k):
            share(k, h, side)

    @pl.when(home)
    def _():
        out_to_sibling().wait_recv()
        for h, side in units(1):
            out_hop(1, h, side).start()

    def out_advance(k):
        for h, side in units(k):

            @pl.when(wanted(k, side))
            def _(h=h, side=side):
                out_hop(k, h, side).wait_recv()
                if k < last and sent(k + 1, h, side):
                    out_hop(k + 1, h, side).start()
                out_share(k, h, side).start()

    advance(1)
    head_of = lax.broadcasted_iota(jnp.int32, (heads, inner_w), 1) // head_size
    spread = (head_of == lax.broadcasted_iota(jnp.int32, (heads, inner_w), 0)).astype(BF16)
    spread_f = spread.astype(F32)

    def expand(v):
        high = v.astype(BF16)
        low = (v - high.astype(F32)).astype(BF16)
        return jnp.dot(high, spread, preferred_element_type=F32) + jnp.dot(low, spread, preferred_element_type=F32)

    row_id = lax.broadcasted_iota(jnp.int32, (rows, rows), 0)
    col_id = lax.broadcasted_iota(jnp.int32, (rows, rows), 1)
    lower = (row_id >= col_id).astype(F32)
    upper = (row_id <= col_id).astype(F32)
    running, running_t, ends, scores = [], [], [], []
    for q in range(2):
        piece = log_decay[q * rows : (q + 1) * rows]
        run = jnp.dot(lower, piece, precision=HIGHEST, preferred_element_type=F32)
        running.append(run)
        running_t.append(
            lax.dot_general(piece, upper, (((0,), (0,)), ((), ())), precision=HIGHEST, preferred_element_type=F32)
        )
        end = run[rows - 1 : rows]
        ends.append(end)
        span = pl.ds(q * rows, rows)
        here = step[q * rows : (q + 1) * rows]
        step_l[span, :] = expand(here)
        tail_l[span, :] = expand(here * jnp.exp(end - run))
        run_l[span, :] = expand(jnp.exp(run))
        grid = lax.dot_general(
            cmat[span, :], bmat[span, :], (((1,), (1,)), ((), ())), precision=HIGHEST, preferred_element_type=F32
        )
        scores.append(jnp.where(row_id >= col_id, grid, 0.0))
    ends_l = [
        jnp.dot(jnp.broadcast_to(end, (8, heads)), spread_f, precision=HIGHEST, preferred_element_type=F32)
        for end in ends
    ]
    dec_out[...] = ends_l[0] + ends_l[1]
    skip_l[...] = jnp.dot(
        jnp.broadcast_to(own_heads(skip_ref[...].reshape(1, 2 * heads)), (8, heads)), spread_f,
        precision=HIGHEST, preferred_element_type=F32,
    )

    def decay_copy(j):
        return remote(dec_out, decs.at[j], dsend.at[j], drecv.at[j], device(dz=j))

    def state_copy(j):
        return remote(state_out, states.at[j], ssend.at[j], srecv.at[j], device(dz=j))

    for j in range(1, Z):

        @pl.when(z + j < Z)
        def _(j=j):
            decay_copy(j).start()

    def weigh(q):
        for i in range(heads):
            gap = jnp.minimum(running[q][:, i : i + 1] - running_t[q][i : i + 1, :], 0.0)
            wmat[q * heads + i] = (jnp.exp(gap) * scores[q]).astype(BF16)

    advance(2)
    out_advance(1)
    weigh(0)
    advance(3)
    out_advance(2)
    weigh(1)

    experts = wr_ref.shape[0]
    line = lax.broadcasted_iota(jnp.int32, (experts, rows), 0)
    hits = [line == ids_ref[k : k + 1, :] for k in range(2)]
    taken = (hits[0] | hits[1]).astype(F32).astype(BF16)
    before = jnp.dot(taken, (row_id < col_id).astype(F32).astype(BF16), preferred_element_type=F32)
    for k in range(2):
        notes[2 * k : 2 * k + 1, :] = jnp.sum(jnp.where(hits[k], line.astype(F32), 0.0), axis=0, keepdims=True)
        notes[2 * k + 1 : 2 * k + 2, :] = jnp.sum(jnp.where(hits[k], before, 0.0), axis=0, keepdims=True)
    notes[6:, :] = jnp.zeros((META - 6, rows), F32)

    advance(last)
    for k in range(1, last + 1):
        for h, side in units(k):
            off = landed(k, side)
            in_whole(nsend.at[off, h], nrecv.at[off, h]).wait_recv()

    out_advance(3)

    @pl.when(z > 0)
    def _():
        halo().wait_recv()

    tile = 256

    def project(i, carry):
        cols = pl.ds(pl.multiple_of(i * tile, tile), tile)
        ext[:, cols] = jnp.dot(normed[...], wi[:, cols], preferred_element_type=F32).astype(BF16).astype(F32)
        return carry

    lax.fori_loop(0, inner_w // tile, project, 0)
    for copy in fetches[8:12]:
        copy.wait()
    taps = cw_ref.shape[0]

    def convolve(i, carry):
        cols = pl.ds(pl.multiple_of(i * 128, 128), 128)
        params = lanes(c * inner_w + i * 128, 128)
        for q in range(2):
            acc = cb_ref[params].reshape(1, 128) + jnp.zeros((rows, 128), F32)
            for k in range(taps):
                acc = acc + cw_ref[k : k + 1, params] * ext[pl.ds(HALO - taps + 1 + k + q * rows, rows), cols]
            sig[pl.ds(q * rows, rows), cols] = acc * jax.nn.sigmoid(acc)
        return carry

    lax.fori_loop(0, inner_w // 128, convolve, 0)
    own_state = []
    for q in range(2):
        span = pl.ds(q * rows, rows)
        own_state.append(
            lax.dot_general(
                bmat[span, :].astype(BF16), (sig[span, :] * tail_l[span, :]).astype(BF16), (((0,), (0,)), ((), ())),
                preferred_element_type=F32,
            )
        )
    state_out[...] = (jnp.exp(ends_l[1][0:1]) * own_state[0] + own_state[1]).astype(BF16)
    for j in range(1, Z):

        @pl.when(z + j < Z)
        def _(j=j):
            state_copy(j).start()

        @pl.when(z < j)
        def _(j=j):
            states[j] = jnp.zeros_like(state_out)
            decs[j] = jnp.zeros_like(dec_out)

    out_advance(last)

    def project_gate(i, carry):
        cols = pl.ds(pl.multiple_of(i * tile, tile), tile)
        weight = wi[:, pl.ds(pl.multiple_of(inner_w + i * tile, tile), tile)]
        gz[:, cols] = jnp.dot(normed[HALO:, :], weight, preferred_element_type=F32)
        return carry

    lax.fori_loop(0, inner_w // tile, project_gate, 0)
    left_lane = lax.broadcasted_iota(jnp.int32, (rows, 128), 1) < head_size

    def within(p, carry):
        cols = pl.ds(pl.multiple_of(p * 128, 128), 128)
        skips = skip_l[0:1, cols]
        for q in range(2):
            span = pl.ds(q * rows, rows)
            fresh = (sig[span, cols] * step_l[span, cols]).astype(BF16)
            a = jnp.dot(wmat[q * heads + 2 * p], fresh, preferred_element_type=F32)
            b = jnp.dot(wmat[q * heads + 2 * p + 1], fresh, preferred_element_type=F32)
            yy[span, cols] = jnp.where(left_lane, a, b) + skips * sig[span, cols]
        return carry

    lax.fori_loop(0, inner_w // 128, within, 0)

    entry = jnp.zeros((n_state, inner_w), F32)
    lead = jnp.zeros((1, inner_w), F32)
    for j in range(1, Z):

        @pl.when(z >= j)
        def _(j=j):
            decay_copy(j).wait_recv()
            state_copy(j).wait_recv()

        entry = entry + jnp.exp(lead) * states[j].astype(F32)
        lead = lead + decs[j, 0:1]
    gain = gain_ref[lanes(c * inner_w, inner_w)].reshape(1, inner_w)
    squares = []
    for q in range(2):
        span = pl.ds(q * rows, rows)
        start = entry if q == 0 else jnp.exp(ends_l[0][0:1]) * entry + own_state[0]
        across = run_l[span, :] * jnp.dot(cmat[span, :].astype(BF16), start.astype(BF16), preferred_element_type=F32)
        gate = gz[span, :]
        gated = (yy[span, :] + across) * (gate * jax.nn.sigmoid(gate))
        squares.append(jnp.sum(gated * gated, axis=1, keepdims=True))
        gg[span, :] = (gated * gain).astype(BF16)

    for k in range(1, last + 1):
        for h, side in units(k):

            @pl.when(wanted(k, side))
            def _(k=k, h=h, side=side):
                out_share(k, h, side).wait_recv()

    theirs = pl.ds(pl.multiple_of((1 - c) * rows, 16), rows)
    ours = pl.ds(pl.multiple_of(c * rows, 16), rows)

    def leave(i, carry):
        cols = pl.ds(pl.multiple_of(i * tile, tile), tile)
        half_out[:, cols] = jnp.dot(gg[theirs, :], wo[:, cols], preferred_element_type=F32).astype(BF16)
        return carry

    lax.fori_loop(0, width // tile, leave, 0)
    wide = lax.broadcasted_iota(jnp.int32, (rows, 128), 1)
    their_square = jnp.where(c == 0, squares[1], squares[0])
    our_square = jnp.where(c == 0, squares[0], squares[1])
    high = their_square.astype(BF16).astype(F32)
    half_out[:, width:] = jnp.where(wide < 64, high, their_square - high).astype(BF16)

    def halves():
        return remote(half_out, half_in, misc_send.at[3], misc_recv.at[3], sibling)

    halves().start()

    def stay(i, carry):
        cols = pl.ds(pl.multiple_of(i * tile, tile), tile)
        yy[0:rows, cols] = jnp.dot(gg[ours, :], wo[:, cols], preferred_element_type=F32)
        return carry

    lax.fori_loop(0, width // tile, stay, 0)
    halves().wait_recv()
    extra = half_in[:, width:].astype(F32)
    total = our_square + extra[:, 0:1] + extra[:, 64:65]
    norm = lax.rsqrt(total / (2 * inner_w) + EPSILON)
    mixed = (
        tok_ref[...].astype(F32) + norm * (yy[0:rows, 0:width] + half_in[:, 0:width].astype(F32))
    ).astype(BF16)
    mixed_ref[...] = mixed
    mixed_f = mixed.astype(F32)
    routed = (mixed_f * lax.rsqrt(jnp.mean(mixed_f * mixed_f, axis=-1, keepdims=True) + EPSILON)).astype(BF16)
    half = rows // 2
    broad = 384
    slots = X * CAP
    up, down = device(dy=1), device(dy=Y - 1)
    bands = (pl.ds(0, half), pl.ds(half, half))

    def right(k, h):
        return remote(
            gath.at[k - 1, bands[h]], gath.at[k, bands[h]], ysend.at[0, k - 1, h], yrecv.at[k, h], up
        )

    def left(k, h):
        return remote(
            gath.at[(Y - k + 1) % Y, bands[h]], gath.at[Y - k, bands[h]], ysend.at[1, k - 1, h], yrecv.at[Y - k, h], down
        )

    gath[0] = routed
    for h in range(2):
        right(1, h).start()
        left(1, h).start()
    logits = lax.dot_general(wr_ref[...], routed, (((1,), (1,)), ((), ())), preferred_element_type=F32)
    picked = [jnp.sum(jnp.where(hit, logits, 0.0), axis=0, keepdims=True) for hit in hits]
    first = jax.nn.sigmoid(picked[0] - picked[1])
    notes[4:5, :] = first
    notes[5:6, :] = 1.0 - first
    memo[0] = notes[...].astype(BF16)

    def notes_right(k):
        return remote(memo.at[k - 1], memo.at[k], asend.at[0, k - 1], arecv.at[k], up)

    def notes_left(k):
        return remote(memo.at[(Y - k + 1) % Y], memo.at[Y - k], asend.at[1, k - 1], arecv.at[Y - k], down)

    def seat_of(d):
        return 0 if d == 0 else 1 if d == last else 2 * d if d < last else 2 * (Y - d) + 1

    def places(d):
        meta = memo[d].astype(F32)
        at = []
        for k in range(2):
            off = meta[2 * k : 2 * k + 1, :] - (y * X).astype(F32)
            turn = off - x.astype(F32)
            turn = jnp.where(turn < 0.0, turn + X, turn)
            inside = (off >= 0.0) & (off < float(X))
            at.append(jnp.where(inside, turn * CAP + meta[2 * k + 1 : 2 * k + 2, :], -1.0))
        order = lax.broadcasted_iota(jnp.int32, (slots, 1), 0).astype(F32)
        return meta, order == at[0], order == at[1]

    def slab(n, k=0, size=slots):
        return pl.ds(n * slots + k * CAP, size)

    def sideways(n, k):
        return remote(sbuf.at[slab(n, k, CAP)], arr.at[slab(n, k, CAP)], xsend.at[n], xrecv.at[n], device(dx=k))

    def homeward(n, k):
        return remote(ans.at[slab(n, k, CAP)], ret.at[slab(n, k, CAP)], rsend.at[n], rrecv.at[n], device(dx=X - k))

    def all_sideways(n):
        span = slab(n, 1, slots - CAP)
        return remote(sbuf.at[span], arr.at[span], xsend.at[n], xrecv.at[n], up)

    def all_homeward(n):
        span = slab(n, 1, slots - CAP)
        return remote(ans.at[span], ret.at[span], rsend.at[n], rrecv.at[n], up)

    def dispatch(d):
        n = seat_of(d)
        meta, hit0, hit1 = places(d)
        pick = jnp.where(hit0 | hit1, 1.0, 0.0).astype(BF16)
        sbuf[slab(n), :] = jnp.dot(pick, gath[d], preferred_element_type=F32).astype(BF16)
        for k in (2, 1, 3):
            sideways(n, k).start()
        arr[slab(n, 0, CAP), :] = sbuf[slab(n, 0, CAP), :]

    def expert(first_seat, count, answer=True):
        for n in range(first_seat, first_seat + count):
            all_sideways(n).wait_recv()
        span = pl.ds(first_seat * slots, count * slots)
        inside = pl.ds(0, count * slots)

        def enter(i, carry):
            cols = pl.ds(pl.multiple_of(i * broad, broad), broad)
            gate = jnp.dot(arr[span, :], wg_ref[0, :, cols], preferred_element_type=F32)
            lift = jnp.dot(arr[span, :], wu_ref[0, :, cols], preferred_element_type=F32)
            hid[inside, cols] = (gate * jax.nn.sigmoid(gate) * lift).astype(BF16)
            return carry

        def close(i, carry):
            cols = pl.ds(pl.multiple_of(i * broad, broad), broad)
            ans[span, cols] = jnp.dot(hid[inside, :], wd_ref[0, :, cols], preferred_element_type=F32).astype(BF16)
            return carry

        lax.fori_loop(0, wg_ref.shape[2] // broad, enter, 0)
        lax.fori_loop(0, width // broad, close, 0)
        if answer:
            reply(first_seat, count)

    def reply(first_seat, count):
        for n in range(first_seat, first_seat + count):
            for k in (2, 1, 3):
                homeward(n, k).start()
            ret[slab(n, 0, CAP), :] = ans[slab(n, 0, CAP), :]

    def combine(d):
        n = seat_of(d)
        all_homeward(n).wait_recv()
        meta, hit0, hit1 = places(d)
        share_of = jnp.where(hit0, meta[4:5, :], 0.0) + jnp.where(hit1, meta[5:6, :], 0.0)
        part_of[d] = lax.dot_general(
            share_of.astype(BF16), ret[slab(n), :], (((0,), (0,)), ((), ())), preferred_element_type=F32
        )

    def ring(k, h):
        if sent(k, h, 0):
            right(k, h).wait_recv()
            if k < last and sent(k + 1, h, 0):
                right(k + 1, h).start()
        if sent(k, h, 1):
            left(k, h).wait_recv()
            if k < last and sent(k + 1, h, 1):
                left(k + 1, h).start()
        if h == 0:
            notes_right(k).wait_recv()
            if k < last:
                notes_left(k).wait_recv()
                notes_right(k + 1).start()
            if k < last - 1:
                notes_left(k + 1).start()

    notes_right(1).start()
    notes_left(1).start()
    for copy in fetches[12:]:
        copy.wait()
    dispatch(0)
    ring(1, 0)
    ring(1, 1)
    dispatch(1)
    dispatch(Y - 1)
    ring(2, 0)
    ring(2, 1)
    dispatch(2)
    dispatch(Y - 2)
    expert(seat_of(0), 1, False)
    ring(3, 0)
    ring(3, 1)
    dispatch(3)
    dispatch(Y - 3)
    expert(seat_of(1), 2, False)
    ring(last, 0)
    ring(last, 1)
    dispatch(last)
    expert(seat_of(2), 2, False)
    expert(seat_of(3), 2)
    expert(seat_of(last), 1)

    def target(d, side):
        return d - 1 if side == 0 else d + 1

    def go(d, h, side):
        land = target(d, side)
        return remote(
            rs_out.at[d, bands[h]], rs_in.at[land, bands[h]], psend.at[d, h], precv.at[land, h],
            down if side == 0 else up,
        )

    def push(k, h, side):
        d = k if side == 0 else Y - k
        total = part_of[d, bands[h]]
        if k < last - 1 or (k == last - 1 and h == side):
            before_d = d + 1 if side == 0 else d - 1
            go(before_d, h, side).wait_recv()
            total = total + rs_in[d, bands[h]].astype(F32)
        rs_out[d, bands[h]] = total.astype(BF16)
        go(d, h, side).start()

    combine(3)
    push(3, 1, 0)
    combine(Y - 3)
    push(3, 0, 1)
    combine(last)
    push(last, 0, 0)
    push(last, 1, 1)
    reply(seat_of(2), 2)
    reply(seat_of(1), 2)
    reply(seat_of(0), 1)
    push(3, 0, 0)
    push(3, 1, 1)
    combine(2)
    push(2, 1, 0)
    combine(Y - 2)
    push(2, 0, 1)
    combine(1)
    combine(Y - 1)
    push(2, 0, 0)
    push(2, 1, 1)
    push(1, 1, 0)
    push(1, 0, 1)
    push(1, 0, 0)
    push(1, 1, 1)
    combine(0)
    for h in range(2):
        go(1, h, 0).wait_recv()
        go(Y - 1, h, 1).wait_recv()
        total = (
            mixed_ref[bands[h]].astype(F32) + part_of[0, bands[h]]
            + rs_in[0, bands[h]].astype(F32) + rs_in[Y, bands[h]].astype(F32)
        )
        out_ref[bands[h]] = total.astype(BF16)

    for copy in (other_in, rows_across(), halves()):
        copy.wait_send()

    @pl.when(z < Z - 1)
    def _():
        halo().wait_send()

    @pl.when(jnp.logical_not(home))
    def _():
        out_to_sibling().wait_send()

    for k in range(1, last + 1):
        for h, side in units(k):
            off = landed(k, side)
            in_whole(isend.at[side, k - 1, h], irecv.at[off, h]).wait_send()
            in_whole(nsend.at[off, h], nrecv.at[off, h]).wait_send()

            @pl.when(wanted(k - 1, side))
            def _(k=k, h=h, side=side):
                out_hop(k, h, side).wait_send()

            @pl.when(wanted(k, side))
            def _(k=k, h=h, side=side):
                out_share(k, h, side).wait_send()

    for j in range(1, Z):

        @pl.when(z + j < Z)
        def _(j=j):
            decay_copy(j).wait_send()
            state_copy(j).wait_send()
    for k in range(1, last + 1):
        notes_right(k).wait_send()
        if k < last:
            notes_left(k).wait_send()
        for h in range(2):
            if sent(k, h, 0):
                right(k, h).wait_send()
            if sent(k, h, 1):
                left(k, h).wait_send()
    for d in range(Y):
        for h in range(2):
            if d != 0:
                go(d, h, 0).wait_send()
        all_sideways(d).wait_send()
        all_homeward(d).wait_send()


def layer(tokens, w_in, w_small, dt_bias, decay_rate, conv_w, conv_b, skip, norm_gain, w_out, w_router, ids, *experts):
    rows, width = tokens.shape
    inner_w = conv_w.shape[1] // 2
    heads = dt_bias.shape[0] // 2
    n_state = (w_small.shape[0] - 2 * heads) // 2
    both = 2 * rows
    slots = X * CAP
    hidden = experts[0].shape[2]
    dma = pltpu.SemaphoreType.DMA
    wide = pltpu.VMEM((both, inner_w), F32)
    operands = (
        tokens, w_in, w_small, dt_bias, decay_rate, conv_w, conv_b, skip, norm_gain, w_out, w_router, ids, *experts
    )
    return pl.pallas_call(
        layer_kernel,
        out_shape=jax.ShapeDtypeStruct((rows, width), BF16),
        in_specs=[pl.BlockSpec(memory_space=pltpu.HBM)] * len(operands),
        out_specs=pl.BlockSpec(memory_space=pltpu.VMEM),
        scratch_shapes=[pltpu.VMEM(v.shape, v.dtype) for v in operands] + [
            pltpu.VMEM((rows, width), BF16),
            pltpu.VMEM((width, 2 * inner_w), BF16),
            pltpu.VMEM((inner_w, width), BF16),
            pltpu.VMEM((HALO + both, width), BF16),
            pltpu.VMEM((HALO + both, inner_w), F32),
            wide, wide, wide, wide, wide,
            pltpu.VMEM((2 * heads, rows, rows), BF16),
            pltpu.VMEM((both, n_state), F32),
            pltpu.VMEM((both, n_state), F32),
            wide,
            pltpu.VMEM((8, inner_w), F32),
            pltpu.VMEM((Z, 8, inner_w), F32),
            pltpu.VMEM((8, inner_w), F32),
            pltpu.VMEM((Z, n_state, inner_w), BF16),
            pltpu.VMEM((n_state, inner_w), BF16),
            pltpu.VMEM((both, inner_w), BF16),
            pltpu.VMEM((rows, width + 128), BF16),
            pltpu.VMEM((rows, width + 128), BF16),
            pltpu.VMEM((META, rows), F32),
            pltpu.VMEM((Y, rows, width), BF16),
            pltpu.VMEM((Y, META, rows), BF16),
            pltpu.VMEM((Y * slots, width), BF16),
            pltpu.VMEM((Y * slots, width), BF16),
            pltpu.VMEM((Y * slots, width), BF16),
            pltpu.VMEM((Y * slots, width), BF16),
            pltpu.VMEM((Y, rows, width), F32),
            pltpu.VMEM((Y, rows, width), BF16),
            pltpu.VMEM((Y + 1, rows, width), BF16),
            pltpu.VMEM((2 * slots, hidden), BF16),
            dma((len(operands),)),
            dma((2, Z // 2, 2)), dma((Z, 2)), dma((Z, 2)), dma((Z, 2)),
            dma((2, Z // 2, 2)), dma((Z, 2)), dma((Z, 2)), dma((Z, 2)),
            dma((Z,)), dma((Z,)), dma((Z,)), dma((Z,)),
            dma((5,)), dma((5,)),
            dma((2, Y // 2, 2)), dma((Y, 2)), dma((2, Y // 2)), dma((Y,)), dma((Y,)), dma((Y,)), dma((Y,)), dma((Y,)),
            dma((Y, 2)), dma((Y + 1, 2)),
        ],
        compiler_params=pltpu.CompilerParams(
            collective_id=1, has_side_effects=True, vmem_limit_bytes=60 * 1024 * 1024
        ),
        name="mixer_and_experts",
    )(*operands)


def local(
    tokens,
    w_in,
    w_small,
    dt_bias,
    decay_rate,
    conv_w,
    conv_b,
    skip,
    norm_gain,
    w_out,
    w_router,
    expert_ids,
    w_gate,
    w_up,
    w_down,
):
    return layer(
        tokens[0], w_in, w_small.T, dt_bias, decay_rate, conv_w, conv_b, skip, norm_gain, w_out, w_router.T,
        expert_ids[0].T, w_gate, w_up, w_down,
    )[None]


def solution(mesh):
    in_specs = (
        P("exp", "seq", None),
        P("seq", None),
        P(),
        P(),
        P(),
        P(),
        P(),
        P(),
        P(),
        P("seq", None),
        P(),
        P("exp", "seq", None),
        P("exp", None, None),
        P("exp", None, None),
        P("exp", None, None),
    )
    out_specs = P("exp", "seq", None)
    return jax.shard_map(local, mesh=mesh, in_specs=in_specs, out_specs=out_specs, check_vma=False)
```
